32 devices in a mesh: freq: 2 (over x), gz: 16 (over z, y, core).
Axes of the slice: x: 2, y: 2, z: 4, core: 2. Of those that a mesh axis runs over, the one named last changes fastest.
Arguments:
- initial_guess: float32 [128, 2, 8, 32, 128], P(('freq', 'gz')), parts along dimension 0
- velocity_class: int32 [64, 32, 128], P('gz'), may hold values from 0 to 15
- layer_code: int32 [64, 32, 128], P('gz'), may hold values from 0 to 7
- wavenumber: float32 [32], P('freq'), parts along dimension 0, may hold values from 0.5 to 3
- damping: float32 [8], replicated, may hold values from 0.05 to 1
- shot_cells: int32 [8, 3], replicated, may hold values from 0 to 127, as said below
- wavelet: float32 [4, 8], P('freq'), parts along dimension 0, may hold values from -12 to 12
Outputs:
- basis_two: float32 [128, 2, 8, 32, 128], P(('freq', 'gz')), parts along dimension 0
- hessenberg: float32 [4, 24, 16], P('freq'), parts along dimension 0
The draws below stay inside these ranges and needn't reach their ends.
There are 2 independent parts, one for each index of `freq`. The reference program is written for one: setup_inputs(seed, part) draws one part's arguments, and reference() takes and returns one part's arrays. A program takes and returns all parts, laid end to end along the dimension named above; an argument that names none is the same for every part. Nothing has to cross between parts.
Inputs may be any that keep to these rules, and one draw needn't show every extreme that they name: `shot_cells`: row s holds shot s's depth cell below 64, first lateral cell below 32 and second lateral cell below 128; over all shots some depth cell is 63, some first lateral cell 32 - 1, some second lateral cell 128 - 1, and some depth cell 0.
All inputs are finite; a program needn't handle non-finite values.
Results may differ from the reference program's by a relative error of at most 0.0003.
Values sent between devices are 32-bit elements; how exact they have to be, the bound alone decides.
No kernel may reach another device: no remote copies, remote signals or barrier semaphores. Data moves between devices by JAX's collectives and lax.ppermute only.
A program may use at most 64 MiB of HBM per device.

```python
import math
import jax
import jax.numpy as jnp
from jax import lax

SHOTS = 8
CLASSES = 16
LEVELS = 8
NX = 32
NY = 128
NZ = 64
CELLS = 262144


def draw_initial_guess(key, part):
    key = jax.random.fold_in(key, 1)
    first_key, second_key = jax.random.split(key, 2)
    fraction = jnp.arange(NZ, dtype=jnp.float32) / max(NZ - 1, 1)
    shot_scale = jnp.exp(jax.random.uniform(second_key, (SHOTS,), jnp.float32, 0.0, math.log(10.0))) / math.sqrt(10.0)
    shot_scale = shot_scale.reshape(1, 1, SHOTS, 1, 1)
    depth_scale = (10.0 ** (fraction - 0.5)).reshape(NZ, 1, 1, 1, 1)
    values = jax.random.normal(first_key, (NZ, 2, SHOTS, NX, NY), jnp.float32) * depth_scale * shot_scale
    return values.astype(jnp.float32)


def draw_shot_cells(key, part):
    key = jax.random.fold_in(key, 2)
    first_key, second_key, third_key = jax.random.split(key, 3)
    depth_cell = jax.random.randint(first_key, (SHOTS,), 0, NZ)
    across_cell = jax.random.randint(second_key, (SHOTS,), 0, NX)
    along_cell = jax.random.randint(third_key, (SHOTS,), 0, NY)
    depth_cell = depth_cell.at[0].set(NZ - 1).at[3].set(0)
    across_cell = across_cell.at[1].set(NX - 1)
    along_cell = along_cell.at[2].set(NY - 1)
    return jnp.stack([depth_cell, across_cell, along_cell], axis=1).astype(jnp.int32)


def touch_ends(array, stream_key, smallest, top_value):
    spot = [jax.random.randint(jax.random.fold_in(stream_key, axis), (), 0, length) for axis, length in enumerate(array.shape)]
    widest = array.shape.index(max(array.shape))
    beside = spot[:widest] + [(spot[widest] + 1) % array.shape[widest]] + spot[widest + 1:]
    return array.at[tuple(spot)].set(smallest).at[tuple(beside)].set(top_value)


def normal_values(stream_key, dims, deviation, bound, held_as=jnp.bfloat16):
    array = deviation * jax.random.normal(stream_key, dims, jnp.float32)
    return jnp.clip(array, min=-bound, max=bound).astype(held_as)


def setup_inputs(seed: int = 0, part: int = 0) -> dict:
    keys = jax.random.split(jax.random.key(seed), 8)
    part_keys = jax.random.split(jax.random.fold_in(keys[7], part), 8)
    initial_guess = draw_initial_guess(jax.random.fold_in(jax.random.fold_in(keys[7], part), 71), part)
    velocity_class = touch_ends(jax.random.randint(keys[1], (NZ, NX, NY), 0, CLASSES), jax.random.fold_in(keys[1], 1), 0, CLASSES - 1).astype(jnp.int32)
    layer_code = touch_ends(jax.random.randint(keys[2], (NZ, NX, NY), 0, LEVELS), jax.random.fold_in(keys[2], 1), 0, LEVELS - 1).astype(jnp.int32)
    wavenumber = jnp.clip(jnp.exp(jax.random.uniform(part_keys[3], (CLASSES,), jnp.float32, math.log(0.5), math.log(3.0))), 0.5, 3.0)
    damping = jnp.clip(jax.random.uniform(keys[4], (LEVELS,), jnp.float32, 0.05, 1.0), 0.05, 1.0)
    shot_cells = draw_shot_cells(jax.random.fold_in(keys[7], 71), part)
    wavelet = normal_values(part_keys[6], (2, SHOTS), 3.0, 12.0, jnp.float32)
    return {"initial_guess": initial_guess, "velocity_class": velocity_class, "layer_code": layer_code, "wavenumber": wavenumber, "damping": damping, "shot_cells": shot_cells, "wavelet": wavelet}


highest = lax.Precision.HIGHEST

def paired(values, dimension):
    padded = jnp.pad(values, [(1, 1) if d == dimension else (0, 0) for d in range(values.ndim)])
    length = values.shape[dimension]
    return lax.slice_in_dim(padded, 2, length + 2, axis=dimension) + lax.slice_in_dim(padded, 0, length, axis=dimension)

def apply_operator(padded, wave_terms):
    center = padded[1:-1]
    along_depth = padded[2:] + padded[:-2]
    smooth = along_depth + 3.0 * center
    smooth = paired(smooth, 3) + 3.0 * smooth
    smooth = paired(smooth, 4) + 3.0 * smooth
    face_sum = along_depth + paired(center, 3) + paired(center, 4)
    negative = (155.0 * center - smooth - 5.0 * face_sum) / 30.0
    wave_real = wave_terms[:, 0][:, None]
    wave_imag = wave_terms[:, 1][:, None]
    out_real = negative[:, 0] - (wave_real * center[:, 0] - wave_imag * center[:, 1])
    out_imag = negative[:, 1] - (wave_real * center[:, 1] + wave_imag * center[:, 0])
    return jnp.stack([out_real, out_imag], axis=1)

def inner_block(left_block, right_block):
    flat_left = left_block.reshape(left_block.shape[0], 2, left_block.shape[2], -1)
    flat_right = right_block.reshape(right_block.shape[0], 2, right_block.shape[2], -1)
    real_part = jnp.einsum('zcsm,zctm->st', flat_left, flat_right, precision=highest)
    imag_part = jnp.einsum('zsm,ztm->st', flat_left[:, 0], flat_right[:, 1], precision=highest) - jnp.einsum('zsm,ztm->st', flat_left[:, 1], flat_right[:, 0], precision=highest)
    return jnp.stack([real_part, imag_part])

def mix_block(vectors, matrix):
    flat = vectors.reshape(vectors.shape[0], 2, vectors.shape[2], -1)
    real_part = jnp.einsum('zsm,st->ztm', flat[:, 0], matrix[0], precision=highest) - jnp.einsum('zsm,st->ztm', flat[:, 1], matrix[1], precision=highest)
    imag_part = jnp.einsum('zsm,st->ztm', flat[:, 0], matrix[1], precision=highest) + jnp.einsum('zsm,st->ztm', flat[:, 1], matrix[0], precision=highest)
    joined = jnp.stack([real_part, imag_part], axis=1)
    return joined.reshape(vectors.shape[0], 2, matrix.shape[2], vectors.shape[3], vectors.shape[4])

def adjoint(matrix):
    return jnp.stack([matrix[0].T, -matrix[1].T])

def cholesky_lower(gram_matrix):
    order_n = gram_matrix.shape[1]
    indices = jnp.arange(order_n)
    lower_real = jnp.zeros((order_n, order_n), jnp.float32)
    lower_imag = jnp.zeros((order_n, order_n), jnp.float32)
    for j in range(order_n):
        column_real = gram_matrix[0, :, j] - lax.optimization_barrier(jnp.sum(lower_real * lower_real[j][None, :] + lower_imag * lower_imag[j][None, :], axis=1))
        column_imag = gram_matrix[1, :, j] - lax.optimization_barrier(jnp.sum(lower_imag * lower_real[j][None, :] - lower_real * lower_imag[j][None, :], axis=1))
        pivot_value = jnp.sqrt(column_real[j])
        column_real = jnp.where(indices > j, column_real / pivot_value, jnp.where(indices == j, pivot_value, 0.0))
        column_imag = jnp.where(indices > j, column_imag / pivot_value, 0.0)
        lower_real = lower_real.at[:, j].set(column_real)
        lower_imag = lower_imag.at[:, j].set(column_imag)
    return jnp.stack([lower_real, lower_imag])

def lower_inverse(lower_factor):
    order_n = lower_factor.shape[1]
    identity = jnp.eye(order_n, dtype=jnp.float32)
    inverse_real = jnp.zeros((order_n, order_n), jnp.float32)
    inverse_imag = jnp.zeros((order_n, order_n), jnp.float32)
    for i in range(order_n):
        total_real = identity[i] - lax.optimization_barrier(jnp.sum(lower_factor[0, i][:, None] * inverse_real - lower_factor[1, i][:, None] * inverse_imag, axis=0))
        total_imag = -lax.optimization_barrier(jnp.sum(lower_factor[0, i][:, None] * inverse_imag + lower_factor[1, i][:, None] * inverse_real, axis=0))
        inverse_real = inverse_real.at[i].set(total_real / lower_factor[0, i, i])
        inverse_imag = inverse_imag.at[i].set(total_imag / lower_factor[0, i, i])
    return jnp.stack([inverse_real, inverse_imag])

def factored(vectors, gram_matrix):
    lower_factor = cholesky_lower(gram_matrix)
    return (mix_block(vectors, adjoint(lower_inverse(lower_factor))), adjoint(lower_factor))

def coefficients(velocity_class, layer_code, wavenumber, damping):
    labels = jnp.arange(wavenumber.shape[0]).astype(jnp.int32)
    levels = jnp.arange(damping.shape[0]).astype(jnp.int32)
    wave_real = lax.optimization_barrier(jnp.sum(jnp.where(labels[:, None, None, None] == velocity_class[None], wavenumber[:, None, None, None], 0.0), axis=0))
    loss_rate = lax.optimization_barrier(jnp.sum(jnp.where(levels[:, None, None, None] == layer_code[None], damping[:, None, None, None], 0.0), axis=0))
    return jnp.stack([wave_real, wave_real * loss_rate], axis=1)

def source_block(shot_cells, wavelet, first_plane, layers, width_first, width_second):
    planes = first_plane + jnp.arange(layers).astype(jnp.int32)
    hit_depth = (planes[:, None] == shot_cells[None, :, 0]).astype(jnp.float32)
    hit_across = (jnp.arange(width_first).astype(jnp.int32)[None, :] == shot_cells[:, 1][:, None]).astype(jnp.float32)
    hit_along = (jnp.arange(width_second).astype(jnp.int32)[None, :] == shot_cells[:, 2][:, None]).astype(jnp.float32)
    return hit_depth[:, None, :, None, None] * wavelet[None, :, :, None, None] * hit_across[None, None, :, :, None] * hit_along[None, None, :, None, :]

def pad_depth(vectors):
    return jnp.pad(vectors, ((1, 1), (0, 0), (0, 0), (0, 0), (0, 0)))

def reference(initial_guess, velocity_class, layer_code, wavenumber, damping, shot_cells, wavelet):
    wave_terms = coefficients(velocity_class, layer_code, wavenumber, damping)
    start_block = source_block(shot_cells, wavelet, 0, NZ, NX, NY) - apply_operator(pad_depth(initial_guess), wave_terms)
    basis_zero = factored(start_block, inner_block(start_block, start_block) / CELLS)[0]
    image_one = apply_operator(pad_depth(basis_zero), wave_terms)
    coef_zero_zero = inner_block(basis_zero, image_one) / CELLS
    image_one = image_one - mix_block(basis_zero, coef_zero_zero)
    basis_one, coef_one_zero = factored(image_one, inner_block(image_one, image_one) / CELLS)
    image_two = apply_operator(pad_depth(basis_one), wave_terms)
    coef_zero_one = inner_block(basis_zero, image_two) / CELLS
    coef_one_one = inner_block(basis_one, image_two) / CELLS
    image_two = image_two - mix_block(basis_zero, coef_zero_one)
    image_two = image_two - mix_block(basis_one, coef_one_one)
    basis_two, coef_two_one = factored(image_two, inner_block(image_two, image_two) / CELLS)
    zero_block = jnp.zeros_like(coef_zero_zero)
    first_column = jnp.concatenate([coef_zero_zero, coef_one_zero, zero_block], axis=1)
    second_column = jnp.concatenate([coef_zero_one, coef_one_one, coef_two_one], axis=1)
    hessenberg = jnp.concatenate([first_column, second_column], axis=2)
    return (basis_two, hessenberg)
```

```python
import functools

import jax
import jax.numpy as jnp
from jax import lax
from jax.experimental import pallas as pl
from jax.experimental.pallas import tpu as pltpu
from jax.sharding import PartitionSpec as P

SHIFT_BASE = 2.9
BLOCKS = 3
REACH = 3
VMEM_BYTES = 48 * 1024 * 1024


def shift_of(wave_ref, damp_ref):
    classes, levels = wave_ref.shape[0], damp_ref.shape[0]
    wave_mean = sum(wave_ref[i] for i in range(classes)) * (1.0 / classes)
    damp_mean = sum(damp_ref[i] for i in range(levels)) * (1.0 / levels)
    return SHIFT_BASE - wave_mean, -wave_mean * damp_mean


def stencil_plane(src, src_plane, dst, dst_plane, real_table, imag_table, table_plane, scale, keep):
    width = real_table.shape[1]
    left, right = keep

    def load(column):
        center, away = [], []
        for part in range(2):
            v = src[src_plane, column, part]
            d = src[src_plane - 1, column, part] + src[src_plane + 1, column, part]
            center.append(v)
            away.append(d + 3.0 * v)
        return center, away

    before_v, before_u = load(0)
    here_v, here_u = load(1)
    for column in range(width):
        after_v, after_u = load(column + 2)
        real_row = jnp.broadcast_to(real_table[table_plane, column : column + 1, :], here_v[0].shape)
        imag_row = jnp.broadcast_to(imag_table[table_plane, column : column + 1, :], here_v[0].shape)
        for part in range(2):
            near = here_u[part] + (before_v[part] + after_v[part])
            wide = (before_u[part] + after_u[part]) + (3.0 * here_u[part] + 5.0 * here_v[part])
            sides = pltpu.roll(wide, 1, 1) * left + pltpu.roll(wide, 127, 1) * right
            total = 3.0 * wide + 5.0 * near + sides
            if part == 0:
                own = real_row * here_v[0] + imag_row * here_v[1]
            else:
                own = real_row * here_v[1] - imag_row * here_v[0]
            dst[dst_plane, column + 1, part] = own - scale * total
        before_v, before_u, here_v, here_u = here_v, here_u, after_v, after_u


def front_kernel(
    depth_total,
    index_ref,
    wave_ref,
    damp_ref,
    cells_ref,
    wavelet_ref,
    guess_ref,
    below_ref,
    above_ref,
    class_ref,
    layer_ref,
    split_ref,
    gram_ref,
    field,
    start,
    first,
    second,
    real_start,
    imag_start,
    real_shift,
    imag_shift,
    products,
):
    layers, _, shots, width, lanes = guess_ref.shape
    first_plane = index_ref[0] * layers
    shift_real, shift_imag = shift_of(wave_ref, damp_ref)
    fields = 2 * shots

    def inside(plane):
        return jnp.where((plane >= 0) & (plane < depth_total), 1.0, 0.0).astype(jnp.float32)

    zero_column = jnp.zeros((2, shots, lanes), jnp.float32)
    for buffer in (field, start, first):
        for plane in range(buffer.shape[0]):
            buffer[plane, 0] = zero_column
            buffer[plane, width + 1] = zero_column

    def bring(source, source_row, plane):
        for column in range(width):
            for part in range(2):
                field[plane, column + 1, part] = source[
                    pl.ds(source_row + part * shots * width + column, shots, stride=width), :
                ]

    guess_rows = guess_ref.reshape(layers * fields * width, lanes)
    below_rows = below_ref.reshape(below_ref.shape[0] * width, lanes)
    above_rows = above_ref.reshape(above_ref.shape[0] * width, lanes)

    def bring_guess(plane, carry):
        bring(guess_rows, plane * (fields * width), plane + REACH)
        return carry

    def bring_below(plane, carry):
        bring(below_rows, plane * (fields * width), plane)
        return carry

    def bring_above(plane, carry):
        bring(above_rows, plane * (fields * width), plane + REACH + layers)
        return carry

    lax.fori_loop(0, layers, bring_guess, 0)
    lax.fori_loop(0, REACH, bring_below, 0)
    lax.fori_loop(0, REACH, bring_above, 0)

    extra = REACH * fields

    def table(plane, labels, codes, inside_flag):
        wave = jnp.zeros(labels.shape, jnp.float32)
        for i in range(wave_ref.shape[0]):
            wave = jnp.where(labels == float(i), wave_ref[i], wave)
        loss = jnp.zeros(labels.shape, jnp.float32)
        for i in range(damp_ref.shape[0]):
            loss = jnp.where(codes == float(i), damp_ref[i], loss)
        real = 185.0 / 30.0 - wave
        imag = wave * loss
        real_start[plane] = -inside_flag * real
        imag_start[plane] = -inside_flag * imag
        real_shift[plane] = inside_flag * (real - shift_real)
        imag_shift[plane] = inside_flag * (imag + shift_imag)

    for plane in range(layers):
        table(
            plane + 2,
            class_ref[plane].astype(jnp.float32),
            layer_ref[plane].astype(jnp.float32),
            jnp.float32(1.0),
        )
    for k in range(2):
        table(k, below_ref[extra + k], below_ref[extra + 2 + k], inside(first_plane - 2 + k))
        table(
            layers + 2 + k,
            above_ref[extra + k],
            above_ref[extra + 2 + k],
            inside(first_plane + layers + k),
        )

    lane = lax.broadcasted_iota(jnp.int32, (shots, lanes), 1)
    keep = (
        jnp.where(lane == 0, 0.0, 1.0).astype(jnp.float32),
        jnp.where(lane == lanes - 1, 0.0, 1.0).astype(jnp.float32),
    )

    def start_plane(i, carry):
        scale = inside(first_plane + i - 2) * (-1.0 / 30.0)
        stencil_plane(field, i + 1, start, i, real_start, imag_start, i, scale, keep)
        return carry

    lax.fori_loop(0, layers + 4, start_plane, 0)

    lane_row = lax.broadcasted_iota(jnp.int32, (1, lanes), 1)
    for s in range(shots):
        plane = cells_ref[s, 0] - first_plane + 2

        @pl.when((plane >= 0) & (plane < layers + 4))
        def _():
            column = cells_ref[s, 1] + 1
            hit = lane_row == cells_ref[s, 2]
            for part in range(2):
                start[plane, column, part, s : s + 1, :] += jnp.where(hit, wavelet_ref[part, s], 0.0)

    def first_image(i, carry):
        scale = inside(first_plane + i - 1) * (1.0 / 30.0)
        stencil_plane(start, i + 1, first, i, real_shift, imag_shift, i + 1, scale, keep)
        return carry

    lax.fori_loop(0, layers + 2, first_image, 0)

    def second_image(i, carry):
        stencil_plane(first, i + 1, second, i, real_shift, imag_shift, i + 2, 1.0 / 30.0, keep)
        return carry

    lax.fori_loop(0, layers, second_image, 0)

    rows = BLOCKS * fields
    products[...] = jnp.zeros_like(products)

    def split_plane(plane, carry):
        for column in range(width):
            pieces = [
                start[plane + 2, column + 1, 0],
                first[plane + 1, column + 1, 0],
                second[plane, column + 1, 0],
                start[plane + 2, column + 1, 1],
                first[plane + 1, column + 1, 1],
                second[plane, column + 1, 1],
            ]
            spot = pl.ds(pl.multiple_of(plane * (width * lanes) + column * lanes, lanes), lanes)
            for pair in range(3):
                value = jnp.concatenate(pieces[2 * pair : 2 * pair + 2], axis=0)
                for part in range(3):
                    short = value.astype(jnp.bfloat16)
                    split_ref[pl.ds(part * rows + 2 * shots * pair, 2 * shots), spot] = short
                    if part < 2:
                        value = value - short.astype(jnp.float32)
        spot = pl.ds(pl.multiple_of(plane * (width * lanes), lanes), width * lanes)
        chunk = split_ref[:, spot]
        products[...] += lax.dot_general(
            chunk, chunk, (((1,), (1,)), ((), ())), preferred_element_type=jnp.float32
        )
        return carry

    lax.fori_loop(0, layers, split_plane, 0)

    cells = float(depth_total * width * lanes)
    summed = products[0:rows] + products[rows : 2 * rows] + products[2 * rows : 3 * rows]
    summed = summed[:, 0:rows] + summed[:, rows : 2 * rows] + summed[:, 2 * rows : 3 * rows]
    summed = summed * (1.0 / cells)
    half = rows // 2
    gram_real = summed[0:half, 0:half] + summed[half:rows, half:rows]
    gram_imag = summed[0:half, half:rows] - summed[half:rows, 0:half]
    lead = BLOCKS * rows - 128
    gram = jnp.concatenate([gram_real, gram_imag], axis=0)
    gram_ref[...] = jnp.concatenate(
        [
            jnp.zeros((rows, lead), jnp.float32),
            gram,
            jnp.zeros((rows, 128 - lead - half), jnp.float32),
        ],
        axis=1,
    )


def back_kernel(wave_ref, damp_ref, mine_ref, other_ref, split_ref, basis_ref, hessenberg_ref, mixer):
    rows = mine_ref.shape[0]
    half = rows // 2
    tile = 8
    tiles = half // tile
    lanes = mine_ref.shape[1]
    spread = BLOCKS * rows

    @pl.when(pl.program_id(0) == 0)
    def _():
        gram = mine_ref[...] + other_ref[...]
        lane = lax.broadcasted_iota(jnp.int32, (tile, lanes), 1)
        sub = lax.broadcasted_iota(jnp.int32, (tile, lanes), 0)
        wide_lane = lax.broadcasted_iota(jnp.int32, (tile, 2 * lanes), 1)
        wide_sub = lax.broadcasted_iota(jnp.int32, (tile, 2 * lanes), 0)
        in_gram = (lane >= spread - lanes) & (lane < spread - lanes + half)
        real, imag = [], []
        for t in range(tiles):
            match = (wide_lane < spread) & (lax.rem(wide_lane, half) == wide_sub + t * tile)
            unit = jnp.where(match, 1.0, 0.0).astype(jnp.float32)
            blank = jnp.zeros((tile, lanes), jnp.float32)
            real.append(
                unit + jnp.concatenate([blank, gram[t * tile : (t + 1) * tile]], axis=1)
            )
            imag.append(
                jnp.concatenate([blank, gram[half + t * tile : half + (t + 1) * tile]], axis=1)
            )
        pivots = []
        for k in range(half):
            owner, row = divmod(k, tile)
            row_real = real[owner][row : row + 1]
            row_imag = imag[owner][row : row + 1]
            spot = spread + k
            pivot = row_real[:, spot : spot + 1]
            pivots.append(pivot)
            inverse = 1.0 / pivot
            for t in range(owner, tiles):
                column_real = real[t][:, spot : spot + 1] * inverse
                column_imag = imag[t][:, spot : spot + 1] * inverse
                if t == owner:
                    below = sub[:, 0:1] > row
                    column_real = jnp.where(below, column_real, 0.0)
                    column_imag = jnp.where(below, column_imag, 0.0)
                new_real = real[t] - (column_real * row_real - column_imag * row_imag)
                new_imag = imag[t] - (column_real * row_imag + column_imag * row_real)
                real[t], imag[t] = new_real, new_imag
        for t in range(tiles):
            scales = lax.rsqrt(jnp.concatenate(pivots[t * tile : (t + 1) * tile], axis=0))
            real[t] = real[t] * scales
            imag[t] = imag[t] * scales

        last_real, last_imag = real[tiles - 1], imag[tiles - 1]
        first_half = lax.rem(wide_lane, rows) < half
        mix = jnp.concatenate(
            [
                jnp.where(first_half, last_real, last_imag),
                jnp.where(first_half, -last_imag, last_real),
            ],
            axis=0,
        )
        pieces = []
        for part in range(3):
            short = mix.astype(jnp.bfloat16)
            pieces.append(short)
            mix = mix - short.astype(jnp.float32)
        mixer[...] = jnp.concatenate(pieces, axis=0)

        wide = 2 * tile
        full_real = jnp.concatenate(real, axis=0)
        full_imag = jnp.concatenate(imag, axis=0)
        row_index = lax.broadcasted_iota(jnp.int32, (half, wide), 0)
        column_index = lax.broadcasted_iota(jnp.int32, (half, wide), 1)
        upper = row_index <= column_index + tile
        factor_real = jnp.where(upper, full_real[:, spread + tile : spread + half], 0.0)
        factor_imag = jnp.where(upper, full_imag[:, spread + tile : spread + half], 0.0)
        lower_real = full_real[0:wide, 0:wide]
        lower_imag = full_imag[0:wide, 0:wide]

        def times(left, right):
            return lax.dot_general(
                left,
                right,
                (((1,), (1,)), ((), ())),
                precision=lax.Precision.HIGHEST,
                preferred_element_type=jnp.float32,
            )

        shift_real, shift_imag = shift_of(wave_ref, damp_ref)
        diagonal = row_index == column_index
        hessenberg_ref[0] = (
            times(factor_real, lower_real)
            + times(factor_imag, lower_imag)
            + jnp.where(diagonal, shift_real, 0.0)
        )
        hessenberg_ref[1] = (
            times(factor_imag, lower_real)
            - times(factor_real, lower_imag)
            + jnp.where(diagonal, shift_imag, 0.0)
        )

    _, parts, shots, width, y = basis_ref.shape
    fields = parts * shots
    out_rows = basis_ref.reshape(fields * width, y)
    left = mixer[:, 0:spread]
    group = 8
    for begin in range(0, width, group):
        mixed = jnp.dot(
            left,
            split_ref[:, begin * y : (begin + group) * y],
            preferred_element_type=jnp.float32,
        )
        mixed = mixed[0:fields] + mixed[fields : 2 * fields] + mixed[2 * fields : 3 * fields]
        for column in range(group):
            out_rows[pl.ds(begin + column, fields, stride=width), :] = mixed[
                :, column * y : (column + 1) * y
            ]


def neighbour_buffer(planes, classes, codes):
    flat = planes.reshape(-1, planes.shape[3], planes.shape[4])
    return jnp.concatenate([flat, classes.astype(jnp.float32), codes.astype(jnp.float32)], axis=0)


def shards(initial_guess, velocity_class, layer_code, wavenumber, damping, shot_cells, wavelet):
    layers, _, shots, width, lanes = initial_guess.shape
    devices = lax.axis_size("gz")
    fields = 2 * shots
    rows = BLOCKS * fields
    cells = layers * width * lanes

    up = [(i, i + 1) for i in range(devices - 1)]
    down = [(i + 1, i) for i in range(devices - 1)]
    below = lax.ppermute(
        neighbour_buffer(initial_guess[-REACH:], velocity_class[-2:], layer_code[-2:]), "gz", up
    )
    above = lax.ppermute(
        neighbour_buffer(initial_guess[:REACH], velocity_class[:2], layer_code[:2]), "gz", down
    )
    index = lax.axis_index("gz").astype(jnp.int32).reshape(1)

    smem = pl.BlockSpec(memory_space=pltpu.SMEM)
    vmem = pl.BlockSpec(memory_space=pltpu.VMEM)
    split, gram = pl.pallas_call(
        functools.partial(front_kernel, devices * layers),
        out_shape=(
            jax.ShapeDtypeStruct((BLOCKS * rows, cells), jnp.bfloat16),
            jax.ShapeDtypeStruct((rows, 128), jnp.float32),
        ),
        in_specs=[smem] * 5 + [vmem] * 5,
        out_specs=(vmem, vmem),
        scratch_shapes=[
            pltpu.VMEM((layers + 6, width + 2, 2, shots, lanes), jnp.float32),
            pltpu.VMEM((layers + 4, width + 2, 2, shots, lanes), jnp.float32),
            pltpu.VMEM((layers + 2, width + 2, 2, shots, lanes), jnp.float32),
            pltpu.VMEM((layers, width + 2, 2, shots, lanes), jnp.float32),
        ]
        + [pltpu.VMEM((layers + 4, width, lanes), jnp.float32)] * 4
        + [pltpu.VMEM((BLOCKS * rows, BLOCKS * rows), jnp.float32)],
        compiler_params=pltpu.CompilerParams(vmem_limit_bytes=VMEM_BYTES),
        name="front",
    )(
        index,
        wavenumber,
        damping,
        shot_cells,
        wavelet,
        initial_guess,
        below,
        above,
        velocity_class,
        layer_code,
    )

    mine, step = gram, 1
    other = None
    while step < devices:
        if other is not None:
            mine = mine + other
        other = lax.ppermute(mine, "gz", [(i, i ^ step) for i in range(devices)])
        step *= 2

    return pl.pallas_call(
        back_kernel,
        grid=(layers,),
        out_shape=(
            jax.ShapeDtypeStruct(initial_guess.shape, jnp.float32),
            jax.ShapeDtypeStruct((2, BLOCKS * shots, 2 * shots), jnp.float32),
        ),
        in_specs=[
            smem,
            smem,
            pl.BlockSpec((rows, 128), lambda z: (0, 0)),
            pl.BlockSpec((rows, 128), lambda z: (0, 0)),
            pl.BlockSpec((BLOCKS * rows, width * lanes), lambda z: (0, z)),
        ],
        out_specs=(
            pl.BlockSpec((1, 2, shots, width, lanes), lambda z: (z, 0, 0, 0, 0)),
            pl.BlockSpec((2, BLOCKS * shots, 2 * shots), lambda z: (0, 0, 0)),
        ),
        scratch_shapes=[pltpu.VMEM((3 * fields, 256), jnp.bfloat16)],
        compiler_params=pltpu.CompilerParams(vmem_limit_bytes=VMEM_BYTES),
        name="back",
    )(wavenumber, damping, mine, other, split)


def solution(mesh):
    return jax.shard_map(
        shards,
        mesh=mesh,
        in_specs=(
            P(("freq", "gz"), None, None, None, None),
            P("gz", None, None),
            P("gz", None, None),
            P("freq"),
            P(),
            P(),
            P("freq", None),
        ),
        out_specs=(P(("freq", "gz"), None, None, None, None), P("freq", None, None)),
        check_vma=False,
    )
```

```python
import functools

import jax
import jax.numpy as jnp
from jax import lax
from jax.experimental import pallas as pl
from jax.experimental.pallas import tpu as pltpu
from jax.sharding import PartitionSpec as P

SHIFT_BASE = 2.9
BLOCKS = 3
REACH = 3
VMEM_BYTES = 24 * 1024 * 1024
PAIRS = ((0, 0), (0, 1), (0, 2), (1, 1), (1, 2), (2, 2))


def shift_of(wave_ref, damp_ref):
    classes, levels = wave_ref.shape[0], damp_ref.shape[0]
    wave_mean = sum(wave_ref[i] for i in range(classes)) * (1.0 / classes)
    damp_mean = sum(damp_ref[i] for i in range(levels)) * (1.0 / levels)
    return SHIFT_BASE - wave_mean, -wave_mean * damp_mean


def edge_masks(shots, lanes):
    lane = lax.broadcasted_iota(jnp.int32, (shots, lanes), 1)
    return (
        jnp.where(lane == 0, 0.0, 1.0).astype(jnp.float32),
        jnp.where(lane == lanes - 1, 0.0, 1.0).astype(jnp.float32),
    )


def stencil_plane(sources, target, table, scale, keep):
    (low, low_plane), (mid, mid_plane), (high, high_plane) = sources
    out, out_plane = target
    table_ref, table_plane, kind = table
    width = table_ref.shape[2]
    left, right = keep

    def load(column):
        center, away = [], []
        for part in range(2):
            v = mid[mid_plane, column, part]
            d = low[low_plane, column, part] + high[high_plane, column, part]
            center.append(v)
            away.append(d + 3.0 * v)
        return center, away

    here_v, here_u = load(0)
    before_v = [jnp.zeros_like(v) for v in here_v]
    before_u = before_v
    for column in range(width):
        if column + 1 < width:
            after_v, after_u = load(column + 1)
        else:
            after_v = [jnp.zeros_like(v) for v in here_v]
            after_u = after_v
        real_row, imag_row = [
            jnp.broadcast_to(table_ref[table_plane, 2 * kind + part, column : column + 1, :], here_v[0].shape)
            for part in range(2)
        ]
        for part in range(2):
            near = here_u[part] + (before_v[part] + after_v[part])
            wide = (before_u[part] + after_u[part]) + (3.0 * here_u[part] + 5.0 * here_v[part])
            sides = pltpu.roll(wide, 1, 1) * left + pltpu.roll(wide, 127, 1) * right
            total = 3.0 * wide + 5.0 * near + sides
            if part == 0:
                own = real_row * here_v[0] + imag_row * here_v[1]
            else:
                own = real_row * here_v[1] - imag_row * here_v[0]
            out[out_plane, column, part] = own - scale * total
        before_v, before_u, here_v, here_u = here_v, here_u, after_v, after_u


def bring(rows, first_row, field, plane):
    width, parts, shots = field.shape[1:4]
    for column in range(width):
        for part in range(parts):
            field[plane, column, part] = rows[
                pl.ds(first_row + part * shots * width + column, shots, stride=width), :
            ]


def fill_tables(tables, plane, labels, codes, inside_flag, wave_ref, damp_ref):
    shift_real, shift_imag = shift_of(wave_ref, damp_ref)
    wave = jnp.zeros(labels.shape, jnp.float32)
    for i in range(wave_ref.shape[0]):
        wave = jnp.where(labels == float(i), wave_ref[i], wave)
    loss = jnp.zeros(labels.shape, jnp.float32)
    for i in range(damp_ref.shape[0]):
        loss = jnp.where(codes == float(i), damp_ref[i], loss)
    real = 185.0 / 30.0 - wave
    imag = wave * loss
    tables[plane, 0] = -inside_flag * real
    tables[plane, 1] = -inside_flag * imag
    tables[plane, 2] = inside_flag * (real - shift_real)
    tables[plane, 3] = inside_flag * (imag + shift_imag)


def add_sources(start, first_start, place_of, cells_ref, wavelet_ref):
    count, _, _, shots, lanes = start.shape
    lane_row = lax.broadcasted_iota(jnp.int32, (1, lanes), 1)
    for s in range(shots):
        place = place_of(cells_ref[0, s]) - first_start

        @pl.when((place >= 0) & (place < count))
        def _():
            column = cells_ref[1, s]
            hit = lane_row == cells_ref[2, s]
            for part in range(2):
                start[place, column, part, s : s + 1, :] += jnp.where(hit, wavelet_ref[part, s], 0.0)


def split_plane(sources, split_ref, spot_plane):
    width, _, shots, lanes = sources[0][0].shape[1:]
    rows = BLOCKS * 2 * shots
    for column in range(width):
        pieces = [ref[plane, column, part] for part in range(2) for ref, plane in sources]
        begin = (spot_plane * width + column) * lanes
        for pair in range(BLOCKS):
            value = jnp.concatenate(pieces[2 * pair : 2 * pair + 2], axis=0)
            for part in range(3):
                short = value.astype(jnp.bfloat16)
                row = part * rows + 2 * shots * pair
                split_ref[row : row + 2 * shots, begin : begin + lanes] = short
                if part < 2:
                    value = value - short.astype(jnp.float32)


def products_of(split_ref, spot_plane, span):
    chunk = split_ref[:, spot_plane * span : (spot_plane + 1) * span]
    return lax.dot_general(
        chunk, chunk, (((1,), (1,)), ((), ())), preferred_element_type=jnp.float32
    )


def pack_kernel(index_ref, guess_ref, codes_ref, far_ref, near_ref, sems):
    layers, parts, shots, width, lanes = guess_ref.shape
    fields = parts * shots
    odd = lax.rem(index_ref[0], 2) == 1
    planes = guess_ref.reshape(layers * fields, width, lanes)
    codes = codes_ref.reshape(2 * layers, width, lanes)
    far_begin = jnp.where(odd, layers - 2, 0) * fields
    far_code = jnp.where(odd, layers - 1, 0)
    near_begin = jnp.where(odd, 0, layers - REACH) * fields
    near_code = jnp.where(odd, 0, layers - 2)
    copies = []
    for number, (source, target) in enumerate(
        (
            (planes.at[pl.ds(far_begin, 2 * fields)], far_ref.at[pl.ds(0, 2 * fields)]),
            (codes.at[pl.ds(far_code, 1)], far_ref.at[pl.ds(2 * fields, 1)]),
            (codes.at[pl.ds(far_code + layers, 1)], far_ref.at[pl.ds(2 * fields + 1, 1)]),
            (planes.at[pl.ds(near_begin, REACH * fields)], near_ref.at[pl.ds(0, REACH * fields)]),
            (codes.at[pl.ds(near_code, 2)], near_ref.at[pl.ds(REACH * fields, 2)]),
            (codes.at[pl.ds(near_code + layers, 2)], near_ref.at[pl.ds(REACH * fields + 2, 2)]),
        )
    ):
        copies.append(pltpu.make_async_copy(source, target, sems.at[number]))
        copies[-1].start()
    for copy in copies:
        copy.wait()


def orientation(index_ref, layers, depth_total):
    index = index_ref[0]
    odd = lax.rem(index, 2) == 1
    first_plane = index * layers

    def place_of(plane):
        local = plane - first_plane
        return jnp.where(odd, local, layers - 1 - local)

    def inside(place):
        plane = first_plane + jnp.where(odd, place, layers - 1 - place)
        return jnp.where((plane >= 0) & (plane < depth_total), 1.0, 0.0).astype(jnp.float32)

    return odd, place_of, inside


def early_kernel(
    depth_total,
    index_ref,
    wave_ref,
    damp_ref,
    cells_ref,
    wavelet_ref,
    guess_ref,
    near_ref,
    codes_ref,
    field,
    start,
    first,
    second,
    tables,
    split_ref,
    products_ref,
    send_ref,
):
    layers, parts, shots, width, lanes = guess_ref.shape
    fields = parts * shots
    odd, place_of, inside = orientation(index_ref, layers, depth_total)
    guess_rows = guess_ref.reshape(layers * fields * width, lanes)
    near_rows = near_ref.reshape(near_ref.shape[0] * width, lanes)
    span = fields * width
    keep = edge_masks(shots, lanes)

    far_plane = jnp.where(odd, layers - REACH, REACH - 1)
    far_code = jnp.where(odd, layers - 2, 1)
    for part in range(parts):
        send_ref[part * shots : (part + 1) * shots] = guess_ref[far_plane, part]
    send_ref[fields] = codes_ref[0, far_code]
    send_ref[fields + 1] = codes_ref[1, far_code]

    extra = REACH * fields
    for k in range(2):
        pick = jnp.where(odd, k, 1 - k)
        fill_tables(
            tables, k, near_ref[extra + pick], near_ref[extra + 2 + pick], inside(k - 2), wave_ref, damp_ref
        )
    for q in range(layers):
        pick = jnp.where(odd, q, layers - 1 - q)
        fill_tables(
            tables, q + 2, codes_ref[0, pick], codes_ref[1, pick], jnp.float32(1.0), wave_ref, damp_ref
        )

    def bring_near(k, carry):
        bring(near_rows, jnp.where(odd, k, REACH - 1 - k) * span, field, k)
        return carry

    def bring_own(q, carry):
        bring(guess_rows, jnp.where(odd, q, layers - 1 - q) * span, field, q + REACH)
        return carry

    lax.fori_loop(0, REACH, bring_near, 0)
    lax.fori_loop(0, layers, bring_own, 0)

    def start_plane(i, carry):
        stencil_plane(
            ((field, i), (field, i + 1), (field, i + 2)),
            (start, i),
            (tables, i, 0),
            inside(i - 2) * (-1.0 / 30.0),
            keep,
        )
        return carry

    lax.fori_loop(0, layers + 1, start_plane, 0)
    add_sources(start, -2, place_of, cells_ref, wavelet_ref)

    def first_plane(j, carry):
        stencil_plane(
            ((start, j), (start, j + 1), (start, j + 2)),
            (first, j),
            (tables, j + 1, 1),
            inside(j - 1) * (1.0 / 30.0),
            keep,
        )
        return carry

    lax.fori_loop(0, layers - 1, first_plane, 0)
    products = jnp.zeros(products_ref.shape, jnp.float32)
    for k in range(layers - 3):
        stencil_plane(
            ((first, k), (first, k + 1), (first, k + 2)),
            (second, k),
            (tables, k + 2, 1),
            1.0 / 30.0,
            keep,
        )
        split_plane(((start, k + 2), (first, k + 1), (second, k)), split_ref, k)
        products += products_of(split_ref, k, width * lanes)
    products_ref[...] = products


def middle_kernel(
    depth_total,
    index_ref,
    wave_ref,
    damp_ref,
    cells_ref,
    wavelet_ref,
    far_ref,
    old_field,
    old_start,
    old_first,
    old_tables,
    old_products,
    field,
    start,
    first,
    second,
    tables,
    split_ref,
    products_ref,
):
    layers = old_field.shape[0] - REACH
    _, width, parts, shots, lanes = field.shape
    fields = parts * shots
    odd, place_of, inside = orientation(index_ref, layers, depth_total)
    far_rows = far_ref.reshape(far_ref.shape[0] * width, lanes)
    span = fields * width
    keep = edge_masks(shots, lanes)
    fill_tables(
        tables, 0, far_ref[2 * fields], far_ref[2 * fields + 1], inside(jnp.int32(layers)), wave_ref, damp_ref
    )
    for k in range(2):
        bring(far_rows, jnp.where(odd, k, 1 - k) * span, field, k)

    def at_field(place):
        return (old_field, place + REACH) if place < layers else (field, place - layers)

    def at_start(place):
        return (old_start, place + 2) if place < layers - 1 else (start, place - (layers - 1))

    def at_first(place):
        return (old_first, place + 1) if place < layers - 2 else (first, place - (layers - 2))

    def at_table(place, kind):
        return (old_tables, place + 2, kind) if place < layers else (tables, place - layers, kind)

    for place in range(layers - 1, layers + 1):
        stencil_plane(
            (at_field(place - 1), at_field(place), at_field(place + 1)),
            at_start(place),
            at_table(place, 0),
            inside(jnp.int32(place)) * (-1.0 / 30.0),
            keep,
        )
    add_sources(start, layers - 1, place_of, cells_ref, wavelet_ref)
    for place in range(layers - 2, layers):
        stencil_plane(
            (at_start(place - 1), at_start(place), at_start(place + 1)),
            at_first(place),
            at_table(place, 1),
            1.0 / 30.0,
            keep,
        )
    products = old_products[...]
    for k in range(2):
        place = layers - 3 + k
        stencil_plane(
            (at_first(place - 1), at_first(place), at_first(place + 1)),
            (second, k),
            at_table(place, 1),
            1.0 / 30.0,
            keep,
        )
        split_plane((at_start(place), at_first(place), (second, k)), split_ref, k)
        products += products_of(split_ref, k, width * lanes)
    products_ref[...] = products


def late_kernel(
    depth_total,
    layers,
    index_ref,
    wave_ref,
    damp_ref,
    cells_ref,
    wavelet_ref,
    last_ref,
    old_field,
    old_start,
    old_first,
    own_tables,
    far_tables,
    old_products,
    split_ref,
    gram_ref,
    field,
    start,
    first,
    second,
    tables,
):
    _, width, parts, shots, lanes = field.shape
    fields = parts * shots
    odd, place_of, inside = orientation(index_ref, layers, depth_total)
    last_rows = last_ref.reshape(last_ref.shape[0] * width, lanes)
    keep = edge_masks(shots, lanes)
    fill_tables(
        tables, 0, last_ref[fields], last_ref[fields + 1], inside(jnp.int32(layers + 1)), wave_ref, damp_ref
    )
    bring(last_rows, 0, field, 0)
    stencil_plane(
        ((old_field, 0), (old_field, 1), (field, 0)),
        (start, 0),
        (tables, 0, 0),
        inside(jnp.int32(layers + 1)) * (-1.0 / 30.0),
        keep,
    )
    add_sources(start, layers + 1, place_of, cells_ref, wavelet_ref)
    stencil_plane(
        ((old_start, 0), (old_start, 1), (start, 0)),
        (first, 0),
        (far_tables, 0, 1),
        inside(jnp.int32(layers)) * (1.0 / 30.0),
        keep,
    )
    stencil_plane(
        ((old_first, 0), (old_first, 1), (first, 0)),
        (second, 0),
        (own_tables, layers + 1, 1),
        1.0 / 30.0,
        keep,
    )
    split_plane(((old_start, 0), (old_first, 1), (second, 0)), split_ref, 0)
    products = old_products[...] + products_of(split_ref, 0, width * lanes)

    rows = BLOCKS * fields
    half = rows // 2
    cells = float(depth_total * width * lanes)
    summed = products[0:rows] + products[rows : 2 * rows] + products[2 * rows : 3 * rows]
    summed = summed[:, 0:rows] + summed[:, rows : 2 * rows] + summed[:, 2 * rows : 3 * rows]
    summed = summed * (1.0 / cells)
    real = summed[0:half, 0:half] + summed[half:rows, half:rows]
    imag = summed[0:half, half:rows] - summed[half:rows, 0:half]
    blocks = []
    for i, j in PAIRS:
        for values in (real, imag):
            blocks.append(values[i * shots : (i + 1) * shots, j * shots : (j + 1) * shots])
    blocks.append(jnp.zeros((shots, 128 - 2 * len(PAIRS) * shots), jnp.float32))
    packed = jnp.concatenate(blocks, axis=1)
    for copy in range(gram_ref.shape[0]):
        gram_ref[copy] = packed


def back_kernel(
    index_ref, wave_ref, damp_ref, grams_ref, early_ref, middle_ref, late_ref, basis_ref, hessenberg_ref
):
    layers, parts, shots, width, y = basis_ref.shape
    fields = parts * shots
    rows = BLOCKS * fields
    half = rows // 2
    tile = shots
    tiles = BLOCKS
    spread = BLOCKS * rows
    lanes = 128
    lead = spread - lanes

    grams = [grams_ref[i] for i in range(grams_ref.shape[0])]
    while len(grams) > 1:
        grams = [sum(grams[i : i + 2]) for i in range(0, len(grams), 2)]
    packed = grams[0]
    turned = packed.T
    lane = lax.broadcasted_iota(jnp.int32, (tile, lanes), 1)
    sub = lax.broadcasted_iota(jnp.int32, (tile, lanes), 0)
    wide_lane = lax.broadcasted_iota(jnp.int32, (tile, 2 * lanes), 1)
    wide_sub = lax.broadcasted_iota(jnp.int32, (tile, 2 * lanes), 0)
    real, imag = [], []
    for t in range(tiles):
        match = (wide_lane < spread) & (lax.rem(wide_lane, half) == wide_sub + t * tile)
        unit = jnp.where(match, 1.0, 0.0).astype(jnp.float32)
        blank = jnp.zeros((tile, lanes), jnp.float32)
        parts_of = []
        for part in range(2):
            blocks = [jnp.zeros((tile, lead), jnp.float32)]
            for j in range(tiles):
                if j >= t:
                    begin = (2 * PAIRS.index((t, j)) + part) * tile
                    blocks.append(packed[:, begin : begin + tile])
                else:
                    begin = (2 * PAIRS.index((j, t)) + part) * tile
                    block = turned[begin : begin + tile, 0:tile]
                    blocks.append(block if part == 0 else -block)
            blocks.append(jnp.zeros((tile, lanes - lead - half), jnp.float32))
            parts_of.append(jnp.concatenate(blocks, axis=1))
        real.append(unit + jnp.concatenate([blank, parts_of[0]], axis=1))
        imag.append(jnp.concatenate([blank, parts_of[1]], axis=1))
    pivots = []
    for k in range(half):
        owner, row = divmod(k, tile)
        row_real = real[owner][row : row + 1]
        row_imag = imag[owner][row : row + 1]
        spot = spread + k
        pivot = row_real[:, spot : spot + 1]
        pivots.append(pivot)
        inverse = 1.0 / pivot
        for t in range(owner, tiles):
            column_real = real[t][:, spot : spot + 1] * inverse
            column_imag = imag[t][:, spot : spot + 1] * inverse
            if t == owner:
                below = sub[:, 0:1] > row
                column_real = jnp.where(below, column_real, 0.0)
                column_imag = jnp.where(below, column_imag, 0.0)
            new_real = real[t] - (column_real * row_real - column_imag * row_imag)
            new_imag = imag[t] - (column_real * row_imag + column_imag * row_real)
            real[t], imag[t] = new_real, new_imag
    for t in range(tiles):
        scales = lax.rsqrt(jnp.concatenate(pivots[t * tile : (t + 1) * tile], axis=0))
        real[t] = real[t] * scales
        imag[t] = imag[t] * scales

    last_real, last_imag = real[tiles - 1], imag[tiles - 1]
    first_half = lax.rem(wide_lane, rows) < half
    mix = jnp.concatenate(
        [
            jnp.where(first_half, last_real, last_imag),
            jnp.where(first_half, -last_imag, last_real),
        ],
        axis=0,
    )
    pieces = []
    for part in range(3):
        short = mix.astype(jnp.bfloat16)
        pieces.append(short)
        mix = mix - short.astype(jnp.float32)
    left = jnp.concatenate(pieces, axis=0)[:, 0:spread]

    odd = lax.rem(index_ref[0], 2) == 1
    out_rows = basis_ref.reshape(layers * fields * width, y)
    spots = [
        (ref, spot)
        for ref in (early_ref, middle_ref, late_ref)
        for spot in range(ref.shape[1] // (width * y))
    ]
    group = 16
    for q in range(layers):
        source, spot = spots[q]
        plane = jnp.where(odd, q, layers - 1 - q)
        for begin in range(0, width, group):
            offset = (spot * width + begin) * y
            mixed = jnp.dot(
                left, source[:, offset : offset + group * y], preferred_element_type=jnp.float32
            )
            mixed = mixed[0:fields] + mixed[fields : 2 * fields] + mixed[2 * fields : 3 * fields]
            for column in range(group):
                out_rows[pl.ds(plane * (fields * width) + begin + column, fields, stride=width), :] = mixed[
                    :, column * y : (column + 1) * y
                ]

    wide = 2 * tile
    full_real = jnp.concatenate(real, axis=0)
    full_imag = jnp.concatenate(imag, axis=0)
    row_index = lax.broadcasted_iota(jnp.int32, (half, wide), 0)
    column_index = lax.broadcasted_iota(jnp.int32, (half, wide), 1)
    upper = row_index <= column_index + tile
    factor_real = jnp.where(upper, full_real[:, spread + tile : spread + half], 0.0)
    factor_imag = jnp.where(upper, full_imag[:, spread + tile : spread + half], 0.0)
    lower_real = full_real[0:wide, 0:wide]
    lower_imag = full_imag[0:wide, 0:wide]

    def times(left, right):
        return lax.dot_general(
            left,
            right,
            (((1,), (1,)), ((), ())),
            precision=lax.Precision.HIGHEST,
            preferred_element_type=jnp.float32,
        )

    shift_real, shift_imag = shift_of(wave_ref, damp_ref)
    diagonal = lax.broadcasted_iota(jnp.int32, (wide, half), 0) == lax.broadcasted_iota(
        jnp.int32, (wide, half), 1
    )
    hessenberg_ref[0] = (
        times(lower_real, factor_real)
        + times(lower_imag, factor_imag)
        + jnp.where(diagonal, shift_real, 0.0)
    )
    hessenberg_ref[1] = (
        times(lower_real, factor_imag)
        - times(lower_imag, factor_real)
        + jnp.where(diagonal, shift_imag, 0.0)
    )


def shards(initial_guess, velocity_class, layer_code, wavenumber, damping, shot_cells, wavelet):
    layers, parts, shots, width, lanes = initial_guess.shape
    devices = lax.axis_size("gz")
    fields = parts * shots
    rows = BLOCKS * fields
    span = width * lanes
    depth_total = devices * layers
    index = lax.axis_index("gz").astype(jnp.int32).reshape(1)
    shot_cells = shot_cells.T

    smem = pl.BlockSpec(memory_space=pltpu.SMEM)
    vmem = pl.BlockSpec(memory_space=pltpu.VMEM)
    hbm = pl.BlockSpec(memory_space=pl.ANY)
    params = pltpu.CompilerParams(vmem_limit_bytes=VMEM_BYTES)

    codes = jnp.stack([velocity_class, layer_code]).astype(jnp.float32)

    def float_shape(*dims):
        return jax.ShapeDtypeStruct(dims, jnp.float32)

    far, near = pl.pallas_call(
        pack_kernel,
        out_shape=(
            float_shape(2 * fields + 2, width, lanes),
            float_shape(REACH * fields + 4, width, lanes),
        ),
        in_specs=[smem, hbm, hbm],
        out_specs=(vmem, vmem),
        scratch_shapes=[pltpu.SemaphoreType.DMA((6,))],
        compiler_params=params,
        name="pack",
    )(index, initial_guess, codes)
    odd_to_even = [(i, i + 1) for i in range(1, devices - 1, 2)]
    even_to_odd = [(i, i + 1) for i in range(0, devices, 2)]
    far_pairs = odd_to_even + [(b, a) for a, b in odd_to_even]
    near_pairs = even_to_odd + [(b, a) for a, b in even_to_odd]
    far = lax.ppermute(far, "gz", far_pairs)
    near = lax.ppermute(near, "gz", near_pairs)

    def planes(count):
        return float_shape(count, width, parts, shots, lanes)

    def tables(count):
        return float_shape(count, 4, width, lanes)

    def split(count):
        return jax.ShapeDtypeStruct((BLOCKS * rows, count * span), jnp.bfloat16)

    def scratch(shape):
        return pltpu.VMEM(shape.shape, shape.dtype)

    products = float_shape(BLOCKS * rows, BLOCKS * rows)
    common = (index, wavenumber, damping, shot_cells, wavelet)
    field, start, first, _, own_tables, early_split, products_one, last = pl.pallas_call(
        functools.partial(early_kernel, depth_total),
        out_shape=(
            planes(layers + REACH),
            planes(layers + 1),
            planes(layers - 1),
            planes(layers - 3),
            tables(layers + 2),
            split(layers - 3),
            products,
            float_shape(fields + 2, width, lanes),
        ),
        in_specs=[smem] * 5 + [vmem] * 3,
        out_specs=(vmem,) * 8,
        compiler_params=params,
        cost_estimate=pl.CostEstimate(flops=10_000_000, bytes_accessed=16_000_000, transcendentals=0),
        name="early",
    )(*common, initial_guess, near, codes)
    last = lax.ppermute(last, "gz", far_pairs)
    field, start, first, _, far_tables, middle_split, products_two = pl.pallas_call(
        functools.partial(middle_kernel, depth_total),
        out_shape=(planes(2), planes(2), planes(2), planes(2), tables(1), split(2), products),
        in_specs=[smem] * 5 + [vmem] * 6,
        out_specs=(vmem,) * 7,
        compiler_params=params,
        cost_estimate=pl.CostEstimate(flops=8_000_000, bytes_accessed=12_000_000, transcendentals=0),
        name="middle",
    )(*common, far, field, start, first, own_tables, products_one)
    late_split, grams = pl.pallas_call(
        functools.partial(late_kernel, depth_total, layers),
        out_shape=(split(1), float_shape(devices, shots, 128)),
        in_specs=[smem] * 5 + [vmem] * 7,
        out_specs=(vmem, vmem),
        scratch_shapes=[scratch(planes(1))] * 4 + [scratch(tables(1))],
        compiler_params=params,
        name="late",
    )(*common, last, field, start, first, own_tables, far_tables, products_two)
    grams = lax.all_to_all(grams, "gz", 0, 0)
    basis_two, turned = pl.pallas_call(
        back_kernel,
        out_shape=(
            jax.ShapeDtypeStruct(initial_guess.shape, jnp.float32),
            jax.ShapeDtypeStruct((2, 2 * shots, BLOCKS * shots), jnp.float32),
        ),
        in_specs=[smem] * 3 + [vmem] * 4,
        out_specs=(vmem, vmem),
        compiler_params=params,
        name="back",
    )(index, wavenumber, damping, grams, early_split, middle_split, late_split)
    return basis_two, jnp.swapaxes(turned, 1, 2)


def solution(mesh):
    return jax.shard_map(
        shards,
        mesh=mesh,
        in_specs=(
            P(("freq", "gz"), None, None, None, None),
            P("gz", None, None),
            P("gz", None, None),
            P("freq"),
            P(),
            P(),
            P("freq", None),
        ),
        out_specs=(P(("freq", "gz"), None, None, None, None), P("freq", None, None)),
        check_vma=False,
    )
```

```python
import functools

import jax
import jax.numpy as jnp
from jax import lax
from jax.experimental import pallas as pl
from jax.experimental.pallas import tpu as pltpu
from jax.sharding import PartitionSpec as P

SHIFT_BASE = 2.9
BLOCKS = 3
REACH = 3
VMEM_BYTES = 24 * 1024 * 1024
PAIRS = ((0, 0), (0, 1), (0, 2), (1, 1), (1, 2), (2, 2))


def shift_of(wave_ref, damp_ref):
    classes, levels = wave_ref.shape[0], damp_ref.shape[0]
    wave_mean = sum(wave_ref[i] for i in range(classes)) * (1.0 / classes)
    damp_mean = sum(damp_ref[i] for i in range(levels)) * (1.0 / levels)
    return SHIFT_BASE - wave_mean, -wave_mean * damp_mean


def edge_masks(shots, lanes):
    lane = lax.broadcasted_iota(jnp.int32, (shots, lanes), 1)
    return (
        jnp.where(lane == 0, 0.0, 1.0).astype(jnp.float32),
        jnp.where(lane == lanes - 1, 0.0, 1.0).astype(jnp.float32),
    )


def stencil_plane(sources, target, table, scale, keep):
    (low, low_plane), (mid, mid_plane), (high, high_plane) = sources
    out, out_plane = target
    table_ref, table_plane, kind = table
    width = table_ref.shape[2]
    left, right = keep

    def load(column):
        center, away = [], []
        for part in range(2):
            v = mid[mid_plane, column, part]
            d = low[low_plane, column, part] + high[high_plane, column, part]
            center.append(v)
            away.append(d + 3.0 * v)
        return center, away

    here_v, here_u = load(0)
    before_v = [jnp.zeros_like(v) for v in here_v]
    before_u = before_v
    for column in range(width):
        if column + 1 < width:
            after_v, after_u = load(column + 1)
        else:
            after_v = [jnp.zeros_like(v) for v in here_v]
            after_u = after_v
        real_row, imag_row = [
            jnp.broadcast_to(table_ref[table_plane, 2 * kind + part, column : column + 1, :], here_v[0].shape)
            for part in range(2)
        ]
        for part in range(2):
            near = here_u[part] + (before_v[part] + after_v[part])
            wide = (before_u[part] + after_u[part]) + (3.0 * here_u[part] + 5.0 * here_v[part])
            sides = pltpu.roll(wide, 1, 1) * left + pltpu.roll(wide, 127, 1) * right
            total = 3.0 * wide + 5.0 * near + sides
            if part == 0:
                own = real_row * here_v[0] + imag_row * here_v[1]
            else:
                own = real_row * here_v[1] - imag_row * here_v[0]
            out[out_plane, column, part] = own - scale * total
        before_v, before_u, here_v, here_u = here_v, here_u, after_v, after_u


def bring(rows, first_row, field, plane):
    width, parts, shots = field.shape[1:4]
    for column in range(width):
        for part in range(parts):
            field[plane, column, part] = rows[
                pl.ds(first_row + part * shots * width + column, shots, stride=width), :
            ]


def fill_tables(tables, plane, labels, codes, inside_flag, wave_ref, damp_ref):
    shift_real, shift_imag = shift_of(wave_ref, damp_ref)
    wave = jnp.zeros(labels.shape, jnp.float32)
    for i in range(wave_ref.shape[0]):
        wave = jnp.where(labels == float(i), wave_ref[i], wave)
    loss = jnp.zeros(labels.shape, jnp.float32)
    for i in range(damp_ref.shape[0]):
        loss = jnp.where(codes == float(i), damp_ref[i], loss)
    real = 185.0 / 30.0 - wave
    imag = wave * loss
    tables[plane, 0] = -inside_flag * real
    tables[plane, 1] = -inside_flag * imag
    tables[plane, 2] = inside_flag * (real - shift_real)
    tables[plane, 3] = inside_flag * (imag + shift_imag)


def add_sources(start, first_start, place_of, cells_ref, wavelet_ref):
    count, _, _, shots, lanes = start.shape
    lane_row = lax.broadcasted_iota(jnp.int32, (1, lanes), 1)
    for s in range(shots):
        place = place_of(cells_ref[0, s]) - first_start

        @pl.when((place >= 0) & (place < count))
        def _():
            column = cells_ref[1, s]
            hit = lane_row == cells_ref[2, s]
            for part in range(2):
                start[place, column, part, s : s + 1, :] += jnp.where(hit, wavelet_ref[part, s], 0.0)


def split_plane(sources, split_ref, spot_plane):
    width, _, shots, lanes = sources[0][0].shape[1:]
    rows = BLOCKS * 2 * shots
    for column in range(width):
        pieces = [ref[plane, column, part] for part in range(2) for ref, plane in sources]
        begin = (spot_plane * width + column) * lanes
        for pair in range(BLOCKS):
            value = jnp.concatenate(pieces[2 * pair : 2 * pair + 2], axis=0)
            for part in range(3):
                short = value.astype(jnp.bfloat16)
                row = part * rows + 2 * shots * pair
                split_ref[row : row + 2 * shots, begin : begin + lanes] = short
                if part < 2:
                    value = value - short.astype(jnp.float32)


def products_of(split_ref, spot_plane, span):
    chunk = split_ref[:, spot_plane * span : (spot_plane + 1) * span]
    return lax.dot_general(
        chunk, chunk, (((1,), (1,)), ((), ())), preferred_element_type=jnp.float32
    )


def pack_kernel(index_ref, guess_ref, class_ref, layer_ref, edge_ref, near_ref, codes_ref, held, sems):
    layers, parts, shots, width, lanes = guess_ref.shape
    fields = parts * shots
    odd = lax.rem(index_ref[0], 2) == 1
    planes = guess_ref.reshape(layers * fields, width, lanes)
    edge = jnp.where(odd, layers - 1, 0) * fields
    begin = jnp.where(odd, 0, layers - REACH) * fields
    code = jnp.where(odd, 0, layers - 2)
    moves = [(class_ref, held.at[0]), (layer_ref, held.at[1])]
    moves.append((planes.at[pl.ds(edge, fields)], edge_ref))
    for k in range(REACH):
        moves.append(
            (planes.at[pl.ds(begin + k * fields, fields)], near_ref.at[pl.ds(k * fields, fields)])
        )
    copies = []
    for number, (source, target) in enumerate(moves):
        copies.append(pltpu.make_async_copy(source, target, sems.at[number]))
        copies[-1].start()
    copies[0].wait()
    copies[1].wait()
    for kind in range(2):
        for q in range(layers):
            codes_ref[kind, q] = held[kind, q].astype(jnp.float32)
        for k in range(2):
            near_ref[REACH * fields + 2 * kind + k] = held[kind, code + k].astype(jnp.float32)
    for copy in copies[2:]:
        copy.wait()


def fill_send(send_ref, guess_ref, codes_ref, odd, step):
    layers, parts, shots = guess_ref.shape[:3]
    plane = jnp.where(odd, layers - 1 - step, step)
    code = jnp.where(odd, layers - step, step - 1)
    for part in range(parts):
        send_ref[part * shots : (part + 1) * shots] = guess_ref[plane, part]
    send_ref[parts * shots] = codes_ref[0, code]
    send_ref[parts * shots + 1] = codes_ref[1, code]


def orientation(index_ref, layers, depth_total):
    index = index_ref[0]
    odd = lax.rem(index, 2) == 1
    first_plane = index * layers

    def place_of(plane):
        local = plane - first_plane
        return jnp.where(odd, local, layers - 1 - local)

    def inside(place):
        plane = first_plane + jnp.where(odd, place, layers - 1 - place)
        return jnp.where((plane >= 0) & (plane < depth_total), 1.0, 0.0).astype(jnp.float32)

    return odd, place_of, inside


def early_kernel(
    depth_total,
    index_ref,
    wave_ref,
    damp_ref,
    cells_ref,
    wavelet_ref,
    guess_ref,
    near_ref,
    codes_ref,
    field,
    start,
    tables,
    send_ref,
):
    layers, parts, shots, width, lanes = guess_ref.shape
    fields = parts * shots
    odd, place_of, inside = orientation(index_ref, layers, depth_total)
    guess_rows = guess_ref.reshape(layers * fields * width, lanes)
    near_rows = near_ref.reshape(near_ref.shape[0] * width, lanes)
    span = fields * width
    keep = edge_masks(shots, lanes)
    fill_send(send_ref, guess_ref, codes_ref, odd, 1)
    extra = REACH * fields
    for k in range(2):
        pick = jnp.where(odd, k, 1 - k)
        fill_tables(
            tables, k, near_ref[extra + pick], near_ref[extra + 2 + pick], inside(k - 2), wave_ref, damp_ref
        )
    for q in range(layers):
        pick = jnp.where(odd, q, layers - 1 - q)
        fill_tables(
            tables, q + 2, codes_ref[0, pick], codes_ref[1, pick], jnp.float32(1.0), wave_ref, damp_ref
        )

    def bring_near(k, carry):
        bring(near_rows, jnp.where(odd, k, REACH - 1 - k) * span, field, k)
        return carry

    def bring_own(q, carry):
        bring(guess_rows, jnp.where(odd, q, layers - 1 - q) * span, field, q + REACH)
        return carry

    lax.fori_loop(0, REACH, bring_near, 0)
    lax.fori_loop(0, layers, bring_own, 0)

    def start_plane(i, carry):
        stencil_plane(
            ((field, i), (field, i + 1), (field, i + 2)),
            (start, i),
            (tables, i, 0),
            inside(i - 2) * (-1.0 / 30.0),
            keep,
        )
        return carry

    lax.fori_loop(0, layers + 1, start_plane, 0)
    add_sources(start, -2, place_of, cells_ref, wavelet_ref)


def image_kernel(
    depth_total,
    index_ref,
    start,
    tables,
    nearest_ref,
    first,
    split_ref,
    products_ref,
    send_ref,
    second,
):
    _, width, _, shots, lanes = start.shape
    layers = start.shape[0] - 1
    _, _, inside = orientation(index_ref, layers, depth_total)
    keep = edge_masks(shots, lanes)
    send_ref[0] = start[layers]

    def first_plane(j, carry):
        stencil_plane(
            ((start, j), (start, j + 1), (start, j + 2)),
            (first, j),
            (tables, j + 1, 1),
            inside(j - 1) * (1.0 / 30.0),
            keep,
        )
        return carry

    lax.fori_loop(0, layers - 1, first_plane, 0)
    products = jnp.zeros(products_ref.shape, jnp.float32)
    for k in range(layers - 3):
        stencil_plane(
            ((first, k), (first, k + 1), (first, k + 2)),
            (second, k),
            (tables, k + 2, 1),
            1.0 / 30.0,
            keep,
        )
        split_plane(((start, k + 2), (first, k + 1), (second, k)), split_ref, k)
        products += products_of(split_ref, k, width * lanes)
    products_ref[...] = products


def pack_gram(products, shots, cells):
    rows = 2 * BLOCKS * shots
    half = rows // 2
    summed = products[0:rows] + products[rows : 2 * rows] + products[2 * rows : 3 * rows]
    summed = summed[:, 0:rows] + summed[:, rows : 2 * rows] + summed[:, 2 * rows : 3 * rows]
    summed = summed * (1.0 / cells)
    real = summed[0:half, 0:half] + summed[half:rows, half:rows]
    imag = summed[0:half, half:rows] - summed[half:rows, 0:half]
    blocks = []
    for i, j in PAIRS:
        for values in (real, imag):
            blocks.append(values[i * shots : (i + 1) * shots, j * shots : (j + 1) * shots])
    blocks.append(jnp.zeros((shots, 128 - 2 * len(PAIRS) * shots), jnp.float32))
    return jnp.concatenate(blocks, axis=1)


def stage_kernel(stage, depth_total, layers, names, places, *refs):
    refs = dict(zip(names, refs))
    first, second, far_ref = refs["first"], refs["second"], refs["far"]
    _, width, parts, shots, lanes = first.shape
    odd, place_of, inside = orientation(refs["index"], layers, depth_total)
    keep = edge_masks(shots, lanes)
    top = layers - 1 + stage

    def old(name):
        return (refs[name], places[name])

    if stage == 2:
        start = far_ref
        first_table = (refs["far_tables"], 0, 1)
    else:
        field, start = refs["field"], refs["start"]
        first_table = (refs["own_tables"], top + 1, 1)
        if stage == 0:
            start_table = (refs["own_tables"], top + 2, 0)
        else:
            fill_tables(
                refs["tables"],
                0,
                far_ref[parts * shots],
                far_ref[parts * shots + 1],
                inside(jnp.int32(top)),
                refs["wave"],
                refs["damp"],
            )
            start_table = (refs["tables"], 0, 0)
        bring(far_ref.reshape(far_ref.shape[0] * width, lanes), 0, field, 0)
        stencil_plane(
            (old("field_a"), old("field_b"), (field, 0)),
            (start, 0),
            start_table,
            inside(jnp.int32(top)) * (-1.0 / 30.0),
            keep,
        )
        add_sources(start, top, place_of, refs["cells"], refs["wavelet"])
    stencil_plane(
        (old("start_a"), old("start_b"), (start, 0)),
        (first, 0),
        first_table,
        inside(jnp.int32(top - 1)) * (1.0 / 30.0),
        keep,
    )
    stencil_plane(
        (old("first_a"), old("first_b"), (first, 0)),
        (second, 0),
        (refs["own_tables"], top, 1),
        1.0 / 30.0,
        keep,
    )
    split_ref = refs["split"]
    split_plane((old("start_a"), old("first_b"), (second, 0)), split_ref, 0)
    products = refs["products_in"][...] + products_of(split_ref, 0, width * lanes)
    if stage < 2:
        refs["products"][...] = products
    else:
        packed = pack_gram(products, shots, float(depth_total * width * lanes))
        for copy in range(refs["grams"].shape[0]):
            refs["grams"][copy] = packed


def back_kernel(
    index_ref, wave_ref, damp_ref, grams_ref, *rest
):
    basis_ref, hessenberg_ref = rest[-2:]
    layers, parts, shots, width, y = basis_ref.shape
    fields = parts * shots
    rows = BLOCKS * fields
    half = rows // 2
    tile = shots
    tiles = BLOCKS
    spread = BLOCKS * rows
    lanes = 128
    lead = spread - lanes

    grams = [grams_ref[i] for i in range(grams_ref.shape[0])]
    while len(grams) > 1:
        grams = [sum(grams[i : i + 2]) for i in range(0, len(grams), 2)]
    packed = grams[0]
    turned = packed.T
    lane = lax.broadcasted_iota(jnp.int32, (tile, lanes), 1)
    sub = lax.broadcasted_iota(jnp.int32, (tile, lanes), 0)
    wide_lane = lax.broadcasted_iota(jnp.int32, (tile, 2 * lanes), 1)
    wide_sub = lax.broadcasted_iota(jnp.int32, (tile, 2 * lanes), 0)
    real, imag = [], []
    for t in range(tiles):
        match = (wide_lane < spread) & (lax.rem(wide_lane, half) == wide_sub + t * tile)
        unit = jnp.where(match, 1.0, 0.0).astype(jnp.float32)
        blank = jnp.zeros((tile, lanes), jnp.float32)
        parts_of = []
        for part in range(2):
            blocks = [jnp.zeros((tile, lead), jnp.float32)]
            for j in range(tiles):
                if j >= t:
                    begin = (2 * PAIRS.index((t, j)) + part) * tile
                    blocks.append(packed[:, begin : begin + tile])
                else:
                    begin = (2 * PAIRS.index((j, t)) + part) * tile
                    block = turned[begin : begin + tile, 0:tile]
                    blocks.append(block if part == 0 else -block)
            blocks.append(jnp.zeros((tile, lanes - lead - half), jnp.float32))
            parts_of.append(jnp.concatenate(blocks, axis=1))
        real.append(unit + jnp.concatenate([blank, parts_of[0]], axis=1))
        imag.append(jnp.concatenate([blank, parts_of[1]], axis=1))
    pivots = []
    for k in range(half):
        owner, row = divmod(k, tile)
        row_real = real[owner][row : row + 1]
        row_imag = imag[owner][row : row + 1]
        spot = spread + k
        pivot = row_real[:, spot : spot + 1]
        pivots.append(pivot)
        inverse = 1.0 / pivot
        for t in range(owner, tiles):
            column_real = real[t][:, spot : spot + 1] * inverse
            column_imag = imag[t][:, spot : spot + 1] * inverse
            if t == owner:
                below = sub[:, 0:1] > row
                column_real = jnp.where(below, column_real, 0.0)
                column_imag = jnp.where(below, column_imag, 0.0)
            new_real = real[t] - (column_real * row_real - column_imag * row_imag)
            new_imag = imag[t] - (column_real * row_imag + column_imag * row_real)
            real[t], imag[t] = new_real, new_imag
    for t in range(tiles):
        scales = lax.rsqrt(jnp.concatenate(pivots[t * tile : (t + 1) * tile], axis=0))
        real[t] = real[t] * scales
        imag[t] = imag[t] * scales

    last_real, last_imag = real[tiles - 1], imag[tiles - 1]
    first_half = lax.rem(wide_lane, rows) < half
    mix = jnp.concatenate(
        [
            jnp.where(first_half, last_real, last_imag),
            jnp.where(first_half, -last_imag, last_real),
        ],
        axis=0,
    )
    pieces = []
    for part in range(3):
        short = mix.astype(jnp.bfloat16)
        pieces.append(short)
        mix = mix - short.astype(jnp.float32)
    left = jnp.concatenate(pieces, axis=0)[:, 0:spread]

    odd = lax.rem(index_ref[0], 2) == 1
    out_rows = basis_ref.reshape(layers * fields * width, y)
    spots = [
        (ref, spot)
        for ref in rest[:-2]
        for spot in range(ref.shape[1] // (width * y))
    ]
    group = 16
    for q in range(layers):
        source, spot = spots[q]
        plane = jnp.where(odd, q, layers - 1 - q)
        for begin in range(0, width, group):
            offset = (spot * width + begin) * y
            mixed = jnp.dot(
                left, source[:, offset : offset + group * y], preferred_element_type=jnp.float32
            )
            mixed = mixed[0:fields] + mixed[fields : 2 * fields] + mixed[2 * fields : 3 * fields]
            for column in range(group):
                out_rows[pl.ds(plane * (fields * width) + begin + column, fields, stride=width), :] = mixed[
                    :, column * y : (column + 1) * y
                ]

    wide = 2 * tile
    full_real = jnp.concatenate(real, axis=0)
    full_imag = jnp.concatenate(imag, axis=0)
    row_index = lax.broadcasted_iota(jnp.int32, (half, wide), 0)
    column_index = lax.broadcasted_iota(jnp.int32, (half, wide), 1)
    upper = row_index <= column_index + tile
    factor_real = jnp.where(upper, full_real[:, spread + tile : spread + half], 0.0)
    factor_imag = jnp.where(upper, full_imag[:, spread + tile : spread + half], 0.0)
    lower_real = full_real[0:wide, 0:wide]
    lower_imag = full_imag[0:wide, 0:wide]

    def times(left, right):
        return lax.dot_general(
            left,
            right,
            (((1,), (1,)), ((), ())),
            precision=lax.Precision.HIGHEST,
            preferred_element_type=jnp.float32,
        )

    shift_real, shift_imag = shift_of(wave_ref, damp_ref)
    diagonal = lax.broadcasted_iota(jnp.int32, (wide, half), 0) == lax.broadcasted_iota(
        jnp.int32, (wide, half), 1
    )
    hessenberg_ref[0] = (
        times(lower_real, factor_real)
        + times(lower_imag, factor_imag)
        + jnp.where(diagonal, shift_real, 0.0)
    )
    hessenberg_ref[1] = (
        times(lower_real, factor_imag)
        - times(lower_imag, factor_real)
        + jnp.where(diagonal, shift_imag, 0.0)
    )


def shards(initial_guess, velocity_class, layer_code, wavenumber, damping, shot_cells, wavelet):
    layers, parts, shots, width, lanes = initial_guess.shape
    devices = lax.axis_size("gz")
    fields = parts * shots
    rows = BLOCKS * fields
    span = width * lanes
    depth_total = devices * layers
    index = lax.axis_index("gz").astype(jnp.int32).reshape(1)
    shot_cells = shot_cells.T

    smem = pl.BlockSpec(memory_space=pltpu.SMEM)
    vmem = pl.BlockSpec(memory_space=pltpu.VMEM)
    hbm = pl.BlockSpec(memory_space=pl.ANY)
    params = pltpu.CompilerParams(vmem_limit_bytes=VMEM_BYTES)


    def float_shape(*dims):
        return jax.ShapeDtypeStruct(dims, jnp.float32)

    odd_to_even = [(i, i + 1) for i in range(1, devices - 1, 2)]
    even_to_odd = [(i, i + 1) for i in range(0, devices, 2)]
    far_pairs = odd_to_even + [(b, a) for a, b in odd_to_even]
    near_pairs = even_to_odd + [(b, a) for a, b in even_to_odd]

    edge, near, codes = pl.pallas_call(
        pack_kernel,
        out_shape=(
            float_shape(fields, width, lanes),
            float_shape(REACH * fields + 4, width, lanes),
            float_shape(2, layers, width, lanes),
        ),
        in_specs=[smem, hbm, hbm, hbm],
        out_specs=(vmem, vmem, vmem),
        scratch_shapes=[
            pltpu.VMEM((2, layers, width, lanes), jnp.int32),
            pltpu.SemaphoreType.DMA((3 + REACH,)),
        ],
        compiler_params=params,
        name="pack",
    )(
        index,
        *(
            pltpu.with_memory_space_constraint(array, pltpu.HBM)
            for array in (initial_guess, velocity_class, layer_code)
        ),
    )
    nearest = lax.ppermute(edge, "gz", far_pairs)
    near = lax.ppermute(near, "gz", near_pairs)

    def planes(count):
        return float_shape(count, width, parts, shots, lanes)

    def tables(count):
        return float_shape(count, 4, width, lanes)

    def split(count):
        return jax.ShapeDtypeStruct((BLOCKS * rows, count * span), jnp.bfloat16)

    def scratch(shape):
        return pltpu.VMEM(shape.shape, shape.dtype)

    products = float_shape(BLOCKS * rows, BLOCKS * rows)
    cost = pl.CostEstimate(flops=10_000_000, bytes_accessed=16_000_000, transcendentals=0)
    common = (index, wavenumber, damping, shot_cells, wavelet)
    send_shape = float_shape(fields + 2, width, lanes)
    field, start, own_tables, send = pl.pallas_call(
        functools.partial(early_kernel, depth_total),
        out_shape=(planes(layers + REACH), planes(layers + 1), tables(layers + 2), send_shape),
        in_specs=[smem] * 5 + [vmem] * 3,
        out_specs=(vmem,) * 4,
        compiler_params=params,
        cost_estimate=cost,
        name="early",
    )(*common, initial_guess, near, codes)
    second_far = lax.ppermute(send, "gz", far_pairs)
    first, early_split, early_products, send = pl.pallas_call(
        functools.partial(image_kernel, depth_total),
        out_shape=(planes(layers - 1), split(layers - 3), products, planes(1)),
        in_specs=[smem] + [vmem] * 3,
        out_specs=(vmem,) * 4,
        scratch_shapes=[scratch(planes(layers - 3))],
        compiler_params=params,
        cost_estimate=cost,
        name="images",
    )(index, start, own_tables, nearest)
    third_far = lax.ppermute(send, "gz", far_pairs)
    shapes = {
        "field": planes(1),
        "start": planes(1),
        "first": planes(1),
        "second": planes(1),
        "tables": tables(1),
        "split": split(1),
        "products": products,
        "grams": float_shape(devices, shots, 128),
    }

    def run_stage(stage, far, old, extra, outs, temporaries):
        inputs = {"index": index}
        if stage < 2:
            inputs = dict(zip(("index", "wave", "damp", "cells", "wavelet"), common))
        scalars = len(inputs)
        inputs["far"] = far
        inputs.update({name: array for name, (array, _) in old.items()})
        inputs.update(extra)
        results = pl.pallas_call(
            functools.partial(
                stage_kernel,
                stage,
                depth_total,
                layers,
                list(inputs) + outs + temporaries,
                {name: place for name, (_, place) in old.items()},
            ),
            out_shape=tuple(shapes[name] for name in outs),
            in_specs=[smem] * scalars + [vmem] * (len(inputs) - scalars),
            out_specs=(vmem,) * len(outs),
            scratch_shapes=[scratch(shapes[name]) for name in temporaries],
            compiler_params=params,
            cost_estimate=cost,
            name="stage_%d" % stage,
        )(*inputs.values())
        return dict(zip(outs, results))

    zero = run_stage(
        0,
        nearest,
        {
            "field_a": (field, layers + 1),
            "field_b": (field, layers + 2),
            "start_a": (start, layers - 1),
            "start_b": (start, layers),
            "first_a": (first, layers - 3),
            "first_b": (first, layers - 2),
        },
        {"own_tables": own_tables, "products_in": early_products},
        ["field", "start", "first", "split", "products"],
        ["second"],
    )
    one = run_stage(
        1,
        second_far,
        {
            "field_a": (field, layers + 2),
            "field_b": (zero["field"], 0),
            "start_a": (start, layers),
            "start_b": (zero["start"], 0),
            "first_a": (first, layers - 2),
            "first_b": (zero["first"], 0),
        },
        {"own_tables": own_tables, "products_in": zero["products"]},
        ["start", "first", "tables", "split", "products"],
        ["field", "second"],
    )
    two = run_stage(
        2,
        third_far,
        {
            "start_a": (zero["start"], 0),
            "start_b": (one["start"], 0),
            "first_a": (zero["first"], 0),
            "first_b": (one["first"], 0),
        },
        {"own_tables": own_tables, "far_tables": one["tables"], "products_in": one["products"]},
        ["split", "grams"],
        ["first", "second"],
    )
    grams = two["grams"]
    grams = lax.all_to_all(grams, "gz", 0, 0)
    basis_two, turned = pl.pallas_call(
        back_kernel,
        out_shape=(
            jax.ShapeDtypeStruct(initial_guess.shape, jnp.float32),
            jax.ShapeDtypeStruct((2, 2 * shots, BLOCKS * shots), jnp.float32),
        ),
        in_specs=[smem] * 3 + [vmem] * 5,
        out_specs=(vmem, vmem),
        compiler_params=params,
        name="back",
    )(index, wavenumber, damping, grams, early_split, zero["split"], one["split"], two["split"])
    return basis_two, jnp.swapaxes(turned, 1, 2)


def solution(mesh):
    return jax.shard_map(
        shards,
        mesh=mesh,
        in_specs=(
            P(("freq", "gz"), None, None, None, None),
            P("gz", None, None),
            P("gz", None, None),
            P("freq"),
            P(),
            P(),
            P("freq", None),
        ),
        out_specs=(P(("freq", "gz"), None, None, None, None), P("freq", None, None)),
        check_vma=False,
    )
```

```python
import functools

import jax
import jax.numpy as jnp
from jax import lax
from jax.experimental import pallas as pl
from jax.experimental.pallas import tpu as pltpu
from jax.sharding import PartitionSpec as P

SHIFT_BASE = 2.9
BLOCKS = 3
REACH = 3
VMEM_BYTES = 24 * 1024 * 1024
PAIRS = ((0, 0), (0, 1), (0, 2), (1, 1), (1, 2), (2, 2))


def shift_of(wave_ref, damp_ref):
    classes, levels = wave_ref.shape[0], damp_ref.shape[0]
    wave_mean = sum(wave_ref[i] for i in range(classes)) * (1.0 / classes)
    damp_mean = sum(damp_ref[i] for i in range(levels)) * (1.0 / levels)
    return SHIFT_BASE - wave_mean, -wave_mean * damp_mean


def edge_masks(shots, lanes):
    lane = lax.broadcasted_iota(jnp.int32, (shots, lanes), 1)
    return (
        jnp.where(lane == 0, 0.0, 1.0).astype(jnp.float32),
        jnp.where(lane == lanes - 1, 0.0, 1.0).astype(jnp.float32),
    )


def stencil_plane(sources, target, table, scale, keep):
    (low, low_plane), (mid, mid_plane), (high, high_plane) = sources
    out, out_plane = target
    table_ref, table_plane, kind = table
    width = table_ref.shape[2]
    left, right = keep

    def load(column):
        center, away = [], []
        for part in range(2):
            v = mid[mid_plane, column, part]
            d = low[low_plane, column, part] + high[high_plane, column, part]
            center.append(v)
            away.append(d + 3.0 * v)
        return center, away

    here_v, here_u = load(0)
    before_v = [jnp.zeros_like(v) for v in here_v]
    before_u = before_v
    for column in range(width):
        if column + 1 < width:
            after_v, after_u = load(column + 1)
        else:
            after_v = [jnp.zeros_like(v) for v in here_v]
            after_u = after_v
        real_row, imag_row = [
            jnp.broadcast_to(table_ref[table_plane, 2 * kind + part, column : column + 1, :], here_v[0].shape)
            for part in range(2)
        ]
        for part in range(2):
            near = here_u[part] + (before_v[part] + after_v[part])
            wide = (before_u[part] + after_u[part]) + (3.0 * here_u[part] + 5.0 * here_v[part])
            sides = pltpu.roll(wide, 1, 1) * left + pltpu.roll(wide, 127, 1) * right
            total = 3.0 * wide + 5.0 * near + sides
            if part == 0:
                own = real_row * here_v[0] + imag_row * here_v[1]
            else:
                own = real_row * here_v[1] - imag_row * here_v[0]
            out[out_plane, column, part] = own - scale * total
        before_v, before_u, here_v, here_u = here_v, here_u, after_v, after_u


def bring(rows, first_row, field, plane):
    width, parts, shots = field.shape[1:4]
    for column in range(width):
        for part in range(parts):
            field[plane, column, part] = rows[
                pl.ds(first_row + part * shots * width + column, shots, stride=width), :
            ]


def fill_tables(tables, plane, labels, codes, inside_flag, wave_ref, damp_ref):
    shift_real, shift_imag = shift_of(wave_ref, damp_ref)
    wave = jnp.zeros(labels.shape, jnp.float32)
    for i in range(wave_ref.shape[0]):
        wave = jnp.where(labels == float(i), wave_ref[i], wave)
    loss = jnp.zeros(labels.shape, jnp.float32)
    for i in range(damp_ref.shape[0]):
        loss = jnp.where(codes == float(i), damp_ref[i], loss)
    real = 185.0 / 30.0 - wave
    imag = wave * loss
    tables[plane, 0] = -inside_flag * real
    tables[plane, 1] = -inside_flag * imag
    tables[plane, 2] = inside_flag * (real - shift_real)
    tables[plane, 3] = inside_flag * (imag + shift_imag)


def add_sources(start, first_start, place_of, cells_ref, wavelet_ref):
    count, _, _, shots, lanes = start.shape
    lane_row = lax.broadcasted_iota(jnp.int32, (1, lanes), 1)
    for s in range(shots):
        place = place_of(cells_ref[0, s]) - first_start

        @pl.when((place >= 0) & (place < count))
        def _():
            column = cells_ref[1, s]
            hit = lane_row == cells_ref[2, s]
            for part in range(2):
                start[place, column, part, s : s + 1, :] += jnp.where(hit, wavelet_ref[part, s], 0.0)


def split_plane(sources, split_ref, spot_plane):
    width, _, shots, lanes = sources[0][0].shape[1:]
    rows = BLOCKS * 2 * shots
    for column in range(width):
        pieces = [ref[plane, column, part] for part in range(2) for ref, plane in sources]
        begin = (spot_plane * width + column) * lanes
        for pair in range(BLOCKS):
            value = jnp.concatenate(pieces[2 * pair : 2 * pair + 2], axis=0)
            for part in range(3):
                short = value.astype(jnp.bfloat16)
                row = part * rows + 2 * shots * pair
                split_ref[row : row + 2 * shots, begin : begin + lanes] = short
                if part < 2:
                    value = value - short.astype(jnp.float32)


def products_of(split_ref, spot_plane, span):
    chunk = split_ref[:, spot_plane * span : (spot_plane + 1) * span]
    return lax.dot_general(
        chunk, chunk, (((1,), (1,)), ((), ())), preferred_element_type=jnp.float32
    )


def pack_kernel(index_ref, guess_ref, class_ref, layer_ref, edge_ref, next_ref, near_ref, codes_ref, held, sems):
    layers, parts, shots, width, lanes = guess_ref.shape
    fields = parts * shots
    odd = lax.rem(index_ref[0], 2) == 1
    planes = guess_ref.reshape(layers * fields, width, lanes)
    edge = jnp.where(odd, layers - 1, 0) * fields
    begin = jnp.where(odd, 0, layers - REACH) * fields
    code = jnp.where(odd, 0, layers - 2)
    edge_code = jnp.where(odd, layers - 1, 0)
    moves = [(class_ref, held.at[0]), (layer_ref, held.at[1])]
    moves.append((planes.at[pl.ds(edge, fields)], edge_ref.at[pl.ds(0, fields)]))
    for k in range(REACH):
        moves.append(
            (planes.at[pl.ds(begin + k * fields, fields)], near_ref.at[pl.ds(k * fields, fields)])
        )
    copies = []
    for number, (source, target) in enumerate(moves):
        copies.append(pltpu.make_async_copy(source, target, sems.at[number]))
        copies[-1].start()
    copies[0].wait()
    copies[1].wait()
    for kind in range(2):
        for q in range(layers):
            codes_ref[kind, q] = held[kind, q].astype(jnp.float32)
        for k in range(2):
            near_ref[REACH * fields + 2 * kind + k] = held[kind, code + k].astype(jnp.float32)
        edge_ref[fields + kind] = held[kind, edge_code].astype(jnp.float32)
    for copy in copies[2:]:
        copy.wait()
    following = jnp.where(odd, REACH - 1, 0) * fields
    next_ref[...] = near_ref[pl.ds(following, fields)]


def orientation(index_ref, layers, depth_total):
    index = index_ref[0]
    odd = lax.rem(index, 2) == 1
    first_plane = index * layers

    def place_of(plane):
        local = plane - first_plane
        return jnp.where(odd, local, layers - 1 - local)

    def inside(place):
        plane = first_plane + jnp.where(odd, place, layers - 1 - place)
        return jnp.where((plane >= 0) & (plane < depth_total), 1.0, 0.0).astype(jnp.float32)

    return odd, place_of, inside


def early_kernel(
    depth_total,
    index_ref,
    wave_ref,
    damp_ref,
    cells_ref,
    wavelet_ref,
    edge_ref,
    own_ref,
    near_ref,
    codes_ref,
    field,
    start,
    tables,
):
    _, layers, width, lanes = codes_ref.shape
    parts, shots = start.shape[2:4]
    fields = parts * shots
    odd, place_of, inside = orientation(index_ref, layers, depth_total)
    own_rows = own_ref.reshape(own_ref.shape[0] * width, lanes)
    edge_rows = edge_ref.reshape(edge_ref.shape[0] * width, lanes)
    near_rows = near_ref.reshape(near_ref.shape[0] * width, lanes)
    span = fields * width
    keep = edge_masks(shots, lanes)
    extra = REACH * fields
    for k in range(2):
        pick = jnp.where(odd, k, 1 - k)
        fill_tables(
            tables, k, near_ref[extra + pick], near_ref[extra + 2 + pick], inside(k - 2), wave_ref, damp_ref
        )
    for q in range(layers):
        pick = jnp.where(odd, q, layers - 1 - q)
        fill_tables(
            tables, q + 2, codes_ref[0, pick], codes_ref[1, pick], jnp.float32(1.0), wave_ref, damp_ref
        )

    def bring_near(k, carry):
        bring(near_rows, jnp.where(odd, k, REACH - 1 - k) * span, field, k)
        return carry

    def bring_own(q, carry):
        bring(own_rows, jnp.where(odd, q, REACH - 1 - q) * span, field, q + REACH)
        return carry

    lax.fori_loop(0, REACH, bring_near, 0)
    lax.fori_loop(0, REACH, bring_own, 0)
    bring(edge_rows, 0, field, REACH + layers - 1)

    def start_plane(i, carry):
        stencil_plane(
            ((field, i), (field, i + 1), (field, i + 2)),
            (start, i),
            (tables, i, 0),
            inside(i - 2) * (-1.0 / 30.0),
            keep,
        )
        return carry

    lax.fori_loop(0, layers + 1, start_plane, 0)
    add_sources(start, -2, place_of, cells_ref, wavelet_ref)


def image_kernel(
    depth_total,
    index_ref,
    start,
    tables,
    first,
    split_ref,
    products_ref,
    send_ref,
    second,
):
    _, width, _, shots, lanes = start.shape
    layers = start.shape[0] - 1
    _, _, inside = orientation(index_ref, layers, depth_total)
    keep = edge_masks(shots, lanes)
    send_ref[0] = start[layers]

    def first_plane(j, carry):
        stencil_plane(
            ((start, j), (start, j + 1), (start, j + 2)),
            (first, j),
            (tables, j + 1, 1),
            inside(j - 1) * (1.0 / 30.0),
            keep,
        )
        return carry

    lax.fori_loop(0, layers - 1, first_plane, 0)
    products = jnp.zeros(products_ref.shape, jnp.float32)
    for k in range(layers - 3):
        stencil_plane(
            ((first, k), (first, k + 1), (first, k + 2)),
            (second, k),
            (tables, k + 2, 1),
            1.0 / 30.0,
            keep,
        )
        split_plane(((start, k + 2), (first, k + 1), (second, k)), split_ref, k)
        products += products_of(split_ref, k, width * lanes)
    products_ref[...] = products


def pack_gram(products, shots, cells):
    rows = 2 * BLOCKS * shots
    half = rows // 2
    summed = products[0:rows] + products[rows : 2 * rows] + products[2 * rows : 3 * rows]
    summed = summed[:, 0:rows] + summed[:, rows : 2 * rows] + summed[:, 2 * rows : 3 * rows]
    summed = summed * (1.0 / cells)
    real = summed[0:half, 0:half] + summed[half:rows, half:rows]
    imag = summed[0:half, half:rows] - summed[half:rows, 0:half]
    blocks = []
    for i, j in PAIRS:
        for values in (real, imag):
            blocks.append(values[i * shots : (i + 1) * shots, j * shots : (j + 1) * shots])
    blocks.append(jnp.zeros((shots, 128 - 2 * len(PAIRS) * shots), jnp.float32))
    return jnp.concatenate(blocks, axis=1)


def stage_kernel(stage, depth_total, layers, names, places, *refs):
    refs = dict(zip(names, refs))
    first, second, far_ref = refs["first"], refs["second"], refs["far"]
    _, width, parts, shots, lanes = first.shape
    odd, place_of, inside = orientation(refs["index"], layers, depth_total)
    keep = edge_masks(shots, lanes)
    top = layers - 1 + stage

    def old(name):
        return (refs[name], places[name])

    if stage == 2:
        start = far_ref
        first_table = (refs["far_tables"], 0, 1)
    else:
        field, start = refs["field"], refs["start"]
        first_table = (refs["own_tables"], top + 1, 1)
        if stage == 0:
            start_table = (refs["own_tables"], top + 2, 0)
        else:
            fill_tables(
                refs["tables"],
                0,
                refs["nearest"][parts * shots],
                refs["nearest"][parts * shots + 1],
                inside(jnp.int32(top)),
                refs["wave"],
                refs["damp"],
            )
            start_table = (refs["tables"], 0, 0)
        bring(far_ref.reshape(far_ref.shape[0] * width, lanes), 0, field, 0)
        stencil_plane(
            (old("field_a"), old("field_b"), (field, 0)),
            (start, 0),
            start_table,
            inside(jnp.int32(top)) * (-1.0 / 30.0),
            keep,
        )
        add_sources(start, top, place_of, refs["cells"], refs["wavelet"])
    stencil_plane(
        (old("start_a"), old("start_b"), (start, 0)),
        (first, 0),
        first_table,
        inside(jnp.int32(top - 1)) * (1.0 / 30.0),
        keep,
    )
    stencil_plane(
        (old("first_a"), old("first_b"), (first, 0)),
        (second, 0),
        (refs["own_tables"], top, 1),
        1.0 / 30.0,
        keep,
    )
    split_ref = refs["split"]
    split_plane((old("start_a"), old("first_b"), (second, 0)), split_ref, 0)
    products = refs["products_in"][...] + products_of(split_ref, 0, width * lanes)
    if stage < 2:
        refs["products"][...] = products
    else:
        packed = pack_gram(products, shots, float(depth_total * width * lanes))
        for copy in range(refs["grams"].shape[0]):
            refs["grams"][copy] = packed


def back_kernel(
    index_ref, wave_ref, damp_ref, grams_ref, *rest
):
    basis_ref, hessenberg_ref = rest[-2:]
    layers, parts, shots, width, y = basis_ref.shape
    fields = parts * shots
    rows = BLOCKS * fields
    half = rows // 2
    tile = shots
    tiles = BLOCKS
    spread = BLOCKS * rows
    lanes = 128
    lead = spread - lanes

    grams = [grams_ref[i] for i in range(grams_ref.shape[0])]
    while len(grams) > 1:
        grams = [sum(grams[i : i + 2]) for i in range(0, len(grams), 2)]
    packed = grams[0]
    turned = packed.T
    lane = lax.broadcasted_iota(jnp.int32, (tile, lanes), 1)
    sub = lax.broadcasted_iota(jnp.int32, (tile, lanes), 0)
    wide_lane = lax.broadcasted_iota(jnp.int32, (tile, 2 * lanes), 1)
    wide_sub = lax.broadcasted_iota(jnp.int32, (tile, 2 * lanes), 0)
    real, imag = [], []
    for t in range(tiles):
        match = (wide_lane < spread) & (lax.rem(wide_lane, half) == wide_sub + t * tile)
        unit = jnp.where(match, 1.0, 0.0).astype(jnp.float32)
        blank = jnp.zeros((tile, lanes), jnp.float32)
        parts_of = []
        for part in range(2):
            blocks = [jnp.zeros((tile, lead), jnp.float32)]
            for j in range(tiles):
                if j >= t:
                    begin = (2 * PAIRS.index((t, j)) + part) * tile
                    blocks.append(packed[:, begin : begin + tile])
                else:
                    begin = (2 * PAIRS.index((j, t)) + part) * tile
                    block = turned[begin : begin + tile, 0:tile]
                    blocks.append(block if part == 0 else -block)
            blocks.append(jnp.zeros((tile, lanes - lead - half), jnp.float32))
            parts_of.append(jnp.concatenate(blocks, axis=1))
        real.append(unit + jnp.concatenate([blank, parts_of[0]], axis=1))
        imag.append(jnp.concatenate([blank, parts_of[1]], axis=1))
    pivots = []
    for owner in range(tiles):
        spots = [spread + owner * tile + r for r in range(tile)]
        shape = (tile, lanes)
        ahead = {
            (t, r): [
                jnp.broadcast_to(values[t][:, spots[r] : spots[r] + 1], shape) for values in (real, imag)
            ]
            for t in range(owner, tiles)
            for r in range(tile)
        }
        for r in range(tile):
            own_real, own_imag = ahead[owner, r]
            pivot = jnp.broadcast_to(own_real[r : r + 1], shape)
            pivots.append(pivot)
            inverse = pl.reciprocal(pivot, approx=True)
            for _ in range(2):
                inverse = inverse * (2.0 - pivot * inverse)
            scaled = {}
            for t in range(owner, tiles):
                column_real, column_imag = [value * inverse for value in ahead[t, r]]
                if t == owner:
                    column_real = jnp.where(sub > r, column_real, 0.0)
                    column_imag = jnp.where(sub > r, column_imag, 0.0)
                scaled[t] = column_real, column_imag
            for later in range(r + 1, tile):
                entry_real = jnp.broadcast_to(own_real[later : later + 1], shape)
                entry_imag = jnp.broadcast_to(own_imag[later : later + 1], shape)
                for t in range(owner, tiles):
                    column_real, column_imag = scaled[t]
                    old_real, old_imag = ahead[t, later]
                    ahead[t, later] = [
                        old_real - (column_real * entry_real + column_imag * entry_imag),
                        old_imag - (column_imag * entry_real - column_real * entry_imag),
                    ]
            row_real = real[owner][r : r + 1]
            row_imag = imag[owner][r : r + 1]
            for t in range(owner, tiles):
                column_real, column_imag = [
                    jnp.concatenate([value, value], axis=1) for value in scaled[t]
                ]
                new_real = real[t] - (column_real * row_real - column_imag * row_imag)
                new_imag = imag[t] - (column_real * row_imag + column_imag * row_real)
                real[t], imag[t] = new_real, new_imag
    for t in range(tiles):
        scales = pivots[t * tile]
        for r in range(1, tile):
            scales = jnp.where(sub == r, pivots[t * tile + r], scales)
        scales = lax.rsqrt(scales)
        scales = jnp.concatenate([scales, scales], axis=1)
        real[t] = real[t] * scales
        imag[t] = imag[t] * scales

    last_real, last_imag = real[tiles - 1], imag[tiles - 1]
    first_half = lax.rem(wide_lane, rows) < half
    mix = jnp.concatenate(
        [
            jnp.where(first_half, last_real, last_imag),
            jnp.where(first_half, -last_imag, last_real),
        ],
        axis=0,
    )
    pieces = []
    for part in range(3):
        short = mix.astype(jnp.bfloat16)
        pieces.append(short)
        mix = mix - short.astype(jnp.float32)
    left = jnp.concatenate(pieces, axis=0)[:, 0:spread]

    odd = lax.rem(index_ref[0], 2) == 1
    out_rows = basis_ref.reshape(layers * fields * width, y)
    spots = [
        (ref, spot)
        for ref in rest[:-2]
        for spot in range(ref.shape[1] // (width * y))
    ]
    group = 16
    for q in range(layers):
        source, spot = spots[q]
        plane = jnp.where(odd, q, layers - 1 - q)
        for begin in range(0, width, group):
            offset = (spot * width + begin) * y
            mixed = jnp.dot(
                left, source[:, offset : offset + group * y], preferred_element_type=jnp.float32
            )
            mixed = mixed[0:fields] + mixed[fields : 2 * fields] + mixed[2 * fields : 3 * fields]
            for column in range(group):
                out_rows[pl.ds(plane * (fields * width) + begin + column, fields, stride=width), :] = mixed[
                    :, column * y : (column + 1) * y
                ]

    wide = 2 * tile
    full_real = jnp.concatenate(real, axis=0)
    full_imag = jnp.concatenate(imag, axis=0)
    row_index = lax.broadcasted_iota(jnp.int32, (half, wide), 0)
    column_index = lax.broadcasted_iota(jnp.int32, (half, wide), 1)
    upper = row_index <= column_index + tile
    factor_real = jnp.where(upper, full_real[:, spread + tile : spread + half], 0.0)
    factor_imag = jnp.where(upper, full_imag[:, spread + tile : spread + half], 0.0)
    lower_real = full_real[0:wide, 0:wide]
    lower_imag = full_imag[0:wide, 0:wide]

    def times(left, right):
        return lax.dot_general(
            left,
            right,
            (((1,), (1,)), ((), ())),
            precision=lax.Precision.HIGHEST,
            preferred_element_type=jnp.float32,
        )

    shift_real, shift_imag = shift_of(wave_ref, damp_ref)
    diagonal = lax.broadcasted_iota(jnp.int32, (wide, half), 0) == lax.broadcasted_iota(
        jnp.int32, (wide, half), 1
    )
    hessenberg_ref[0] = (
        times(lower_real, factor_real)
        + times(lower_imag, factor_imag)
        + jnp.where(diagonal, shift_real, 0.0)
    )
    hessenberg_ref[1] = (
        times(lower_real, factor_imag)
        - times(lower_imag, factor_real)
        + jnp.where(diagonal, shift_imag, 0.0)
    )


def shards(initial_guess, velocity_class, layer_code, wavenumber, damping, shot_cells, wavelet):
    layers, parts, shots, width, lanes = initial_guess.shape
    devices = lax.axis_size("gz")
    assert layers == REACH + 1 and devices % 2 == 0
    fields = parts * shots
    rows = BLOCKS * fields
    span = width * lanes
    depth_total = devices * layers
    index = lax.axis_index("gz").astype(jnp.int32).reshape(1)
    shot_cells = shot_cells.T

    smem = pl.BlockSpec(memory_space=pltpu.SMEM)
    vmem = pl.BlockSpec(memory_space=pltpu.VMEM)
    hbm = pl.BlockSpec(memory_space=pl.ANY)
    params = pltpu.CompilerParams(vmem_limit_bytes=VMEM_BYTES)


    def float_shape(*dims):
        return jax.ShapeDtypeStruct(dims, jnp.float32)

    odd_to_even = [(i, i + 1) for i in range(1, devices - 1, 2)]
    even_to_odd = [(i, i + 1) for i in range(0, devices, 2)]
    far_pairs = odd_to_even + [(b, a) for a, b in odd_to_even]
    near_pairs = even_to_odd + [(b, a) for a, b in even_to_odd]

    edge, following, near, codes = pl.pallas_call(
        pack_kernel,
        out_shape=(
            float_shape(fields + 2, width, lanes),
            float_shape(fields, width, lanes),
            float_shape(REACH * fields + 4, width, lanes),
            float_shape(2, layers, width, lanes),
        ),
        in_specs=[smem, hbm, hbm, hbm],
        out_specs=(vmem, vmem, vmem, vmem),
        scratch_shapes=[
            pltpu.VMEM((2, layers, width, lanes), jnp.int32),
            pltpu.SemaphoreType.DMA((3 + REACH,)),
        ],
        compiler_params=params,
        name="pack",
    )(
        index,
        *(
            pltpu.with_memory_space_constraint(array, pltpu.HBM)
            for array in (initial_guess, velocity_class, layer_code)
        ),
    )
    nearest = lax.ppermute(edge, "gz", far_pairs)
    second_far = lax.ppermute(following, "gz", far_pairs)
    own = near
    near = lax.ppermute(own, "gz", near_pairs)

    def planes(count):
        return float_shape(count, width, parts, shots, lanes)

    def tables(count):
        return float_shape(count, 4, width, lanes)

    def split(count):
        return jax.ShapeDtypeStruct((BLOCKS * rows, count * span), jnp.bfloat16)

    def scratch(shape):
        return pltpu.VMEM(shape.shape, shape.dtype)

    products = float_shape(BLOCKS * rows, BLOCKS * rows)
    cost = pl.CostEstimate(flops=10_000_000, bytes_accessed=16_000_000, transcendentals=0)
    common = (index, wavenumber, damping, shot_cells, wavelet)
    field, start, own_tables = pl.pallas_call(
        functools.partial(early_kernel, depth_total),
        out_shape=(planes(layers + REACH), planes(layers + 1), tables(layers + 2)),
        in_specs=[smem] * 5 + [vmem] * 4,
        out_specs=(vmem,) * 3,
        compiler_params=params,
        cost_estimate=cost,
        name="early",
    )(*common, edge, own, near, codes)
    first, early_split, early_products, send = pl.pallas_call(
        functools.partial(image_kernel, depth_total),
        out_shape=(planes(layers - 1), split(layers - 3), products, planes(1)),
        in_specs=[smem] + [vmem] * 2,
        out_specs=(vmem,) * 4,
        scratch_shapes=[scratch(planes(layers - 3))],
        compiler_params=params,
        cost_estimate=cost,
        name="images",
    )(index, start, own_tables)
    third_far = lax.ppermute(send, "gz", far_pairs)
    shapes = {
        "field": planes(1),
        "start": planes(1),
        "first": planes(1),
        "second": planes(1),
        "tables": tables(1),
        "split": split(1),
        "products": products,
        "grams": float_shape(devices, shots, 128),
    }

    def run_stage(stage, far, old, extra, outs, temporaries):
        inputs = {"index": index}
        if stage < 2:
            inputs = dict(zip(("index", "wave", "damp", "cells", "wavelet"), common))
        scalars = len(inputs)
        inputs["far"] = far
        inputs.update({name: array for name, (array, _) in old.items()})
        inputs.update(extra)
        results = pl.pallas_call(
            functools.partial(
                stage_kernel,
                stage,
                depth_total,
                layers,
                list(inputs) + outs + temporaries,
                {name: place for name, (_, place) in old.items()},
            ),
            out_shape=tuple(shapes[name] for name in outs),
            in_specs=[smem] * scalars + [vmem] * (len(inputs) - scalars),
            out_specs=(vmem,) * len(outs),
            scratch_shapes=[scratch(shapes[name]) for name in temporaries],
            compiler_params=params,
            cost_estimate=cost,
            name="stage_%d" % stage,
        )(*inputs.values())
        return dict(zip(outs, results))

    zero = run_stage(
        0,
        nearest,
        {
            "field_a": (field, layers + 1),
            "field_b": (field, layers + 2),
            "start_a": (start, layers - 1),
            "start_b": (start, layers),
            "first_a": (first, layers - 3),
            "first_b": (first, layers - 2),
        },
        {"own_tables": own_tables, "products_in": early_products},
        ["field", "start", "first", "split", "products"],
        ["second"],
    )
    one = run_stage(
        1,
        second_far,
        {
            "field_a": (field, layers + 2),
            "field_b": (zero["field"], 0),
            "start_a": (start, layers),
            "start_b": (zero["start"], 0),
            "first_a": (first, layers - 2),
            "first_b": (zero["first"], 0),
        },
        {"own_tables": own_tables, "products_in": zero["products"], "nearest": nearest},
        ["start", "first", "tables", "split", "products"],
        ["field", "second"],
    )
    two = run_stage(
        2,
        third_far,
        {
            "start_a": (zero["start"], 0),
            "start_b": (one["start"], 0),
            "first_a": (zero["first"], 0),
            "first_b": (one["first"], 0),
        },
        {"own_tables": own_tables, "far_tables": one["tables"], "products_in": one["products"]},
        ["split", "grams"],
        ["first", "second"],
    )
    grams = two["grams"]
    grams = lax.all_to_all(grams, "gz", 0, 0)
    basis_two, turned = pl.pallas_call(
        back_kernel,
        out_shape=(
            jax.ShapeDtypeStruct(initial_guess.shape, jnp.float32),
            jax.ShapeDtypeStruct((2, 2 * shots, BLOCKS * shots), jnp.float32),
        ),
        in_specs=[smem] * 3 + [vmem] * 5,
        out_specs=(vmem, vmem),
        compiler_params=params,
        name="back",
    )(index, wavenumber, damping, grams, early_split, zero["split"], one["split"], two["split"])
    return basis_two, jnp.swapaxes(turned, 1, 2)


def solution(mesh):
    return jax.shard_map(
        shards,
        mesh=mesh,
        in_specs=(
            P(("freq", "gz"), None, None, None, None),
            P("gz", None, None),
            P("gz", None, None),
            P("freq"),
            P(),
            P(),
            P("freq", None),
        ),
        out_specs=(P(("freq", "gz"), None, None, None, None), P("freq", None, None)),
        check_vma=False,
    )
```

```python
import functools

import jax
import jax.numpy as jnp
from jax import lax
from jax.experimental import pallas as pl
from jax.experimental.pallas import tpu as pltpu
from jax.sharding import PartitionSpec as P

SHIFT_BASE = 2.9
BLOCKS = 3
REACH = 3
VMEM_BYTES = 24 * 1024 * 1024
PAIRS = ((0, 0), (0, 1), (0, 2), (1, 1), (1, 2), (2, 2))


def shift_of(wave_ref, damp_ref):
    classes, levels = wave_ref.shape[0], damp_ref.shape[0]
    wave_mean = sum(wave_ref[i] for i in range(classes)) * (1.0 / classes)
    damp_mean = sum(damp_ref[i] for i in range(levels)) * (1.0 / levels)
    return SHIFT_BASE - wave_mean, -wave_mean * damp_mean


def edge_masks(shots, lanes):
    lane = lax.broadcasted_iota(jnp.int32, (shots, lanes), 1)
    return (
        jnp.where(lane == 0, 0.0, 1.0).astype(jnp.float32),
        jnp.where(lane == lanes - 1, 0.0, 1.0).astype(jnp.float32),
    )


def stencil_plane(sources, target, table, scale, keep):
    (low, low_plane), (mid, mid_plane), (high, high_plane) = sources
    out, out_plane = target
    table_ref, table_plane, kind = table
    width = table_ref.shape[2]
    left, right = keep

    def load(column):
        center, away = [], []
        for part in range(2):
            v = mid[mid_plane, column, part]
            d = low[low_plane, column, part] + high[high_plane, column, part]
            center.append(v)
            away.append(d + 3.0 * v)
        return center, away

    here_v, here_u = load(0)
    before_v = [jnp.zeros_like(v) for v in here_v]
    before_u = before_v
    for column in range(width):
        if column + 1 < width:
            after_v, after_u = load(column + 1)
        else:
            after_v = [jnp.zeros_like(v) for v in here_v]
            after_u = after_v
        real_row, imag_row = [
            jnp.broadcast_to(table_ref[table_plane, 2 * kind + part, column : column + 1, :], here_v[0].shape)
            for part in range(2)
        ]
        for part in range(2):
            near = here_u[part] + (before_v[part] + after_v[part])
            wide = (before_u[part] + after_u[part]) + (3.0 * here_u[part] + 5.0 * here_v[part])
            sides = pltpu.roll(wide, 1, 1) * left + pltpu.roll(wide, 127, 1) * right
            total = 3.0 * wide + 5.0 * near + sides
            if part == 0:
                own = real_row * here_v[0] + imag_row * here_v[1]
            else:
                own = real_row * here_v[1] - imag_row * here_v[0]
            out[out_plane, column, part] = own - scale * total
        before_v, before_u, here_v, here_u = here_v, here_u, after_v, after_u


def bring(rows, first_row, field, plane):
    width, parts, shots = field.shape[1:4]
    for column in range(width):
        for part in range(parts):
            field[plane, column, part] = rows[
                pl.ds(first_row + part * shots * width + column, shots, stride=width), :
            ]


def fill_tables(tables, plane, labels, codes, inside_flag, wave_ref, damp_ref):
    shift_real, shift_imag = shift_of(wave_ref, damp_ref)
    wave = jnp.zeros(labels.shape, jnp.float32)
    for i in range(wave_ref.shape[0]):
        wave = jnp.where(labels == float(i), wave_ref[i], wave)
    loss = jnp.zeros(labels.shape, jnp.float32)
    for i in range(damp_ref.shape[0]):
        loss = jnp.where(codes == float(i), damp_ref[i], loss)
    real = 185.0 / 30.0 - wave
    imag = wave * loss
    tables[plane, 0] = -inside_flag * real
    tables[plane, 1] = -inside_flag * imag
    tables[plane, 2] = inside_flag * (real - shift_real)
    tables[plane, 3] = inside_flag * (imag + shift_imag)


def add_sources(start, first_start, place_of, cells_ref, wavelet_ref):
    count, _, _, shots, lanes = start.shape
    lane_row = lax.broadcasted_iota(jnp.int32, (1, lanes), 1)
    for s in range(shots):
        place = place_of(cells_ref[0, s]) - first_start

        @pl.when((place >= 0) & (place < count))
        def _():
            column = cells_ref[1, s]
            hit = lane_row == cells_ref[2, s]
            for part in range(2):
                start[place, column, part, s : s + 1, :] += jnp.where(hit, wavelet_ref[part, s], 0.0)


def split_plane(sources, split_ref, spot_plane):
    width, _, shots, lanes = sources[0][0].shape[1:]
    rows = BLOCKS * 2 * shots
    for column in range(width):
        pieces = [ref[plane, column, part] for part in range(2) for ref, plane in sources]
        begin = (spot_plane * width + column) * lanes
        for pair in range(BLOCKS):
            value = jnp.concatenate(pieces[2 * pair : 2 * pair + 2], axis=0)
            for part in range(3):
                short = value.astype(jnp.bfloat16)
                row = part * rows + 2 * shots * pair
                split_ref[row : row + 2 * shots, begin : begin + lanes] = short
                if part < 2:
                    value = value - short.astype(jnp.float32)


def products_of(split_ref, spot_plane, span):
    chunk = split_ref[:, spot_plane * span : (spot_plane + 1) * span]
    return lax.dot_general(
        chunk, chunk, (((1,), (1,)), ((), ())), preferred_element_type=jnp.float32
    )


def pack_kernel(guess_ref, class_ref, layer_ref, edge_ref, next_ref, near_ref, codes_ref, held, sems):
    layers, parts, shots, width, lanes = guess_ref.shape
    fields = parts * shots
    odd = lax.rem(lax.axis_index("gz"), 2) == 1
    planes = guess_ref.reshape(layers * fields, width, lanes)
    edge = jnp.where(odd, layers - 1, 0) * fields
    begin = jnp.where(odd, 0, layers - REACH) * fields
    code = jnp.where(odd, 0, layers - 2)
    edge_code = jnp.where(odd, layers - 1, 0)
    moves = [(class_ref, held.at[0]), (layer_ref, held.at[1])]
    moves.append((planes.at[pl.ds(edge, fields)], edge_ref.at[pl.ds(0, fields)]))
    for k in range(REACH):
        moves.append(
            (planes.at[pl.ds(begin + k * fields, fields)], near_ref.at[pl.ds(k * fields, fields)])
        )
    copies = []
    for number, (source, target) in enumerate(moves):
        copies.append(pltpu.make_async_copy(source, target, sems.at[number]))
        copies[-1].start()
    copies[0].wait()
    copies[1].wait()
    for kind in range(2):
        for q in range(layers):
            codes_ref[kind, q] = held[kind, q].astype(jnp.float32)
        for k in range(2):
            near_ref[REACH * fields + 2 * kind + k] = held[kind, code + k].astype(jnp.float32)
        edge_ref[fields + kind] = held[kind, edge_code].astype(jnp.float32)
    for copy in copies[2:]:
        copy.wait()
    following = jnp.where(odd, REACH - 1, 0) * fields
    next_ref[...] = near_ref[pl.ds(following, fields)]


def orientation(layers, depth_total):
    index = lax.axis_index("gz")
    odd = lax.rem(index, 2) == 1
    first_plane = index * layers

    def place_of(plane):
        local = plane - first_plane
        return jnp.where(odd, local, layers - 1 - local)

    def inside(place):
        plane = first_plane + jnp.where(odd, place, layers - 1 - place)
        return jnp.where((plane >= 0) & (plane < depth_total), 1.0, 0.0).astype(jnp.float32)

    return odd, place_of, inside


def early_kernel(
    depth_total,
    wave_ref,
    damp_ref,
    cells_ref,
    wavelet_ref,
    edge_ref,
    own_ref,
    near_ref,
    codes_ref,
    field,
    start,
    tables,
    shift_ref,
):
    _, layers, width, lanes = codes_ref.shape
    parts, shots = start.shape[2:4]
    fields = parts * shots
    odd, place_of, inside = orientation(layers, depth_total)
    own_rows = own_ref.reshape(own_ref.shape[0] * width, lanes)
    edge_rows = edge_ref.reshape(edge_ref.shape[0] * width, lanes)
    near_rows = near_ref.reshape(near_ref.shape[0] * width, lanes)
    span = fields * width
    keep = edge_masks(shots, lanes)
    diagonal = lax.broadcasted_iota(jnp.int32, shift_ref.shape[1:], 0) == lax.broadcasted_iota(
        jnp.int32, shift_ref.shape[1:], 1
    )
    for part, value in enumerate(shift_of(wave_ref, damp_ref)):
        shift_ref[part] = jnp.where(diagonal, value, 0.0)

    extra = REACH * fields
    for k in range(2):
        pick = jnp.where(odd, k, 1 - k)
        fill_tables(
            tables, k, near_ref[extra + pick], near_ref[extra + 2 + pick], inside(k - 2), wave_ref, damp_ref
        )
    for q in range(layers):
        pick = jnp.where(odd, q, layers - 1 - q)
        fill_tables(
            tables, q + 2, codes_ref[0, pick], codes_ref[1, pick], jnp.float32(1.0), wave_ref, damp_ref
        )

    def bring_near(k, carry):
        bring(near_rows, jnp.where(odd, k, REACH - 1 - k) * span, field, k)
        return carry

    def bring_own(q, carry):
        bring(own_rows, jnp.where(odd, q, REACH - 1 - q) * span, field, q + REACH)
        return carry

    lax.fori_loop(0, REACH, bring_near, 0)
    lax.fori_loop(0, REACH, bring_own, 0)
    bring(edge_rows, 0, field, REACH + layers - 1)

    def start_plane(i, carry):
        stencil_plane(
            ((field, i), (field, i + 1), (field, i + 2)),
            (start, i),
            (tables, i, 0),
            inside(i - 2) * (-1.0 / 30.0),
            keep,
        )
        return carry

    lax.fori_loop(0, layers + 1, start_plane, 0)
    add_sources(start, -2, place_of, cells_ref, wavelet_ref)


def image_kernel(
    depth_total,
    start,
    tables,
    first,
    split_ref,
    products_ref,
    send_ref,
    second,
):
    _, width, _, shots, lanes = start.shape
    layers = start.shape[0] - 1
    _, _, inside = orientation(layers, depth_total)
    keep = edge_masks(shots, lanes)
    send_ref[0] = start[layers]

    def first_plane(j, carry):
        stencil_plane(
            ((start, j), (start, j + 1), (start, j + 2)),
            (first, j),
            (tables, j + 1, 1),
            inside(j - 1) * (1.0 / 30.0),
            keep,
        )
        return carry

    lax.fori_loop(0, layers - 1, first_plane, 0)
    products = jnp.zeros(products_ref.shape, jnp.float32)
    for k in range(layers - 3):
        stencil_plane(
            ((first, k), (first, k + 1), (first, k + 2)),
            (second, k),
            (tables, k + 2, 1),
            1.0 / 30.0,
            keep,
        )
        split_plane(((start, k + 2), (first, k + 1), (second, k)), split_ref, k)
        products += products_of(split_ref, k, width * lanes)
    products_ref[...] = products


def pack_gram(products, shots, cells):
    rows = 2 * BLOCKS * shots
    half = rows // 2
    summed = products[0:rows] + products[rows : 2 * rows] + products[2 * rows : 3 * rows]
    summed = summed[:, 0:rows] + summed[:, rows : 2 * rows] + summed[:, 2 * rows : 3 * rows]
    summed = summed * (1.0 / cells)
    real = summed[0:half, 0:half] + summed[half:rows, half:rows]
    imag = summed[0:half, half:rows] - summed[half:rows, 0:half]
    blocks = []
    for i, j in PAIRS:
        for values in (real, imag):
            blocks.append(values[i * shots : (i + 1) * shots, j * shots : (j + 1) * shots])
    blocks.append(jnp.zeros((shots, 128 - 2 * len(PAIRS) * shots), jnp.float32))
    return jnp.concatenate(blocks, axis=1)


def stage_kernel(stage, depth_total, layers, names, places, *refs):
    refs = dict(zip(names, refs))
    first, second, far_ref = refs["first"], refs["second"], refs["far"]
    _, width, parts, shots, lanes = first.shape
    odd, place_of, inside = orientation(layers, depth_total)
    keep = edge_masks(shots, lanes)
    top = layers - 1 + stage

    def old(name):
        return (refs[name], places[name])

    if stage == 2:
        start = far_ref
        first_table = (refs["far_tables"], 0, 1)
    else:
        field, start = refs["field"], refs["start"]
        first_table = (refs["own_tables"], top + 1, 1)
        if stage == 0:
            start_table = (refs["own_tables"], top + 2, 0)
        else:
            fill_tables(
                refs["tables"],
                0,
                refs["nearest"][parts * shots],
                refs["nearest"][parts * shots + 1],
                inside(jnp.int32(top)),
                refs["wave"],
                refs["damp"],
            )
            start_table = (refs["tables"], 0, 0)
        bring(far_ref.reshape(far_ref.shape[0] * width, lanes), 0, field, 0)
        stencil_plane(
            (old("field_a"), old("field_b"), (field, 0)),
            (start, 0),
            start_table,
            inside(jnp.int32(top)) * (-1.0 / 30.0),
            keep,
        )
        add_sources(start, top, place_of, refs["cells"], refs["wavelet"])
    stencil_plane(
        (old("start_a"), old("start_b"), (start, 0)),
        (first, 0),
        first_table,
        inside(jnp.int32(top - 1)) * (1.0 / 30.0),
        keep,
    )
    stencil_plane(
        (old("first_a"), old("first_b"), (first, 0)),
        (second, 0),
        (refs["own_tables"], top, 1),
        1.0 / 30.0,
        keep,
    )
    split_ref = refs["split"]
    split_plane((old("start_a"), old("first_b"), (second, 0)), split_ref, 0)
    products = refs["products_in"][...] + products_of(split_ref, 0, width * lanes)
    if stage < 2:
        refs["products"][...] = products
    else:
        packed = pack_gram(products, shots, float(depth_total * width * lanes))
        for copy in range(refs["grams"].shape[0]):
            refs["grams"][copy] = packed


def back_kernel(
    shift_ref, grams_ref, *rest
):
    basis_ref, hessenberg_ref = rest[-2:]
    layers, parts, shots, width, y = basis_ref.shape
    fields = parts * shots
    rows = BLOCKS * fields
    half = rows // 2
    tile = shots
    tiles = BLOCKS
    spread = BLOCKS * rows
    lanes = 128
    lead = spread - lanes

    grams = [grams_ref[i] for i in range(grams_ref.shape[0])]
    while len(grams) > 1:
        grams = [sum(grams[i : i + 2]) for i in range(0, len(grams), 2)]
    packed = grams[0]
    turned = packed.T
    lane = lax.broadcasted_iota(jnp.int32, (tile, lanes), 1)
    sub = lax.broadcasted_iota(jnp.int32, (tile, lanes), 0)
    wide_lane = lax.broadcasted_iota(jnp.int32, (tile, 2 * lanes), 1)
    wide_sub = lax.broadcasted_iota(jnp.int32, (tile, 2 * lanes), 0)
    real, imag = [], []
    for t in range(tiles):
        match = (wide_lane < spread) & (lax.rem(wide_lane, half) == wide_sub + t * tile)
        unit = jnp.where(match, 1.0, 0.0).astype(jnp.float32)
        blank = jnp.zeros((tile, lanes), jnp.float32)
        parts_of = []
        for part in range(2):
            blocks = [jnp.zeros((tile, lead), jnp.float32)]
            for j in range(tiles):
                if j >= t:
                    begin = (2 * PAIRS.index((t, j)) + part) * tile
                    blocks.append(packed[:, begin : begin + tile])
                else:
                    begin = (2 * PAIRS.index((j, t)) + part) * tile
                    block = turned[begin : begin + tile, 0:tile]
                    blocks.append(block if part == 0 else -block)
            blocks.append(jnp.zeros((tile, lanes - lead - half), jnp.float32))
            parts_of.append(jnp.concatenate(blocks, axis=1))
        real.append(unit + jnp.concatenate([blank, parts_of[0]], axis=1))
        imag.append(jnp.concatenate([blank, parts_of[1]], axis=1))
    pivots = []
    for owner in range(tiles):
        spots = [spread + owner * tile + r for r in range(tile)]
        shape = (tile, lanes)
        ahead = {
            (t, r): [
                jnp.broadcast_to(values[t][:, spots[r] : spots[r] + 1], shape) for values in (real, imag)
            ]
            for t in range(owner, tiles)
            for r in range(tile)
        }
        for r in range(tile):
            own_real, own_imag = ahead[owner, r]
            pivot = jnp.broadcast_to(own_real[r : r + 1], shape)
            pivots.append(pivot)
            inverse = pl.reciprocal(pivot, approx=True)
            for _ in range(2):
                inverse = inverse * (2.0 - pivot * inverse)
            scaled = {}
            for t in range(owner, tiles):
                column_real, column_imag = [value * inverse for value in ahead[t, r]]
                if t == owner:
                    column_real = jnp.where(sub > r, column_real, 0.0)
                    column_imag = jnp.where(sub > r, column_imag, 0.0)
                scaled[t] = column_real, column_imag
            for later in range(r + 1, tile):
                entry_real = jnp.broadcast_to(own_real[later : later + 1], shape)
                entry_imag = jnp.broadcast_to(own_imag[later : later + 1], shape)
                for t in range(owner, tiles):
                    column_real, column_imag = scaled[t]
                    old_real, old_imag = ahead[t, later]
                    ahead[t, later] = [
                        old_real - (column_real * entry_real + column_imag * entry_imag),
                        old_imag - (column_imag * entry_real - column_real * entry_imag),
                    ]
            row_real = real[owner][r : r + 1]
            row_imag = imag[owner][r : r + 1]
            for t in range(owner, tiles):
                column_real, column_imag = [
                    jnp.concatenate([value, value], axis=1) for value in scaled[t]
                ]
                new_real = real[t] - (column_real * row_real - column_imag * row_imag)
                new_imag = imag[t] - (column_real * row_imag + column_imag * row_real)
                real[t], imag[t] = new_real, new_imag
    for t in range(tiles):
        scales = pivots[t * tile]
        for r in range(1, tile):
            scales = jnp.where(sub == r, pivots[t * tile + r], scales)
        scales = lax.rsqrt(scales)
        scales = jnp.concatenate([scales, scales], axis=1)
        real[t] = real[t] * scales
        imag[t] = imag[t] * scales

    last_real, last_imag = real[tiles - 1], imag[tiles - 1]
    first_half = lax.rem(wide_lane, rows) < half
    mix = jnp.concatenate(
        [
            jnp.where(first_half, last_real, last_imag),
            jnp.where(first_half, -last_imag, last_real),
        ],
        axis=0,
    )
    pieces = []
    for part in range(3):
        short = mix.astype(jnp.bfloat16)
        pieces.append(short)
        mix = mix - short.astype(jnp.float32)
    left = jnp.concatenate(pieces, axis=0)[:, 0:spread]

    odd = lax.rem(lax.axis_index("gz"), 2) == 1
    out_rows = basis_ref.reshape(layers * fields * width, y)
    spots = [
        (ref, spot)
        for ref in rest[:-2]
        for spot in range(ref.shape[1] // (width * y))
    ]
    group = 16
    for q in range(layers):
        source, spot = spots[q]
        plane = jnp.where(odd, q, layers - 1 - q)
        for begin in range(0, width, group):
            offset = (spot * width + begin) * y
            mixed = jnp.dot(
                left, source[:, offset : offset + group * y], preferred_element_type=jnp.float32
            )
            mixed = mixed[0:fields] + mixed[fields : 2 * fields] + mixed[2 * fields : 3 * fields]
            for column in range(group):
                out_rows[pl.ds(plane * (fields * width) + begin + column, fields, stride=width), :] = mixed[
                    :, column * y : (column + 1) * y
                ]

    wide = 2 * tile
    full_real = jnp.concatenate(real, axis=0)
    full_imag = jnp.concatenate(imag, axis=0)
    row_index = lax.broadcasted_iota(jnp.int32, (half, wide), 0)
    column_index = lax.broadcasted_iota(jnp.int32, (half, wide), 1)
    upper = row_index <= column_index + tile
    factor_real = jnp.where(upper, full_real[:, spread + tile : spread + half], 0.0)
    factor_imag = jnp.where(upper, full_imag[:, spread + tile : spread + half], 0.0)
    lower_real = full_real[0:wide, 0:wide]
    lower_imag = full_imag[0:wide, 0:wide]

    def times(left, right):
        return lax.dot_general(
            left,
            right,
            (((1,), (1,)), ((), ())),
            precision=lax.Precision.HIGHEST,
            preferred_element_type=jnp.float32,
        )

    hessenberg_ref[0] = (
        times(lower_real, factor_real)
        + times(lower_imag, factor_imag)
        + shift_ref[0]
    )
    hessenberg_ref[1] = (
        times(lower_real, factor_imag)
        - times(lower_imag, factor_real)
        + shift_ref[1]
    )


def shards(initial_guess, velocity_class, layer_code, wavenumber, damping, shot_cells, wavelet):
    layers, parts, shots, width, lanes = initial_guess.shape
    devices = lax.axis_size("gz")
    assert layers == REACH + 1 and devices % 2 == 0
    fields = parts * shots
    rows = BLOCKS * fields
    span = width * lanes
    depth_total = devices * layers
    shot_cells = shot_cells.T

    smem = pl.BlockSpec(memory_space=pltpu.SMEM)
    vmem = pl.BlockSpec(memory_space=pltpu.VMEM)
    hbm = pl.BlockSpec(memory_space=pl.ANY)
    params = pltpu.CompilerParams(vmem_limit_bytes=VMEM_BYTES)


    def float_shape(*dims):
        return jax.ShapeDtypeStruct(dims, jnp.float32)

    odd_to_even = [(i, i + 1) for i in range(1, devices - 1, 2)]
    even_to_odd = [(i, i + 1) for i in range(0, devices, 2)]
    far_pairs = odd_to_even + [(b, a) for a, b in odd_to_even]
    near_pairs = even_to_odd + [(b, a) for a, b in even_to_odd]

    edge, following, near, codes = pl.pallas_call(
        pack_kernel,
        out_shape=(
            float_shape(fields + 2, width, lanes),
            float_shape(fields, width, lanes),
            float_shape(REACH * fields + 4, width, lanes),
            float_shape(2, layers, width, lanes),
        ),
        in_specs=[hbm, hbm, hbm],
        out_specs=(vmem, vmem, vmem, vmem),
        scratch_shapes=[
            pltpu.VMEM((2, layers, width, lanes), jnp.int32),
            pltpu.SemaphoreType.DMA((3 + REACH,)),
        ],
        compiler_params=params,
        name="pack",
    )(
        *(
            pltpu.with_memory_space_constraint(array, pltpu.HBM)
            for array in (initial_guess, velocity_class, layer_code)
        )
    )
    nearest = lax.ppermute(edge, "gz", far_pairs)
    second_far = lax.ppermute(following, "gz", far_pairs)
    own = near
    near = lax.ppermute(own, "gz", near_pairs)

    def planes(count):
        return float_shape(count, width, parts, shots, lanes)

    def tables(count):
        return float_shape(count, 4, width, lanes)

    def split(count):
        return jax.ShapeDtypeStruct((BLOCKS * rows, count * span), jnp.bfloat16)

    def scratch(shape):
        return pltpu.VMEM(shape.shape, shape.dtype)

    products = float_shape(BLOCKS * rows, BLOCKS * rows)
    cost = pl.CostEstimate(flops=10_000_000, bytes_accessed=16_000_000, transcendentals=0)
    common = (wavenumber, damping, shot_cells, wavelet)
    turned_shape = float_shape(2, 2 * shots, BLOCKS * shots)
    field, start, own_tables, shift = pl.pallas_call(
        functools.partial(early_kernel, depth_total),
        out_shape=(planes(layers + REACH), planes(layers + 1), tables(layers + 2), turned_shape),
        in_specs=[smem] * 4 + [vmem] * 4,
        out_specs=(vmem,) * 4,
        compiler_params=params,
        cost_estimate=cost,
        name="early",
    )(*common, edge, own, near, codes)
    first, early_split, early_products, send = pl.pallas_call(
        functools.partial(image_kernel, depth_total),
        out_shape=(planes(layers - 1), split(layers - 3), products, planes(1)),
        in_specs=[vmem] * 2,
        out_specs=(vmem,) * 4,
        scratch_shapes=[scratch(planes(layers - 3))],
        compiler_params=params,
        cost_estimate=cost,
        name="images",
    )(start, own_tables)
    third_far = lax.ppermute(send, "gz", far_pairs)
    shapes = {
        "field": planes(1),
        "start": planes(1),
        "first": planes(1),
        "second": planes(1),
        "tables": tables(1),
        "split": split(1),
        "products": products,
        "grams": float_shape(devices, shots, 128),
    }

    def run_stage(stage, far, old, extra, outs, temporaries):
        inputs = {}
        if stage < 2:
            inputs = dict(zip(("wave", "damp", "cells", "wavelet"), common))
        scalars = len(inputs)
        inputs["far"] = far
        inputs.update({name: array for name, (array, _) in old.items()})
        inputs.update(extra)
        results = pl.pallas_call(
            functools.partial(
                stage_kernel,
                stage,
                depth_total,
                layers,
                list(inputs) + outs + temporaries,
                {name: place for name, (_, place) in old.items()},
            ),
            out_shape=tuple(shapes[name] for name in outs),
            in_specs=[smem] * scalars + [vmem] * (len(inputs) - scalars),
            out_specs=(vmem,) * len(outs),
            scratch_shapes=[scratch(shapes[name]) for name in temporaries],
            compiler_params=params,
            cost_estimate=cost,
            name="stage_%d" % stage,
        )(*inputs.values())
        return dict(zip(outs, results))

    zero = run_stage(
        0,
        nearest,
        {
            "field_a": (field, layers + 1),
            "field_b": (field, layers + 2),
            "start_a": (start, layers - 1),
            "start_b": (start, layers),
            "first_a": (first, layers - 3),
            "first_b": (first, layers - 2),
        },
        {"own_tables": own_tables, "products_in": early_products},
        ["field", "start", "first", "split", "products"],
        ["second"],
    )
    one = run_stage(
        1,
        second_far,
        {
            "field_a": (field, layers + 2),
            "field_b": (zero["field"], 0),
            "start_a": (start, layers),
            "start_b": (zero["start"], 0),
            "first_a": (first, layers - 2),
            "first_b": (zero["first"], 0),
        },
        {"own_tables": own_tables, "products_in": zero["products"], "nearest": nearest},
        ["start", "first", "tables", "split", "products"],
        ["field", "second"],
    )
    two = run_stage(
        2,
        third_far,
        {
            "start_a": (zero["start"], 0),
            "start_b": (one["start"], 0),
            "first_a": (zero["first"], 0),
            "first_b": (one["first"], 0),
        },
        {"own_tables": own_tables, "far_tables": one["tables"], "products_in": one["products"]},
        ["split", "grams"],
        ["first", "second"],
    )
    grams = two["grams"]
    grams = lax.all_to_all(grams, "gz", 0, 0)
    basis_two, turned = pl.pallas_call(
        back_kernel,
        out_shape=(
            jax.ShapeDtypeStruct(initial_guess.shape, jnp.float32),
            turned_shape,
        ),
        in_specs=[vmem] * 6,
        out_specs=(vmem, vmem),
        compiler_params=params,
        name="back",
    )(shift, grams, early_split, zero["split"], one["split"], two["split"])
    return basis_two, jnp.swapaxes(turned, 1, 2)


def solution(mesh):
    return jax.shard_map(
        shards,
        mesh=mesh,
        in_specs=(
            P(("freq", "gz"), None, None, None, None),
            P("gz", None, None),
            P("gz", None, None),
            P("freq"),
            P(),
            P(),
            P("freq", None),
        ),
        out_specs=(P(("freq", "gz"), None, None, None, None), P("freq", None, None)),
        check_vma=False,
    )
```

```python
import functools

import jax
import jax.numpy as jnp
from jax import lax
from jax.experimental import pallas as pl
from jax.experimental.pallas import tpu as pltpu
from jax.sharding import PartitionSpec as P

SHIFT_BASE = 2.9
BLOCKS = 3
REACH = 3
VMEM_BYTES = 24 * 1024 * 1024
PAIRS = ((0, 0), (0, 1), (0, 2), (1, 1), (1, 2), (2, 2))


def shift_of(wave_ref, damp_ref):
    classes, levels = wave_ref.shape[0], damp_ref.shape[0]
    wave_mean = sum(wave_ref[i] for i in range(classes)) * (1.0 / classes)
    damp_mean = sum(damp_ref[i] for i in range(levels)) * (1.0 / levels)
    return SHIFT_BASE - wave_mean, -wave_mean * damp_mean


def edge_masks(shots, lanes):
    lane = lax.broadcasted_iota(jnp.int32, (shots, lanes), 1)
    return (
        jnp.where(lane == 0, 0.0, 1.0).astype(jnp.float32),
        jnp.where(lane == lanes - 1, 0.0, 1.0).astype(jnp.float32),
    )


def stencil_plane(sources, target, table, scale, keep):
    (low, low_plane), (mid, mid_plane), (high, high_plane) = sources
    out, out_plane = target
    table_ref, table_plane, kind = table
    width = table_ref.shape[2]
    left, right = keep

    def load(column):
        center, away = [], []
        for part in range(2):
            v = mid[mid_plane, column, part]
            d = low[low_plane, column, part] + high[high_plane, column, part]
            center.append(v)
            away.append(d + 3.0 * v)
        return center, away

    here_v, here_u = load(0)
    before_v = [jnp.zeros_like(v) for v in here_v]
    before_u = before_v
    for column in range(width):
        if column + 1 < width:
            after_v, after_u = load(column + 1)
        else:
            after_v = [jnp.zeros_like(v) for v in here_v]
            after_u = after_v
        real_row, imag_row = [
            jnp.broadcast_to(table_ref[table_plane, 2 * kind + part, column : column + 1, :], here_v[0].shape)
            for part in range(2)
        ]
        for part in range(2):
            near = here_u[part] + (before_v[part] + after_v[part])
            wide = (before_u[part] + after_u[part]) + (3.0 * here_u[part] + 5.0 * here_v[part])
            sides = pltpu.roll(wide, 1, 1) * left + pltpu.roll(wide, 127, 1) * right
            total = 3.0 * wide + 5.0 * near + sides
            if part == 0:
                own = real_row * here_v[0] + imag_row * here_v[1]
            else:
                own = real_row * here_v[1] - imag_row * here_v[0]
            out[out_plane, column, part] = own - scale * total
        before_v, before_u, here_v, here_u = here_v, here_u, after_v, after_u


def bring(rows, first_row, field, plane):
    width, parts, shots = field.shape[1:4]
    for column in range(width):
        for part in range(parts):
            field[plane, column, part] = rows[
                pl.ds(first_row + part * shots * width + column, shots, stride=width), :
            ]


def fill_tables(tables, plane, labels, codes, inside_flag, wave_ref, damp_ref):
    shift_real, shift_imag = shift_of(wave_ref, damp_ref)
    wave = jnp.zeros(labels.shape, jnp.float32)
    for i in range(wave_ref.shape[0]):
        wave = jnp.where(labels == float(i), wave_ref[i], wave)
    loss = jnp.zeros(labels.shape, jnp.float32)
    for i in range(damp_ref.shape[0]):
        loss = jnp.where(codes == float(i), damp_ref[i], loss)
    real = 185.0 / 30.0 - wave
    imag = wave * loss
    tables[plane, 0] = -inside_flag * real
    tables[plane, 1] = -inside_flag * imag
    tables[plane, 2] = inside_flag * (real - shift_real)
    tables[plane, 3] = inside_flag * (imag + shift_imag)


def add_sources(start, first_start, place_of, cells_ref, wavelet_ref):
    count, _, _, shots, lanes = start.shape
    lane_row = lax.broadcasted_iota(jnp.int32, (1, lanes), 1)
    for s in range(shots):
        place = place_of(cells_ref[0, s]) - first_start

        @pl.when((place >= 0) & (place < count))
        def _():
            column = cells_ref[1, s]
            hit = lane_row == cells_ref[2, s]
            for part in range(2):
                start[place, column, part, s : s + 1, :] += jnp.where(hit, wavelet_ref[part, s], 0.0)


def split_level(source, level, split_ref):
    ref, plane = source
    width, parts, shots, lanes = ref.shape[1:]
    fields = parts * shots
    for column in range(width):
        value = ref[plane, column].reshape(fields, lanes)
        for part in range(3):
            short = value.astype(jnp.bfloat16)
            row = (part * BLOCKS + level) * fields
            split_ref[row : row + fields, column * lanes : (column + 1) * lanes] = short
            if part < 2:
                value = value - short.astype(jnp.float32)


def products_of(split_ref):
    chunk = split_ref[...]
    return lax.dot_general(
        chunk, chunk, (((1,), (1,)), ((), ())), preferred_element_type=jnp.float32
    )


def pack_kernel(guess_ref, class_ref, layer_ref, edge_ref, next_ref, near_ref, codes_ref, held, sems):
    layers, parts, shots, width, lanes = guess_ref.shape
    fields = parts * shots
    odd = lax.rem(lax.axis_index("gz"), 2) == 1
    planes = guess_ref.reshape(layers * fields, width, lanes)
    edge = jnp.where(odd, layers - 1, 0) * fields
    begin = jnp.where(odd, 0, layers - REACH) * fields
    code = jnp.where(odd, 0, layers - 2)
    edge_code = jnp.where(odd, layers - 1, 0)
    moves = [(class_ref, held.at[0]), (layer_ref, held.at[1])]
    moves.append((planes.at[pl.ds(edge, fields)], edge_ref.at[pl.ds(0, fields)]))
    for k in range(REACH):
        moves.append(
            (planes.at[pl.ds(begin + k * fields, fields)], near_ref.at[pl.ds(k * fields, fields)])
        )
    copies = []
    for number, (source, target) in enumerate(moves):
        copies.append(pltpu.make_async_copy(source, target, sems.at[number]))
        copies[-1].start()
    copies[0].wait()
    copies[1].wait()
    for kind in range(2):
        for q in range(layers):
            codes_ref[kind, q] = held[kind, q].astype(jnp.float32)
        for k in range(2):
            near_ref[REACH * fields + 2 * kind + k] = held[kind, code + k].astype(jnp.float32)
        edge_ref[fields + kind] = held[kind, edge_code].astype(jnp.float32)
    for copy in copies[2:]:
        copy.wait()
    following = jnp.where(odd, REACH - 1, 0) * fields
    next_ref[...] = near_ref[pl.ds(following, fields)]


def orientation(layers, depth_total):
    index = lax.axis_index("gz")
    odd = lax.rem(index, 2) == 1
    first_plane = index * layers

    def place_of(plane):
        local = plane - first_plane
        return jnp.where(odd, local, layers - 1 - local)

    def inside(place):
        plane = first_plane + jnp.where(odd, place, layers - 1 - place)
        return jnp.where((plane >= 0) & (plane < depth_total), 1.0, 0.0).astype(jnp.float32)

    return odd, place_of, inside


def early_kernel(
    depth_total,
    wave_ref,
    damp_ref,
    cells_ref,
    wavelet_ref,
    edge_ref,
    own_ref,
    near_ref,
    codes_ref,
    field,
    start,
    tables,
    shift_ref,
):
    _, layers, width, lanes = codes_ref.shape
    parts, shots = start.shape[2:4]
    fields = parts * shots
    odd, place_of, inside = orientation(layers, depth_total)
    own_rows = own_ref.reshape(own_ref.shape[0] * width, lanes)
    edge_rows = edge_ref.reshape(edge_ref.shape[0] * width, lanes)
    near_rows = near_ref.reshape(near_ref.shape[0] * width, lanes)
    span = fields * width
    keep = edge_masks(shots, lanes)
    diagonal = lax.broadcasted_iota(jnp.int32, shift_ref.shape[1:], 0) == lax.broadcasted_iota(
        jnp.int32, shift_ref.shape[1:], 1
    )
    for part, value in enumerate(shift_of(wave_ref, damp_ref)):
        shift_ref[part] = jnp.where(diagonal, value, 0.0)

    extra = REACH * fields
    for k in range(2):
        pick = jnp.where(odd, k, 1 - k)
        fill_tables(
            tables, k, near_ref[extra + pick], near_ref[extra + 2 + pick], inside(k - 2), wave_ref, damp_ref
        )
    for q in range(layers):
        pick = jnp.where(odd, q, layers - 1 - q)
        fill_tables(
            tables, q + 2, codes_ref[0, pick], codes_ref[1, pick], jnp.float32(1.0), wave_ref, damp_ref
        )

    def bring_near(k, carry):
        bring(near_rows, jnp.where(odd, k, REACH - 1 - k) * span, field, k)
        return carry

    def bring_own(q, carry):
        bring(own_rows, jnp.where(odd, q, REACH - 1 - q) * span, field, q + REACH)
        return carry

    lax.fori_loop(0, REACH, bring_near, 0)
    lax.fori_loop(0, REACH, bring_own, 0)
    bring(edge_rows, 0, field, REACH + layers - 1)

    def start_plane(i, carry):
        stencil_plane(
            ((field, i), (field, i + 1), (field, i + 2)),
            (start, i),
            (tables, i, 0),
            inside(i - 2) * (-1.0 / 30.0),
            keep,
        )
        return carry

    lax.fori_loop(0, layers + 1, start_plane, 0)
    add_sources(start, -2, place_of, cells_ref, wavelet_ref)


def image_kernel(
    depth_total,
    start,
    tables,
    first,
    split_ref,
    products_ref,
    send_ref,
    second,
):
    _, width, _, shots, lanes = start.shape
    layers = start.shape[0] - 1
    _, _, inside = orientation(layers, depth_total)
    keep = edge_masks(shots, lanes)
    send_ref[0] = start[layers]

    def first_plane(j, carry):
        stencil_plane(
            ((start, j), (start, j + 1), (start, j + 2)),
            (first, j),
            (tables, j + 1, 1),
            inside(j - 1) * (1.0 / 30.0),
            keep,
        )
        return carry

    lax.fori_loop(0, layers - 1, first_plane, 0)
    products = jnp.zeros(products_ref.shape, jnp.float32)
    for k in range(layers - 3):
        stencil_plane(
            ((first, k), (first, k + 1), (first, k + 2)),
            (second, k),
            (tables, k + 2, 1),
            1.0 / 30.0,
            keep,
        )
        for level, source in enumerate(((start, k + 2), (first, k + 1), (second, k))):
            split_level(source, level, split_ref)
        products += products_of(split_ref)
    products_ref[...] = products


def pack_gram(products, shots, cells):
    fields = 2 * shots
    rows = BLOCKS * fields
    summed = products[0:rows] + products[rows : 2 * rows] + products[2 * rows : 3 * rows]
    summed = summed[:, 0:rows] + summed[:, rows : 2 * rows] + summed[:, 2 * rows : 3 * rows]
    summed = summed * (1.0 / cells)
    summed = jnp.concatenate([summed, jnp.zeros((rows, 128 - rows), jnp.float32)], axis=1)
    lane = lax.broadcasted_iota(jnp.int32, (shots, 128), 1)
    blocks = []
    for level in range(BLOCKS):
        real_rows = summed[level * fields : level * fields + shots]
        imag_rows = summed[level * fields + shots : (level + 1) * fields]
        both = jnp.where(
            lax.rem(lane, fields) < shots,
            real_rows + pltpu.roll(imag_rows, 128 - shots, 1),
            real_rows - pltpu.roll(imag_rows, shots, 1),
        )
        blocks.append(both[:, level * fields : rows])
    blocks.append(jnp.zeros((shots, 128 - len(PAIRS) * fields), jnp.float32))
    return jnp.concatenate(blocks, axis=1)


def stage_kernel(stage, depth_total, layers, names, places, *refs):
    refs = dict(zip(names, refs))
    first, second, far_ref = refs["first"], refs["second"], refs["far"]
    _, width, parts, shots, lanes = first.shape
    odd, place_of, inside = orientation(layers, depth_total)
    keep = edge_masks(shots, lanes)
    top = layers - 1 + stage

    def old(name):
        return (refs[name], places[name])

    if stage == 2:
        start = far_ref
        first_table = (refs["far_tables"], 0, 1)
    else:
        field, start = refs["field"], refs["start"]
        first_table = (refs["own_tables"], top + 1, 1)
        if stage == 0:
            start_table = (refs["own_tables"], top + 2, 0)
        else:
            fill_tables(
                refs["tables"],
                0,
                refs["nearest"][parts * shots],
                refs["nearest"][parts * shots + 1],
                inside(jnp.int32(top)),
                refs["wave"],
                refs["damp"],
            )
            start_table = (refs["tables"], 0, 0)
        bring(far_ref.reshape(far_ref.shape[0] * width, lanes), 0, field, 0)
        stencil_plane(
            (old("field_a"), old("field_b"), (field, 0)),
            (start, 0),
            start_table,
            inside(jnp.int32(top)) * (-1.0 / 30.0),
            keep,
        )
        add_sources(start, top, place_of, refs["cells"], refs["wavelet"])
    stencil_plane(
        (old("start_a"), old("start_b"), (start, 0)),
        (first, 0),
        first_table,
        inside(jnp.int32(top - 1)) * (1.0 / 30.0),
        keep,
    )
    stencil_plane(
        (old("first_a"), old("first_b"), (first, 0)),
        (second, 0),
        (refs["own_tables"], top, 1),
        1.0 / 30.0,
        keep,
    )
    split_ref = refs["split"]
    levels = (old("start_a"), old("first_b"), (second, 0))
    for level, source in enumerate(levels):
        if stage < 2 or level == 2:
            split_level(source, level, split_ref)
    if stage == 1:
        for level, source in enumerate((old("start_b"), (first, 0))):
            split_level(source, level, refs["next_split"])
    products = refs["products_in"][...] + products_of(split_ref)
    if stage < 2:
        refs["products"][...] = products
    else:
        packed = pack_gram(products, shots, float(depth_total * width * lanes))
        for copy in range(refs["grams"].shape[0]):
            refs["grams"][copy] = packed


def back_kernel(
    shift_ref, grams_ref, *rest
):
    basis_ref, hessenberg_ref = rest[-2:]
    layers, parts, shots, width, y = basis_ref.shape
    fields = parts * shots
    rows = BLOCKS * fields
    half = rows // 2
    tile = shots
    tiles = BLOCKS
    spread = BLOCKS * rows
    lanes = 128
    lead = spread - lanes

    grams = [grams_ref[i] for i in range(grams_ref.shape[0])]
    while len(grams) > 1:
        grams = [sum(grams[i : i + 2]) for i in range(0, len(grams), 2)]
    packed = grams[0]
    turned = packed.T
    lane = lax.broadcasted_iota(jnp.int32, (tile, lanes), 1)
    sub = lax.broadcasted_iota(jnp.int32, (tile, lanes), 0)
    wide_lane = lax.broadcasted_iota(jnp.int32, (tile, 2 * lanes), 1)
    wide_sub = lax.broadcasted_iota(jnp.int32, (tile, 2 * lanes), 0)
    column = lax.rem(wide_lane, rows) // fields * tile + lax.rem(wide_lane, tile)
    real, imag = [], []
    for t in range(tiles):
        match = (wide_lane < spread) & (column == wide_sub + t * tile)
        unit = jnp.where(match, 1.0, 0.0).astype(jnp.float32)
        blank = jnp.zeros((tile, lanes), jnp.float32)
        parts_of = []
        for part in range(2):
            blocks = [jnp.zeros((tile, lead), jnp.float32)]
            for j in range(tiles):
                if j >= t:
                    begin = (2 * PAIRS.index((t, j)) + part) * tile
                    blocks.append(packed[:, begin : begin + tile])
                else:
                    begin = (2 * PAIRS.index((j, t)) + part) * tile
                    block = turned[begin : begin + tile, 0:tile]
                    blocks.append(block if part == 0 else -block)
            blocks.append(jnp.zeros((tile, lanes - lead - half), jnp.float32))
            parts_of.append(jnp.concatenate(blocks, axis=1))
        real.append(unit + jnp.concatenate([blank, parts_of[0]], axis=1))
        imag.append(jnp.concatenate([blank, parts_of[1]], axis=1))
    pivots = []
    for owner in range(tiles):
        spots = [spread + owner * tile + r for r in range(tile)]
        shape = (tile, lanes)
        ahead = {
            (t, r): [
                jnp.broadcast_to(values[t][:, spots[r] : spots[r] + 1], shape) for values in (real, imag)
            ]
            for t in range(owner, tiles)
            for r in range(tile)
        }
        for r in range(tile):
            own_real, own_imag = ahead[owner, r]
            pivot = jnp.broadcast_to(own_real[r : r + 1], shape)
            pivots.append(pivot)
            inverse = pl.reciprocal(pivot, approx=True)
            inverse = inverse * (2.0 - pivot * inverse)
            scaled = {}
            for t in range(owner, tiles):
                column_real, column_imag = [value * inverse for value in ahead[t, r]]
                if t == owner:
                    column_real = jnp.where(sub > r, column_real, 0.0)
                    column_imag = jnp.where(sub > r, column_imag, 0.0)
                scaled[t] = column_real, column_imag
            for later in range(r + 1, tile):
                entry_real = jnp.broadcast_to(own_real[later : later + 1], shape)
                entry_imag = jnp.broadcast_to(own_imag[later : later + 1], shape)
                for t in range(owner, tiles):
                    column_real, column_imag = scaled[t]
                    old_real, old_imag = ahead[t, later]
                    ahead[t, later] = [
                        old_real - (column_real * entry_real + column_imag * entry_imag),
                        old_imag - (column_imag * entry_real - column_real * entry_imag),
                    ]
            row_real = real[owner][r : r + 1]
            row_imag = imag[owner][r : r + 1]
            for t in range(owner, tiles):
                column_real, column_imag = [
                    jnp.concatenate([value, value], axis=1) for value in scaled[t]
                ]
                new_real = real[t] - (column_real * row_real - column_imag * row_imag)
                new_imag = imag[t] - (column_real * row_imag + column_imag * row_real)
                real[t], imag[t] = new_real, new_imag
    for t in range(tiles):
        scales = pivots[t * tile]
        for r in range(1, tile):
            scales = jnp.where(sub == r, pivots[t * tile + r], scales)
        scales = lax.rsqrt(scales)
        scales = jnp.concatenate([scales, scales], axis=1)
        real[t] = real[t] * scales
        imag[t] = imag[t] * scales

    last_real, last_imag = real[tiles - 1], imag[tiles - 1]
    first_half = lax.rem(wide_lane, fields) < tile
    mix = jnp.concatenate(
        [
            jnp.where(first_half, last_real, last_imag),
            jnp.where(first_half, -last_imag, last_real),
        ],
        axis=0,
    )
    pieces = []
    for part in range(3):
        short = mix.astype(jnp.bfloat16)
        pieces.append(short)
        mix = mix - short.astype(jnp.float32)
    left = jnp.concatenate(pieces, axis=0)[:, 0:spread]

    odd = lax.rem(lax.axis_index("gz"), 2) == 1
    out_rows = basis_ref.reshape(layers * fields * width, y)
    spots = [
        (ref, spot)
        for ref in rest[:-2]
        for spot in range(ref.shape[1] // (width * y))
    ]
    group = 16
    for q in range(layers):
        source, spot = spots[q]
        plane = jnp.where(odd, q, layers - 1 - q)
        for begin in range(0, width, group):
            offset = (spot * width + begin) * y
            mixed = jnp.dot(
                left, source[:, offset : offset + group * y], preferred_element_type=jnp.float32
            )
            mixed = mixed[0:fields] + mixed[fields : 2 * fields] + mixed[2 * fields : 3 * fields]
            for column in range(group):
                out_rows[pl.ds(plane * (fields * width) + begin + column, fields, stride=width), :] = mixed[
                    :, column * y : (column + 1) * y
                ]

    wide = 2 * tile
    full_real = jnp.concatenate(real, axis=0)
    full_imag = jnp.concatenate(imag, axis=0)
    row_index = lax.broadcasted_iota(jnp.int32, (half, wide), 0)
    column_index = lax.broadcasted_iota(jnp.int32, (half, wide), 1)
    upper = row_index <= column_index + tile
    factor_real = jnp.where(upper, full_real[:, spread + tile : spread + half], 0.0)
    factor_imag = jnp.where(upper, full_imag[:, spread + tile : spread + half], 0.0)
    lower_real, lower_imag = [
        jnp.concatenate([value[0:wide, 0:tile], value[0:wide, fields : fields + tile]], axis=1)
        for value in (full_real, full_imag)
    ]

    def times(left, right):
        return lax.dot_general(
            left,
            right,
            (((1,), (1,)), ((), ())),
            precision=lax.Precision.HIGHEST,
            preferred_element_type=jnp.float32,
        )

    hessenberg_ref[0] = (
        times(lower_real, factor_real)
        + times(lower_imag, factor_imag)
        + shift_ref[0]
    )
    hessenberg_ref[1] = (
        times(lower_real, factor_imag)
        - times(lower_imag, factor_real)
        + shift_ref[1]
    )


def shards(initial_guess, velocity_class, layer_code, wavenumber, damping, shot_cells, wavelet):
    layers, parts, shots, width, lanes = initial_guess.shape
    devices = lax.axis_size("gz")
    assert layers == REACH + 1 and devices % 2 == 0
    fields = parts * shots
    rows = BLOCKS * fields
    span = width * lanes
    depth_total = devices * layers
    shot_cells = shot_cells.T

    smem = pl.BlockSpec(memory_space=pltpu.SMEM)
    vmem = pl.BlockSpec(memory_space=pltpu.VMEM)
    hbm = pl.BlockSpec(memory_space=pl.ANY)
    params = pltpu.CompilerParams(vmem_limit_bytes=VMEM_BYTES)


    def float_shape(*dims):
        return jax.ShapeDtypeStruct(dims, jnp.float32)

    odd_to_even = [(i, i + 1) for i in range(1, devices - 1, 2)]
    even_to_odd = [(i, i + 1) for i in range(0, devices, 2)]
    far_pairs = odd_to_even + [(b, a) for a, b in odd_to_even]
    near_pairs = even_to_odd + [(b, a) for a, b in even_to_odd]

    edge, following, near, codes = pl.pallas_call(
        pack_kernel,
        out_shape=(
            float_shape(fields + 2, width, lanes),
            float_shape(fields, width, lanes),
            float_shape(REACH * fields + 4, width, lanes),
            float_shape(2, layers, width, lanes),
        ),
        in_specs=[hbm, hbm, hbm],
        out_specs=(vmem, vmem, vmem, vmem),
        scratch_shapes=[
            pltpu.VMEM((2, layers, width, lanes), jnp.int32),
            pltpu.SemaphoreType.DMA((3 + REACH,)),
        ],
        compiler_params=params,
        name="pack",
    )(
        *(
            pltpu.with_memory_space_constraint(array, pltpu.HBM)
            for array in (initial_guess, velocity_class, layer_code)
        )
    )
    nearest = lax.ppermute(edge, "gz", far_pairs)
    second_far = lax.ppermute(following, "gz", far_pairs)
    own = near
    near = lax.ppermute(own, "gz", near_pairs)

    def planes(count):
        return float_shape(count, width, parts, shots, lanes)

    def tables(count):
        return float_shape(count, 4, width, lanes)

    def split(count):
        return jax.ShapeDtypeStruct((BLOCKS * rows, count * span), jnp.bfloat16)

    def scratch(shape):
        return pltpu.VMEM(shape.shape, shape.dtype)

    products = float_shape(BLOCKS * rows, BLOCKS * rows)
    cost = pl.CostEstimate(flops=10_000_000, bytes_accessed=16_000_000, transcendentals=0)
    common = (wavenumber, damping, shot_cells, wavelet)
    turned_shape = float_shape(2, 2 * shots, BLOCKS * shots)
    field, start, own_tables, shift = pl.pallas_call(
        functools.partial(early_kernel, depth_total),
        out_shape=(planes(layers + REACH), planes(layers + 1), tables(layers + 2), turned_shape),
        in_specs=[smem] * 4 + [vmem] * 4,
        out_specs=(vmem,) * 4,
        compiler_params=params,
        cost_estimate=cost,
        name="early",
    )(*common, edge, own, near, codes)
    first, early_split, early_products, send = pl.pallas_call(
        functools.partial(image_kernel, depth_total),
        out_shape=(planes(layers - 1), split(layers - 3), products, planes(1)),
        in_specs=[vmem] * 2,
        out_specs=(vmem,) * 4,
        scratch_shapes=[scratch(planes(layers - 3))],
        compiler_params=params,
        cost_estimate=cost,
        name="images",
    )(start, own_tables)
    third_far = lax.ppermute(send, "gz", far_pairs)
    shapes = {
        "field": planes(1),
        "start": planes(1),
        "first": planes(1),
        "second": planes(1),
        "tables": tables(1),
        "split": split(1),
        "next_split": split(1),
        "products": products,
        "grams": float_shape(devices, shots, 128),
    }

    def run_stage(stage, far, old, extra, outs, temporaries):
        inputs = {}
        if stage < 2:
            inputs = dict(zip(("wave", "damp", "cells", "wavelet"), common))
        scalars = len(inputs)
        inputs["far"] = far
        inputs.update({name: array for name, (array, _) in old.items()})
        inputs.update(extra)
        results = pl.pallas_call(
            functools.partial(
                stage_kernel,
                stage,
                depth_total,
                layers,
                list(inputs) + outs + temporaries,
                {name: place for name, (_, place) in old.items()},
            ),
            out_shape=tuple(shapes[name] for name in outs),
            in_specs=[smem] * scalars + [vmem] * (len(inputs) - scalars),
            out_specs=(vmem,) * len(outs),
            scratch_shapes=[scratch(shapes[name]) for name in temporaries],
            input_output_aliases={len(inputs) - 1: 0} if stage == 2 else {},
            compiler_params=params,
            cost_estimate=cost,
            name="stage_%d" % stage,
        )(*inputs.values())
        return dict(zip(outs, results))

    zero = run_stage(
        0,
        nearest,
        {
            "field_a": (field, layers + 1),
            "field_b": (field, layers + 2),
            "start_a": (start, layers - 1),
            "start_b": (start, layers),
            "first_a": (first, layers - 3),
            "first_b": (first, layers - 2),
        },
        {"own_tables": own_tables, "products_in": early_products},
        ["field", "start", "first", "split", "products"],
        ["second"],
    )
    one = run_stage(
        1,
        second_far,
        {
            "field_a": (field, layers + 2),
            "field_b": (zero["field"], 0),
            "start_a": (start, layers),
            "start_b": (zero["start"], 0),
            "first_a": (first, layers - 2),
            "first_b": (zero["first"], 0),
        },
        {"own_tables": own_tables, "products_in": zero["products"], "nearest": nearest},
        ["start", "first", "tables", "split", "products", "next_split"],
        ["field", "second"],
    )
    two = run_stage(
        2,
        third_far,
        {
            "start_a": (zero["start"], 0),
            "start_b": (one["start"], 0),
            "first_a": (zero["first"], 0),
            "first_b": (one["first"], 0),
        },
        {"own_tables": own_tables, "far_tables": one["tables"], "products_in": one["products"], "begun": one["next_split"]},
        ["split", "grams"],
        ["first", "second"],
    )
    grams = two["grams"]
    grams = lax.all_to_all(grams, "gz", 0, 0)
    basis_two, turned = pl.pallas_call(
        back_kernel,
        out_shape=(
            jax.ShapeDtypeStruct(initial_guess.shape, jnp.float32),
            turned_shape,
        ),
        in_specs=[vmem] * 6,
        out_specs=(vmem, vmem),
        compiler_params=params,
        name="back",
    )(shift, grams, early_split, zero["split"], one["split"], two["split"])
    return basis_two, jnp.swapaxes(turned, 1, 2)


def solution(mesh):
    return jax.shard_map(
        shards,
        mesh=mesh,
        in_specs=(
            P(("freq", "gz"), None, None, None, None),
            P("gz", None, None),
            P("gz", None, None),
            P("freq"),
            P(),
            P(),
            P("freq", None),
        ),
        out_specs=(P(("freq", "gz"), None, None, None, None), P("freq", None, None)),
        check_vma=False,
    )
```

```python
import functools

import jax
import jax.numpy as jnp
from jax import lax
from jax.experimental import pallas as pl
from jax.experimental.pallas import tpu as pltpu
from jax.sharding import PartitionSpec as P

SHIFT_BASE = 2.9
BLOCKS = 3
REACH = 3
VMEM_BYTES = 24 * 1024 * 1024
PAIRS = ((0, 0), (0, 1), (0, 2), (1, 1), (1, 2), (2, 2))


def shift_of(wave_ref, damp_ref):
    classes, levels = wave_ref.shape[0], damp_ref.shape[0]
    wave_mean = sum(wave_ref[i] for i in range(classes)) * (1.0 / classes)
    damp_mean = sum(damp_ref[i] for i in range(levels)) * (1.0 / levels)
    return SHIFT_BASE - wave_mean, -wave_mean * damp_mean


def edge_masks(shots, lanes):
    lane = lax.broadcasted_iota(jnp.int32, (shots, lanes), 1)
    return (
        jnp.where(lane == 0, 0.0, 1.0).astype(jnp.float32),
        jnp.where(lane == lanes - 1, 0.0, 1.0).astype(jnp.float32),
    )


def stencil_plane(sources, target, table, scale, keep):
    (low, low_plane), (mid, mid_plane), high = sources
    out, out_plane = target
    table_ref, table_plane, kind = table
    width = table_ref.shape[2]
    left, right = keep

    def load(column):
        center, away = [], []
        for part in range(2):
            v = mid[mid_plane, column, part]
            d = low[low_plane, column, part]
            if high is not None:
                d = d + high[0][high[1], column, part]
            center.append(v)
            away.append(d + 3.0 * v)
        return center, away

    here_v, here_u = load(0)
    before_v = [jnp.zeros_like(v) for v in here_v]
    before_u = before_v
    for column in range(width):
        if column + 1 < width:
            after_v, after_u = load(column + 1)
        else:
            after_v = [jnp.zeros_like(v) for v in here_v]
            after_u = after_v
        real_row, imag_row = [
            jnp.broadcast_to(table_ref[table_plane, 2 * kind + part, column : column + 1, :], here_v[0].shape)
            for part in range(2)
        ]
        for part in range(2):
            near = here_u[part] + (before_v[part] + after_v[part])
            wide = (before_u[part] + after_u[part]) + (3.0 * here_u[part] + 5.0 * here_v[part])
            sides = pltpu.roll(wide, 1, 1) * left + pltpu.roll(wide, 127, 1) * right
            total = 3.0 * wide + 5.0 * near + sides
            if part == 0:
                own = real_row * here_v[0] + imag_row * here_v[1]
            else:
                own = real_row * here_v[1] - imag_row * here_v[0]
            out[out_plane, column, part] = own - scale * total
        before_v, before_u, here_v, here_u = here_v, here_u, after_v, after_u


def couple_plane(source, target, scale, keep):
    ref, plane = source
    out, out_plane = target
    width = ref.shape[1]
    left, right = keep
    blank = jnp.zeros(ref.shape[3:], jnp.float32)
    for part in range(2):
        before, here = blank, ref[plane, 0, part]
        for column in range(width):
            after = ref[plane, column + 1, part] if column + 1 < width else blank
            wide = (before + after) + 3.0 * here
            sides = pltpu.roll(wide, 1, 1) * left + pltpu.roll(wide, 127, 1) * right
            out[out_plane, column, part] = scale * (3.0 * wide + 5.0 * here + sides)
            before, here = here, after


def bring(rows, first_row, field, plane):
    width, parts, shots = field.shape[1:4]
    for column in range(width):
        for part in range(parts):
            field[plane, column, part] = rows[
                pl.ds(first_row + part * shots * width + column, shots, stride=width), :
            ]


def fill_tables(tables, plane, labels, codes, inside_flag, wave_ref, damp_ref):
    shift_real, shift_imag = shift_of(wave_ref, damp_ref)
    wave = jnp.zeros(labels.shape, jnp.float32)
    for i in range(wave_ref.shape[0]):
        wave = jnp.where(labels == float(i), wave_ref[i], wave)
    loss = jnp.zeros(labels.shape, jnp.float32)
    for i in range(damp_ref.shape[0]):
        loss = jnp.where(codes == float(i), damp_ref[i], loss)
    real = 185.0 / 30.0 - wave
    imag = wave * loss
    tables[plane, 0] = -inside_flag * real
    tables[plane, 1] = -inside_flag * imag
    tables[plane, 2] = inside_flag * (real - shift_real)
    tables[plane, 3] = inside_flag * (imag + shift_imag)


def add_sources(start, first_start, place_of, cells_ref, wavelet_ref):
    count, _, _, shots, lanes = start.shape
    lane_row = lax.broadcasted_iota(jnp.int32, (1, lanes), 1)
    for s in range(shots):
        place = place_of(cells_ref[0, s]) - first_start

        @pl.when((place >= 0) & (place < count))
        def _():
            column = cells_ref[1, s]
            hit = lane_row == cells_ref[2, s]
            for part in range(2):
                start[place, column, part, s : s + 1, :] += jnp.where(hit, wavelet_ref[part, s], 0.0)


def split_level(source, level, split_ref, more=None):
    ref, plane = source
    width, parts, shots, lanes = ref.shape[1:]
    fields = parts * shots
    for column in range(width):
        value = ref[plane, column]
        if more is not None:
            value = value + more[0][more[1], column]
        value = value.reshape(fields, lanes)
        for part in range(3):
            short = value.astype(jnp.bfloat16)
            row = (part * BLOCKS + level) * fields
            split_ref[row : row + fields, column * lanes : (column + 1) * lanes] = short
            if part < 2:
                value = value - short.astype(jnp.float32)


def products_of(split_ref):
    chunk = split_ref[...]
    return lax.dot_general(
        chunk, chunk, (((1,), (1,)), ((), ())), preferred_element_type=jnp.float32
    )


def pack_kernel(guess_ref, class_ref, layer_ref, edge_ref, next_ref, near_ref, codes_ref, held, sems):
    layers, parts, shots, width, lanes = guess_ref.shape
    fields = parts * shots
    odd = lax.rem(lax.axis_index("gz"), 2) == 1
    planes = guess_ref.reshape(layers * fields, width, lanes)
    edge = jnp.where(odd, layers - 1, 0) * fields
    begin = jnp.where(odd, 0, layers - REACH) * fields
    code = jnp.where(odd, 0, layers - 2)
    edge_code = jnp.where(odd, layers - 1, 0)
    moves = [(class_ref, held.at[0]), (layer_ref, held.at[1])]
    moves.append((planes.at[pl.ds(edge, fields)], edge_ref.at[pl.ds(0, fields)]))
    for k in range(REACH):
        moves.append(
            (planes.at[pl.ds(begin + k * fields, fields)], near_ref.at[pl.ds(k * fields, fields)])
        )
    copies = []
    for number, (source, target) in enumerate(moves):
        copies.append(pltpu.make_async_copy(source, target, sems.at[number]))
        copies[-1].start()
    copies[0].wait()
    copies[1].wait()
    for kind in range(2):
        for q in range(layers):
            codes_ref[kind, q] = held[kind, q].astype(jnp.float32)
        for k in range(2):
            near_ref[REACH * fields + 2 * kind + k] = held[kind, code + k].astype(jnp.float32)
        edge_ref[fields + kind] = held[kind, edge_code].astype(jnp.float32)
    for copy in copies[2:]:
        copy.wait()
    following = jnp.where(odd, REACH - 1, 0) * fields
    next_ref[...] = near_ref[pl.ds(following, fields)]


def orientation(layers, depth_total):
    index = lax.axis_index("gz")
    odd = lax.rem(index, 2) == 1
    first_plane = index * layers

    def place_of(plane):
        local = plane - first_plane
        return jnp.where(odd, local, layers - 1 - local)

    def inside(place):
        plane = first_plane + jnp.where(odd, place, layers - 1 - place)
        return jnp.where((plane >= 0) & (plane < depth_total), 1.0, 0.0).astype(jnp.float32)

    return odd, place_of, inside


def early_kernel(
    depth_total,
    wave_ref,
    damp_ref,
    cells_ref,
    wavelet_ref,
    edge_ref,
    own_ref,
    near_ref,
    codes_ref,
    field,
    start,
    tables,
    shift_ref,
):
    _, layers, width, lanes = codes_ref.shape
    parts, shots = start.shape[2:4]
    fields = parts * shots
    odd, place_of, inside = orientation(layers, depth_total)
    own_rows = own_ref.reshape(own_ref.shape[0] * width, lanes)
    edge_rows = edge_ref.reshape(edge_ref.shape[0] * width, lanes)
    near_rows = near_ref.reshape(near_ref.shape[0] * width, lanes)
    span = fields * width
    keep = edge_masks(shots, lanes)
    diagonal = lax.broadcasted_iota(jnp.int32, shift_ref.shape[1:], 0) == lax.broadcasted_iota(
        jnp.int32, shift_ref.shape[1:], 1
    )
    for part, value in enumerate(shift_of(wave_ref, damp_ref)):
        shift_ref[part] = jnp.where(diagonal, value, 0.0)

    extra = REACH * fields
    for k in range(2):
        pick = jnp.where(odd, k, 1 - k)
        fill_tables(
            tables, k, near_ref[extra + pick], near_ref[extra + 2 + pick], inside(k - 2), wave_ref, damp_ref
        )
    for q in range(layers):
        pick = jnp.where(odd, q, layers - 1 - q)
        fill_tables(
            tables, q + 2, codes_ref[0, pick], codes_ref[1, pick], jnp.float32(1.0), wave_ref, damp_ref
        )

    def bring_near(k, carry):
        bring(near_rows, jnp.where(odd, k, REACH - 1 - k) * span, field, k)
        return carry

    def bring_own(q, carry):
        bring(own_rows, jnp.where(odd, q, REACH - 1 - q) * span, field, q + REACH)
        return carry

    lax.fori_loop(0, REACH, bring_near, 0)
    lax.fori_loop(0, REACH, bring_own, 0)
    bring(edge_rows, 0, field, REACH + layers - 1)

    def start_plane(i, carry):
        stencil_plane(
            ((field, i), (field, i + 1), (field, i + 2)),
            (start, i),
            (tables, i, 0),
            inside(i - 2) * (-1.0 / 30.0),
            keep,
        )
        return carry

    lax.fori_loop(0, layers + 1, start_plane, 0)
    add_sources(start, -2, place_of, cells_ref, wavelet_ref)


def image_kernel(
    depth_total,
    start,
    tables,
    first,
    split_ref,
    products_ref,
    send_ref,
    second,
    coupled,
):
    _, width, _, shots, lanes = start.shape
    layers = start.shape[0] - 1
    _, _, inside = orientation(layers, depth_total)
    keep = edge_masks(shots, lanes)
    couple_plane((start, layers), (coupled, 0), -1.0 / 30.0, keep)
    couple_plane((coupled, 0), (send_ref, 0), -1.0 / 30.0, keep)

    def first_plane(j, carry):
        stencil_plane(
            ((start, j), (start, j + 1), (start, j + 2)),
            (first, j),
            (tables, j + 1, 1),
            inside(j - 1) * (1.0 / 30.0),
            keep,
        )
        return carry

    lax.fori_loop(0, layers - 1, first_plane, 0)
    products = jnp.zeros(products_ref.shape, jnp.float32)
    for k in range(layers - 3):
        stencil_plane(
            ((first, k), (first, k + 1), (first, k + 2)),
            (second, k),
            (tables, k + 2, 1),
            1.0 / 30.0,
            keep,
        )
        for level, source in enumerate(((start, k + 2), (first, k + 1), (second, k))):
            split_level(source, level, split_ref)
        products += products_of(split_ref)
    products_ref[...] = products


def pack_gram(products, shots, cells):
    fields = 2 * shots
    rows = BLOCKS * fields
    summed = products[0:rows] + products[rows : 2 * rows] + products[2 * rows : 3 * rows]
    summed = summed[:, 0:rows] + summed[:, rows : 2 * rows] + summed[:, 2 * rows : 3 * rows]
    summed = summed * (1.0 / cells)
    summed = jnp.concatenate([summed, jnp.zeros((rows, 128 - rows), jnp.float32)], axis=1)
    lane = lax.broadcasted_iota(jnp.int32, (shots, 128), 1)
    blocks = []
    for level in range(BLOCKS):
        real_rows = summed[level * fields : level * fields + shots]
        imag_rows = summed[level * fields + shots : (level + 1) * fields]
        both = jnp.where(
            lax.rem(lane, fields) < shots,
            real_rows + pltpu.roll(imag_rows, 128 - shots, 1),
            real_rows - pltpu.roll(imag_rows, shots, 1),
        )
        blocks.append(both[:, level * fields : rows])
    blocks.append(jnp.zeros((shots, 128 - len(PAIRS) * fields), jnp.float32))
    return jnp.concatenate(blocks, axis=1)


def stage_kernel(stage, depth_total, layers, names, places, *refs):
    refs = dict(zip(names, refs))
    first, second, far_ref = refs["first"], refs["second"], refs["far"]
    field, start = refs["field"], refs["start"]
    own_tables = refs["own_tables"]
    _, width, parts, shots, lanes = first.shape
    odd, place_of, inside = orientation(layers, depth_total)
    keep = edge_masks(shots, lanes)
    top = layers - 1 + stage

    def old(name):
        return (refs[name], places[name])

    if stage == 0:
        start_table = (own_tables, top + 2, 0)
    else:
        fill_tables(
            refs["tables"],
            0,
            refs["nearest"][parts * shots],
            refs["nearest"][parts * shots + 1],
            inside(jnp.int32(top)),
            refs["wave"],
            refs["damp"],
        )
        start_table = (refs["tables"], 0, 0)
    bring(far_ref.reshape(far_ref.shape[0] * width, lanes), 0, field, 0)
    stencil_plane(
        (old("field_a"), old("field_b"), (field, 0)),
        (start, 0),
        start_table,
        inside(jnp.int32(top)) * (-1.0 / 30.0),
        keep,
    )
    add_sources(start, top, place_of, refs["cells"], refs["wavelet"])
    stencil_plane(
        (old("start_a"), old("start_b"), (start, 0)),
        (first, 0),
        (own_tables, top + 1, 1),
        1.0 / 30.0,
        keep,
    )
    stencil_plane(
        (old("first_a"), old("first_b"), (first, 0)),
        (second, 0),
        (own_tables, top, 1),
        1.0 / 30.0,
        keep,
    )
    if stage == 1:
        outer, base = refs["outer"], refs["base"]
        stencil_plane(
            (old("start_b"), (start, 0), None),
            (outer, 0),
            (refs["tables"], 0, 1),
            inside(jnp.int32(top)) * (1.0 / 30.0),
            keep,
        )
        stencil_plane(
            (old("first_b"), (first, 0), (outer, 0)),
            (base, 0),
            (own_tables, top + 1, 1),
            1.0 / 30.0,
            keep,
        )
    split_ref = refs["split"]
    for level, source in enumerate((old("start_a"), old("first_b"), (second, 0))):
        split_level(source, level, split_ref)
    if stage == 1:
        for level, source in enumerate((old("start_b"), (first, 0))):
            split_level(source, level, refs["next_split"])
    refs["products"][...] = refs["products_in"][...] + products_of(split_ref)


def last_kernel(cells, far_ref, base_ref, products_ref, begun_ref, split_ref, grams_ref):
    split_level((base_ref, 0), 2, split_ref, (far_ref, 0))
    packed = pack_gram(products_ref[...] + products_of(split_ref), far_ref.shape[3], cells)
    for copy in range(grams_ref.shape[0]):
        grams_ref[copy] = packed


def back_kernel(
    shift_ref, grams_ref, *rest
):
    basis_ref, hessenberg_ref = rest[-2:]
    layers, parts, shots, width, y = basis_ref.shape
    fields = parts * shots
    rows = BLOCKS * fields
    half = rows // 2
    tile = shots
    tiles = BLOCKS
    spread = BLOCKS * rows
    lanes = 128
    lead = spread - lanes

    grams = [grams_ref[i] for i in range(grams_ref.shape[0])]
    while len(grams) > 1:
        grams = [sum(grams[i : i + 2]) for i in range(0, len(grams), 2)]
    packed = grams[0]
    turned = packed.T
    lane = lax.broadcasted_iota(jnp.int32, (tile, lanes), 1)
    sub = lax.broadcasted_iota(jnp.int32, (tile, lanes), 0)
    wide_lane = lax.broadcasted_iota(jnp.int32, (tile, 2 * lanes), 1)
    wide_sub = lax.broadcasted_iota(jnp.int32, (tile, 2 * lanes), 0)
    column = lax.rem(wide_lane, rows) // fields * tile + lax.rem(wide_lane, tile)
    real, imag = [], []
    for t in range(tiles):
        match = (wide_lane < spread) & (column == wide_sub + t * tile)
        unit = jnp.where(match, 1.0, 0.0).astype(jnp.float32)
        blank = jnp.zeros((tile, lanes), jnp.float32)
        parts_of = []
        for part in range(2):
            blocks = [jnp.zeros((tile, lead), jnp.float32)]
            for j in range(tiles):
                if j >= t:
                    begin = (2 * PAIRS.index((t, j)) + part) * tile
                    blocks.append(packed[:, begin : begin + tile])
                else:
                    begin = (2 * PAIRS.index((j, t)) + part) * tile
                    block = turned[begin : begin + tile, 0:tile]
                    blocks.append(block if part == 0 else -block)
            blocks.append(jnp.zeros((tile, lanes - lead - half), jnp.float32))
            parts_of.append(jnp.concatenate(blocks, axis=1))
        real.append(unit + jnp.concatenate([blank, parts_of[0]], axis=1))
        imag.append(jnp.concatenate([blank, parts_of[1]], axis=1))
    pivots = []
    for owner in range(tiles):
        spots = [spread + owner * tile + r for r in range(tile)]
        shape = (tile, lanes)
        ahead = {
            (t, r): [
                jnp.broadcast_to(values[t][:, spots[r] : spots[r] + 1], shape) for values in (real, imag)
            ]
            for t in range(owner, tiles)
            for r in range(tile)
        }
        for r in range(tile):
            own_real, own_imag = ahead[owner, r]
            pivot = jnp.broadcast_to(own_real[r : r + 1], shape)
            pivots.append(pivot)
            inverse = pl.reciprocal(pivot, approx=True)
            inverse = inverse * (2.0 - pivot * inverse)
            scaled = {}
            for t in range(owner, tiles):
                column_real, column_imag = [value * inverse for value in ahead[t, r]]
                if t == owner:
                    column_real = jnp.where(sub > r, column_real, 0.0)
                    column_imag = jnp.where(sub > r, column_imag, 0.0)
                scaled[t] = column_real, column_imag
            for later in range(r + 1, tile):
                entry_real = jnp.broadcast_to(own_real[later : later + 1], shape)
                entry_imag = jnp.broadcast_to(own_imag[later : later + 1], shape)
                for t in range(owner, tiles):
                    column_real, column_imag = scaled[t]
                    old_real, old_imag = ahead[t, later]
                    ahead[t, later] = [
                        old_real - (column_real * entry_real + column_imag * entry_imag),
                        old_imag - (column_imag * entry_real - column_real * entry_imag),
                    ]
            row_real = real[owner][r : r + 1]
            row_imag = imag[owner][r : r + 1]
            for t in range(owner, tiles):
                column_real, column_imag = [
                    jnp.concatenate([value, value], axis=1) for value in scaled[t]
                ]
                new_real = real[t] - (column_real * row_real - column_imag * row_imag)
                new_imag = imag[t] - (column_real * row_imag + column_imag * row_real)
                real[t], imag[t] = new_real, new_imag
    for t in range(tiles):
        scales = pivots[t * tile]
        for r in range(1, tile):
            scales = jnp.where(sub == r, pivots[t * tile + r], scales)
        scales = lax.rsqrt(scales)
        scales = jnp.concatenate([scales, scales], axis=1)
        real[t] = real[t] * scales
        imag[t] = imag[t] * scales

    last_real, last_imag = real[tiles - 1], imag[tiles - 1]
    first_half = lax.rem(wide_lane, fields) < tile
    mix = jnp.concatenate(
        [
            jnp.where(first_half, last_real, last_imag),
            jnp.where(first_half, -last_imag, last_real),
        ],
        axis=0,
    )
    pieces = []
    for part in range(3):
        short = mix.astype(jnp.bfloat16)
        pieces.append(short)
        mix = mix - short.astype(jnp.float32)
    left = jnp.concatenate(pieces, axis=0)[:, 0:spread]

    odd = lax.rem(lax.axis_index("gz"), 2) == 1
    out_rows = basis_ref.reshape(layers * fields * width, y)
    spots = [
        (ref, spot)
        for ref in rest[:-2]
        for spot in range(ref.shape[1] // (width * y))
    ]
    group = 16
    for q in range(layers):
        source, spot = spots[q]
        plane = jnp.where(odd, q, layers - 1 - q)
        for begin in range(0, width, group):
            offset = (spot * width + begin) * y
            mixed = jnp.dot(
                left, source[:, offset : offset + group * y], preferred_element_type=jnp.float32
            )
            mixed = mixed[0:fields] + mixed[fields : 2 * fields] + mixed[2 * fields : 3 * fields]
            for column in range(group):
                out_rows[pl.ds(plane * (fields * width) + begin + column, fields, stride=width), :] = mixed[
                    :, column * y : (column + 1) * y
                ]

    wide = 2 * tile
    full_real = jnp.concatenate(real, axis=0)
    full_imag = jnp.concatenate(imag, axis=0)
    row_index = lax.broadcasted_iota(jnp.int32, (half, wide), 0)
    column_index = lax.broadcasted_iota(jnp.int32, (half, wide), 1)
    upper = row_index <= column_index + tile
    factor_real = jnp.where(upper, full_real[:, spread + tile : spread + half], 0.0)
    factor_imag = jnp.where(upper, full_imag[:, spread + tile : spread + half], 0.0)
    lower_real, lower_imag = [
        jnp.concatenate([value[0:wide, 0:tile], value[0:wide, fields : fields + tile]], axis=1)
        for value in (full_real, full_imag)
    ]

    def times(left, right):
        return lax.dot_general(
            left,
            right,
            (((1,), (1,)), ((), ())),
            precision=lax.Precision.HIGHEST,
            preferred_element_type=jnp.float32,
        )

    hessenberg_ref[0] = (
        times(lower_real, factor_real)
        + times(lower_imag, factor_imag)
        + shift_ref[0]
    )
    hessenberg_ref[1] = (
        times(lower_real, factor_imag)
        - times(lower_imag, factor_real)
        + shift_ref[1]
    )


def shards(initial_guess, velocity_class, layer_code, wavenumber, damping, shot_cells, wavelet):
    layers, parts, shots, width, lanes = initial_guess.shape
    devices = lax.axis_size("gz")
    assert layers == REACH + 1 and devices % 2 == 0
    fields = parts * shots
    rows = BLOCKS * fields
    span = width * lanes
    depth_total = devices * layers
    shot_cells = shot_cells.T

    smem = pl.BlockSpec(memory_space=pltpu.SMEM)
    vmem = pl.BlockSpec(memory_space=pltpu.VMEM)
    hbm = pl.BlockSpec(memory_space=pl.ANY)
    params = pltpu.CompilerParams(vmem_limit_bytes=VMEM_BYTES)


    def float_shape(*dims):
        return jax.ShapeDtypeStruct(dims, jnp.float32)

    odd_to_even = [(i, i + 1) for i in range(1, devices - 1, 2)]
    even_to_odd = [(i, i + 1) for i in range(0, devices, 2)]
    far_pairs = odd_to_even + [(b, a) for a, b in odd_to_even]
    near_pairs = even_to_odd + [(b, a) for a, b in even_to_odd]

    edge, following, near, codes = pl.pallas_call(
        pack_kernel,
        out_shape=(
            float_shape(fields + 2, width, lanes),
            float_shape(fields, width, lanes),
            float_shape(REACH * fields + 4, width, lanes),
            float_shape(2, layers, width, lanes),
        ),
        in_specs=[hbm, hbm, hbm],
        out_specs=(vmem, vmem, vmem, vmem),
        scratch_shapes=[
            pltpu.VMEM((2, layers, width, lanes), jnp.int32),
            pltpu.SemaphoreType.DMA((3 + REACH,)),
        ],
        compiler_params=params,
        name="pack",
    )(
        *(
            pltpu.with_memory_space_constraint(array, pltpu.HBM)
            for array in (initial_guess, velocity_class, layer_code)
        )
    )
    nearest = lax.ppermute(edge, "gz", far_pairs)
    second_far = lax.ppermute(following, "gz", far_pairs)
    own = near
    near = lax.ppermute(own, "gz", near_pairs)

    def planes(count):
        return float_shape(count, width, parts, shots, lanes)

    def tables(count):
        return float_shape(count, 4, width, lanes)

    def split(count):
        return jax.ShapeDtypeStruct((BLOCKS * rows, count * span), jnp.bfloat16)

    def scratch(shape):
        return pltpu.VMEM(shape.shape, shape.dtype)

    products = float_shape(BLOCKS * rows, BLOCKS * rows)
    cost = pl.CostEstimate(flops=10_000_000, bytes_accessed=16_000_000, transcendentals=0)
    common = (wavenumber, damping, shot_cells, wavelet)
    turned_shape = float_shape(2, 2 * shots, BLOCKS * shots)
    field, start, own_tables, shift = pl.pallas_call(
        functools.partial(early_kernel, depth_total),
        out_shape=(planes(layers + REACH), planes(layers + 1), tables(layers + 2), turned_shape),
        in_specs=[smem] * 4 + [vmem] * 4,
        out_specs=(vmem,) * 4,
        compiler_params=params,
        cost_estimate=cost,
        name="early",
    )(*common, edge, own, near, codes)
    first, early_split, early_products, send = pl.pallas_call(
        functools.partial(image_kernel, depth_total),
        out_shape=(planes(layers - 1), split(layers - 3), products, planes(1)),
        in_specs=[vmem] * 2,
        out_specs=(vmem,) * 4,
        scratch_shapes=[scratch(planes(layers - 3)), scratch(planes(1))],
        compiler_params=params,
        cost_estimate=cost,
        name="images",
    )(start, own_tables)
    third_far = lax.ppermute(send, "gz", far_pairs)
    shapes = {
        "field": planes(1),
        "start": planes(1),
        "first": planes(1),
        "second": planes(1),
        "tables": tables(1),
        "split": split(1),
        "next_split": split(1),
        "outer": planes(1),
        "base": planes(1),
        "products": products,
    }

    def run_stage(stage, far, old, extra, outs, temporaries):
        inputs = dict(zip(("wave", "damp", "cells", "wavelet"), common))
        scalars = len(inputs)
        inputs["far"] = far
        inputs.update({name: array for name, (array, _) in old.items()})
        inputs.update(extra)
        results = pl.pallas_call(
            functools.partial(
                stage_kernel,
                stage,
                depth_total,
                layers,
                list(inputs) + outs + temporaries,
                {name: place for name, (_, place) in old.items()},
            ),
            out_shape=tuple(shapes[name] for name in outs),
            in_specs=[smem] * scalars + [vmem] * (len(inputs) - scalars),
            out_specs=(vmem,) * len(outs),
            scratch_shapes=[scratch(shapes[name]) for name in temporaries],
            compiler_params=params,
            cost_estimate=cost,
            name="stage_%d" % stage,
        )(*inputs.values())
        return dict(zip(outs, results))

    zero = run_stage(
        0,
        nearest,
        {
            "field_a": (field, layers + 1),
            "field_b": (field, layers + 2),
            "start_a": (start, layers - 1),
            "start_b": (start, layers),
            "first_a": (first, layers - 3),
            "first_b": (first, layers - 2),
        },
        {"own_tables": own_tables, "products_in": early_products},
        ["field", "start", "first", "split", "products"],
        ["second"],
    )
    one = run_stage(
        1,
        second_far,
        {
            "field_a": (field, layers + 2),
            "field_b": (zero["field"], 0),
            "start_a": (start, layers),
            "start_b": (zero["start"], 0),
            "first_a": (first, layers - 2),
            "first_b": (zero["first"], 0),
        },
        {"own_tables": own_tables, "products_in": zero["products"], "nearest": nearest},
        ["base", "split", "products", "next_split"],
        ["field", "start", "first", "second", "tables", "outer"],
    )
    last_split, grams = pl.pallas_call(
        functools.partial(last_kernel, float(depth_total * span)),
        out_shape=(split(1), float_shape(devices, shots, 128)),
        in_specs=[vmem] * 4,
        out_specs=(vmem, vmem),
        input_output_aliases={3: 0},
        compiler_params=params,
        name="last",
    )(third_far, one["base"], one["products"], one["next_split"])
    grams = lax.all_to_all(grams, "gz", 0, 0)
    basis_two, turned = pl.pallas_call(
        back_kernel,
        out_shape=(
            jax.ShapeDtypeStruct(initial_guess.shape, jnp.float32),
            turned_shape,
        ),
        in_specs=[vmem] * 6,
        out_specs=(vmem, vmem),
        compiler_params=params,
        name="back",
    )(shift, grams, early_split, zero["split"], one["split"], last_split)
    return basis_two, jnp.swapaxes(turned, 1, 2)


def solution(mesh):
    return jax.shard_map(
        shards,
        mesh=mesh,
        in_specs=(
            P(("freq", "gz"), None, None, None, None),
            P("gz", None, None),
            P("gz", None, None),
            P("freq"),
            P(),
            P(),
            P("freq", None),
        ),
        out_specs=(P(("freq", "gz"), None, None, None, None), P("freq", None, None)),
        check_vma=False,
    )
```

```python
import functools

import jax
import jax.numpy as jnp
from jax import lax
from jax.experimental import pallas as pl
from jax.experimental.pallas import tpu as pltpu
from jax.sharding import PartitionSpec as P

SHIFT_BASE = 1.5
BLOCKS = 3
REACH = 3
VMEM_BYTES = 24 * 1024 * 1024
PAIRS = ((0, 0), (0, 1), (0, 2), (1, 1), (1, 2), (2, 2))


def shift_of(wave_ref, damp_ref):
    classes, levels = wave_ref.shape[0], damp_ref.shape[0]
    wave_mean = sum(wave_ref[i] for i in range(classes)) * (1.0 / classes)
    damp_mean = sum(damp_ref[i] for i in range(levels)) * (1.0 / levels)
    return SHIFT_BASE - wave_mean, -wave_mean * damp_mean


def edge_masks(shots, lanes):
    lane = lax.broadcasted_iota(jnp.int32, (shots, lanes), 1)
    return (
        jnp.where(lane == 0, 0.0, 1.0).astype(jnp.float32),
        jnp.where(lane == lanes - 1, 0.0, 1.0).astype(jnp.float32),
    )


def stencil_plane(sources, target, table, scale, keep):
    (low, low_plane), (mid, mid_plane), high = sources
    out, out_plane = target
    table_ref, table_plane, kind = table
    width = table_ref.shape[2]
    left, right = keep

    def load(column):
        center, away = [], []
        for part in range(2):
            v = mid[mid_plane, column, part]
            d = low[low_plane, column, part]
            if high is not None:
                d = d + high[0][high[1], column, part]
            center.append(v)
            away.append(d + 3.0 * v)
        return center, away

    here_v, here_u = load(0)
    before_v = [jnp.zeros_like(v) for v in here_v]
    before_u = before_v
    for column in range(width):
        if column + 1 < width:
            after_v, after_u = load(column + 1)
        else:
            after_v = [jnp.zeros_like(v) for v in here_v]
            after_u = after_v
        real_row, imag_row = [
            jnp.broadcast_to(table_ref[table_plane, 2 * kind + part, column : column + 1, :], here_v[0].shape)
            for part in range(2)
        ]
        for part in range(2):
            near = here_u[part] + (before_v[part] + after_v[part])
            wide = (before_u[part] + after_u[part]) + (3.0 * here_u[part] + 5.0 * here_v[part])
            sides = pltpu.roll(wide, 1, 1) * left + pltpu.roll(wide, 127, 1) * right
            total = 3.0 * wide + 5.0 * near + sides
            if part == 0:
                own = real_row * here_v[0] + imag_row * here_v[1]
            else:
                own = real_row * here_v[1] - imag_row * here_v[0]
            out[out_plane, column, part] = own - scale * total
        before_v, before_u, here_v, here_u = here_v, here_u, after_v, after_u


def couple_plane(source, target, scale, keep):
    ref, plane = source
    out, out_plane = target
    width = ref.shape[1]
    left, right = keep
    blank = jnp.zeros(ref.shape[3:], jnp.float32)
    for part in range(2):
        before, here = blank, ref[plane, 0, part]
        for column in range(width):
            after = ref[plane, column + 1, part] if column + 1 < width else blank
            wide = (before + after) + 3.0 * here
            sides = pltpu.roll(wide, 1, 1) * left + pltpu.roll(wide, 127, 1) * right
            out[out_plane, column, part] = scale * (3.0 * wide + 5.0 * here + sides)
            before, here = here, after


def bring(rows, first_row, field, plane):
    width, parts, shots = field.shape[1:4]
    for column in range(width):
        for part in range(parts):
            field[plane, column, part] = rows[
                pl.ds(first_row + part * shots * width + column, shots, stride=width), :
            ]


def fill_tables(tables, plane, labels, codes, inside_flag, wave_ref, damp_ref):
    shift_real, shift_imag = shift_of(wave_ref, damp_ref)
    wave = jnp.zeros(labels.shape, jnp.float32)
    for i in range(wave_ref.shape[0]):
        wave = jnp.where(labels == float(i), wave_ref[i], wave)
    loss = jnp.zeros(labels.shape, jnp.float32)
    for i in range(damp_ref.shape[0]):
        loss = jnp.where(codes == float(i), damp_ref[i], loss)
    real = 185.0 / 30.0 - wave
    imag = wave * loss
    tables[plane, 0] = -inside_flag * real
    tables[plane, 1] = -inside_flag * imag
    tables[plane, 2] = inside_flag * (real - shift_real)
    tables[plane, 3] = inside_flag * (imag + shift_imag)


def add_sources(start, first_start, place_of, cells_ref, wavelet_ref):
    count, _, _, shots, lanes = start.shape
    lane_row = lax.broadcasted_iota(jnp.int32, (1, lanes), 1)
    for s in range(shots):
        place = place_of(cells_ref[0, s]) - first_start

        @pl.when((place >= 0) & (place < count))
        def _():
            column = cells_ref[1, s]
            hit = lane_row == cells_ref[2, s]
            for part in range(2):
                start[place, column, part, s : s + 1, :] += jnp.where(hit, wavelet_ref[part, s], 0.0)


def split_level(source, level, split_ref, more=None):
    ref, plane = source
    width, parts, shots, lanes = ref.shape[1:]
    fields = parts * shots
    for column in range(width):
        value = ref[plane, column]
        if more is not None:
            value = value + more[0][more[1], column]
        value = value.reshape(fields, lanes)
        for part in range(3):
            short = value.astype(jnp.bfloat16)
            row = (part * BLOCKS + level) * fields
            split_ref[row : row + fields, column * lanes : (column + 1) * lanes] = short
            if part < 2:
                value = value - short.astype(jnp.float32)


def products_of(split_ref):
    chunk = split_ref[...]
    return lax.dot_general(
        chunk, chunk, (((1,), (1,)), ((), ())), preferred_element_type=jnp.float32
    )


def pack_kernel(guess_ref, class_ref, layer_ref, edge_ref, next_ref, near_ref, codes_ref, held, sems):
    layers, parts, shots, width, lanes = guess_ref.shape
    fields = parts * shots
    odd = lax.rem(lax.axis_index("gz"), 2) == 1
    planes = guess_ref.reshape(layers * fields, width, lanes)
    edge = jnp.where(odd, layers - 1, 0) * fields
    begin = jnp.where(odd, 0, layers - REACH) * fields
    code = jnp.where(odd, 0, layers - 2)
    edge_code = jnp.where(odd, layers - 1, 0)
    moves = [(class_ref, held.at[0]), (layer_ref, held.at[1])]
    moves.append((planes.at[pl.ds(edge, fields)], edge_ref.at[pl.ds(0, fields)]))
    for k in range(REACH):
        moves.append(
            (planes.at[pl.ds(begin + k * fields, fields)], near_ref.at[pl.ds(k * fields, fields)])
        )
    copies = []
    for number, (source, target) in enumerate(moves):
        copies.append(pltpu.make_async_copy(source, target, sems.at[number]))
        copies[-1].start()
    copies[0].wait()
    copies[1].wait()
    for kind in range(2):
        for q in range(layers):
            codes_ref[kind, q] = held[kind, q].astype(jnp.float32)
        for k in range(2):
            near_ref[REACH * fields + 2 * kind + k] = held[kind, code + k].astype(jnp.float32)
        edge_ref[fields + kind] = held[kind, edge_code].astype(jnp.float32)
    for copy in copies[2:]:
        copy.wait()
    following = jnp.where(odd, REACH - 1, 0) * fields
    next_ref[...] = near_ref[pl.ds(following, fields)]


def orientation(layers, depth_total):
    index = lax.axis_index("gz")
    odd = lax.rem(index, 2) == 1
    first_plane = index * layers

    def place_of(plane):
        local = plane - first_plane
        return jnp.where(odd, local, layers - 1 - local)

    def inside(place):
        plane = first_plane + jnp.where(odd, place, layers - 1 - place)
        return jnp.where((plane >= 0) & (plane < depth_total), 1.0, 0.0).astype(jnp.float32)

    return odd, place_of, inside


def early_kernel(
    depth_total,
    wave_ref,
    damp_ref,
    cells_ref,
    wavelet_ref,
    edge_ref,
    own_ref,
    near_ref,
    codes_ref,
    field,
    start,
    tables,
    shift_ref,
):
    _, layers, width, lanes = codes_ref.shape
    parts, shots = start.shape[2:4]
    fields = parts * shots
    odd, place_of, inside = orientation(layers, depth_total)
    own_rows = own_ref.reshape(own_ref.shape[0] * width, lanes)
    edge_rows = edge_ref.reshape(edge_ref.shape[0] * width, lanes)
    near_rows = near_ref.reshape(near_ref.shape[0] * width, lanes)
    span = fields * width
    keep = edge_masks(shots, lanes)
    diagonal = lax.broadcasted_iota(jnp.int32, shift_ref.shape[1:], 0) == lax.broadcasted_iota(
        jnp.int32, shift_ref.shape[1:], 1
    )
    for part, value in enumerate(shift_of(wave_ref, damp_ref)):
        shift_ref[part] = jnp.where(diagonal, value, 0.0)

    extra = REACH * fields
    for k in range(2):
        pick = jnp.where(odd, k, 1 - k)
        fill_tables(
            tables, k, near_ref[extra + pick], near_ref[extra + 2 + pick], inside(k - 2), wave_ref, damp_ref
        )
    for q in range(layers):
        pick = jnp.where(odd, q, layers - 1 - q)
        fill_tables(
            tables, q + 2, codes_ref[0, pick], codes_ref[1, pick], jnp.float32(1.0), wave_ref, damp_ref
        )

    def bring_near(k, carry):
        bring(near_rows, jnp.where(odd, k, REACH - 1 - k) * span, field, k)
        return carry

    def bring_own(q, carry):
        bring(own_rows, jnp.where(odd, q, REACH - 1 - q) * span, field, q + REACH)
        return carry

    lax.fori_loop(0, REACH, bring_near, 0)
    lax.fori_loop(0, REACH, bring_own, 0)
    bring(edge_rows, 0, field, REACH + layers - 1)

    def start_plane(i, carry):
        stencil_plane(
            ((field, i), (field, i + 1), (field, i + 2)),
            (start, i),
            (tables, i, 0),
            inside(i - 2) * (-1.0 / 30.0),
            keep,
        )
        return carry

    lax.fori_loop(0, layers + 1, start_plane, 0)
    add_sources(start, -2, place_of, cells_ref, wavelet_ref)


def image_kernel(
    depth_total,
    start,
    tables,
    first,
    split_ref,
    products_ref,
    send_ref,
    second,
    coupled,
):
    _, width, _, shots, lanes = start.shape
    layers = start.shape[0] - 1
    _, _, inside = orientation(layers, depth_total)
    keep = edge_masks(shots, lanes)
    couple_plane((start, layers), (coupled, 0), -1.0 / 30.0, keep)
    couple_plane((coupled, 0), (send_ref, 0), -1.0 / 30.0, keep)

    def first_plane(j, carry):
        stencil_plane(
            ((start, j), (start, j + 1), (start, j + 2)),
            (first, j),
            (tables, j + 1, 1),
            inside(j - 1) * (1.0 / 30.0),
            keep,
        )
        return carry

    lax.fori_loop(0, layers - 1, first_plane, 0)
    products = jnp.zeros(products_ref.shape, jnp.float32)
    for k in range(layers - 3):
        stencil_plane(
            ((first, k), (first, k + 1), (first, k + 2)),
            (second, k),
            (tables, k + 2, 1),
            1.0 / 30.0,
            keep,
        )
        for level, source in enumerate(((start, k + 2), (first, k + 1), (second, k))):
            split_level(source, level, split_ref)
        products += products_of(split_ref)
    products_ref[...] = products


def pack_gram(products, shots, cells):
    fields = 2 * shots
    rows = BLOCKS * fields
    summed = products[0:rows] + products[rows : 2 * rows] + products[2 * rows : 3 * rows]
    summed = summed[:, 0:rows] + summed[:, rows : 2 * rows] + summed[:, 2 * rows : 3 * rows]
    summed = summed * (1.0 / cells)
    summed = jnp.concatenate([summed, jnp.zeros((rows, 128 - rows), jnp.float32)], axis=1)
    lane = lax.broadcasted_iota(jnp.int32, (shots, 128), 1)
    blocks = []
    for level in range(BLOCKS):
        real_rows = summed[level * fields : level * fields + shots]
        imag_rows = summed[level * fields + shots : (level + 1) * fields]
        both = jnp.where(
            lax.rem(lane, fields) < shots,
            real_rows + pltpu.roll(imag_rows, 128 - shots, 1),
            real_rows - pltpu.roll(imag_rows, shots, 1),
        )
        blocks.append(both[:, level * fields : rows])
    blocks.append(jnp.zeros((shots, 128 - len(PAIRS) * fields), jnp.float32))
    return jnp.concatenate(blocks, axis=1)


def stage_kernel(stage, depth_total, layers, names, places, *refs):
    refs = dict(zip(names, refs))
    first, second, far_ref = refs["first"], refs["second"], refs["far"]
    field, start = refs["field"], refs["start"]
    own_tables = refs["own_tables"]
    _, width, parts, shots, lanes = first.shape
    odd, place_of, inside = orientation(layers, depth_total)
    keep = edge_masks(shots, lanes)
    top = layers - 1 + stage

    def old(name):
        return (refs[name], places[name])

    if stage == 0:
        start_table = (own_tables, top + 2, 0)
    else:
        fill_tables(
            refs["tables"],
            0,
            refs["nearest"][parts * shots],
            refs["nearest"][parts * shots + 1],
            inside(jnp.int32(top)),
            refs["wave"],
            refs["damp"],
        )
        start_table = (refs["tables"], 0, 0)
    bring(far_ref.reshape(far_ref.shape[0] * width, lanes), 0, field, 0)
    stencil_plane(
        (old("field_a"), old("field_b"), (field, 0)),
        (start, 0),
        start_table,
        inside(jnp.int32(top)) * (-1.0 / 30.0),
        keep,
    )
    add_sources(start, top, place_of, refs["cells"], refs["wavelet"])
    stencil_plane(
        (old("start_a"), old("start_b"), (start, 0)),
        (first, 0),
        (own_tables, top + 1, 1),
        1.0 / 30.0,
        keep,
    )
    stencil_plane(
        (old("first_a"), old("first_b"), (first, 0)),
        (second, 0),
        (own_tables, top, 1),
        1.0 / 30.0,
        keep,
    )
    if stage == 1:
        outer, base = refs["outer"], refs["base"]
        stencil_plane(
            (old("start_b"), (start, 0), None),
            (outer, 0),
            (refs["tables"], 0, 1),
            inside(jnp.int32(top)) * (1.0 / 30.0),
            keep,
        )
        stencil_plane(
            (old("first_b"), (first, 0), (outer, 0)),
            (base, 0),
            (own_tables, top + 1, 1),
            1.0 / 30.0,
            keep,
        )
    split_ref = refs["split"]
    for level, source in enumerate((old("start_a"), old("first_b"), (second, 0))):
        split_level(source, level, split_ref)
    if stage == 1:
        for level, source in enumerate((old("start_b"), (first, 0))):
            split_level(source, level, refs["next_split"])
    refs["products"][...] = refs["products_in"][...] + products_of(split_ref)


def last_kernel(cells, far_ref, base_ref, products_ref, begun_ref, split_ref, grams_ref):
    split_level((base_ref, 0), 2, split_ref, (far_ref, 0))
    packed = pack_gram(products_ref[...] + products_of(split_ref), far_ref.shape[3], cells)
    for copy in range(grams_ref.shape[0]):
        grams_ref[copy] = packed


def back_kernel(
    shift_ref, grams_ref, *rest
):
    basis_ref, hessenberg_ref = rest[-2:]
    layers, parts, shots, width, y = basis_ref.shape
    fields = parts * shots
    rows = BLOCKS * fields
    half = rows // 2
    tile = shots
    tiles = BLOCKS
    spread = BLOCKS * rows
    lanes = 128
    lead = spread - lanes

    grams = [grams_ref[i] for i in range(grams_ref.shape[0])]
    while len(grams) > 1:
        grams = [sum(grams[i : i + 2]) for i in range(0, len(grams), 2)]
    packed = grams[0]
    turned = packed.T
    lane = lax.broadcasted_iota(jnp.int32, (tile, lanes), 1)
    sub = lax.broadcasted_iota(jnp.int32, (tile, lanes), 0)
    wide_lane = lax.broadcasted_iota(jnp.int32, (tile, 2 * lanes), 1)
    wide_sub = lax.broadcasted_iota(jnp.int32, (tile, 2 * lanes), 0)
    column = lax.rem(wide_lane, rows) // fields * tile + lax.rem(wide_lane, tile)
    real, imag = [], []
    for t in range(tiles):
        match = (wide_lane < spread) & (column == wide_sub + t * tile)
        unit = jnp.where(match, 1.0, 0.0).astype(jnp.float32)
        blank = jnp.zeros((tile, lanes), jnp.float32)
        parts_of = []
        for part in range(2):
            blocks = [jnp.zeros((tile, lead), jnp.float32)]
            for j in range(tiles):
                if j >= t:
                    begin = (2 * PAIRS.index((t, j)) + part) * tile
                    blocks.append(packed[:, begin : begin + tile])
                else:
                    begin = (2 * PAIRS.index((j, t)) + part) * tile
                    block = turned[begin : begin + tile, 0:tile]
                    blocks.append(block if part == 0 else -block)
            blocks.append(jnp.zeros((tile, lanes - lead - half), jnp.float32))
            parts_of.append(jnp.concatenate(blocks, axis=1))
        real.append(unit + jnp.concatenate([blank, parts_of[0]], axis=1))
        imag.append(jnp.concatenate([blank, parts_of[1]], axis=1))
    pivots = []
    for owner in range(tiles):
        spots = [spread + owner * tile + r for r in range(tile)]
        shape = (tile, lanes)
        ahead = {
            (t, r): [
                jnp.broadcast_to(values[t][:, spots[r] : spots[r] + 1], shape) for values in (real, imag)
            ]
            for t in range(owner, tiles)
            for r in range(tile)
        }
        for r in range(tile):
            own_real, own_imag = ahead[owner, r]
            pivot = jnp.broadcast_to(own_real[r : r + 1], shape)
            pivots.append(pivot)
            inverse = pl.reciprocal(pivot, approx=True)
            inverse = inverse * (2.0 - pivot * inverse)
            scaled = {}
            for t in range(owner, tiles):
                column_real, column_imag = [value * inverse for value in ahead[t, r]]
                if t == owner:
                    column_real = jnp.where(sub > r, column_real, 0.0)
                    column_imag = jnp.where(sub > r, column_imag, 0.0)
                scaled[t] = column_real, column_imag
            for later in range(r + 1, tile):
                entry_real = jnp.broadcast_to(own_real[later : later + 1], shape)
                entry_imag = jnp.broadcast_to(own_imag[later : later + 1], shape)
                for t in range(owner, tiles):
                    column_real, column_imag = scaled[t]
                    old_real, old_imag = ahead[t, later]
                    ahead[t, later] = [
                        old_real - (column_real * entry_real + column_imag * entry_imag),
                        old_imag - (column_imag * entry_real - column_real * entry_imag),
                    ]
            row_real = real[owner][r : r + 1]
            row_imag = imag[owner][r : r + 1]
            for t in range(owner, tiles):
                column_real, column_imag = [
                    jnp.concatenate([value, value], axis=1) for value in scaled[t]
                ]
                new_real = real[t] - (column_real * row_real - column_imag * row_imag)
                new_imag = imag[t] - (column_real * row_imag + column_imag * row_real)
                real[t], imag[t] = new_real, new_imag
    for t in range(tiles):
        scales = pivots[t * tile]
        for r in range(1, tile):
            scales = jnp.where(sub == r, pivots[t * tile + r], scales)
        scales = lax.rsqrt(scales)
        scales = jnp.concatenate([scales, scales], axis=1)
        real[t] = real[t] * scales
        imag[t] = imag[t] * scales

    last_real, last_imag = real[tiles - 1], imag[tiles - 1]
    first_half = lax.rem(wide_lane, fields) < tile
    mix = jnp.concatenate(
        [
            jnp.where(first_half, last_real, last_imag),
            jnp.where(first_half, -last_imag, last_real),
        ],
        axis=0,
    )
    pieces = []
    for part in range(3):
        short = mix.astype(jnp.bfloat16)
        pieces.append(short)
        mix = mix - short.astype(jnp.float32)
    left = jnp.concatenate(pieces, axis=0)[:, 0:spread]

    odd = lax.rem(lax.axis_index("gz"), 2) == 1
    out_rows = basis_ref.reshape(layers * fields * width, y)
    spots = [
        (ref, spot)
        for ref in rest[:-2]
        for spot in range(ref.shape[1] // (width * y))
    ]
    group = 16
    for q in range(layers):
        source, spot = spots[q]
        plane = jnp.where(odd, q, layers - 1 - q)
        for begin in range(0, width, group):
            offset = (spot * width + begin) * y
            mixed = jnp.dot(
                left, source[:, offset : offset + group * y], preferred_element_type=jnp.float32
            )
            mixed = mixed[0:fields] + mixed[fields : 2 * fields] + mixed[2 * fields : 3 * fields]
            for column in range(group):
                out_rows[pl.ds(plane * (fields * width) + begin + column, fields, stride=width), :] = mixed[
                    :, column * y : (column + 1) * y
                ]

    wide = 2 * tile
    full_real = jnp.concatenate(real, axis=0)
    full_imag = jnp.concatenate(imag, axis=0)
    row_index = lax.broadcasted_iota(jnp.int32, (half, wide), 0)
    column_index = lax.broadcasted_iota(jnp.int32, (half, wide), 1)
    upper = row_index <= column_index + tile
    factor_real = jnp.where(upper, full_real[:, spread + tile : spread + half], 0.0)
    factor_imag = jnp.where(upper, full_imag[:, spread + tile : spread + half], 0.0)
    lower_real, lower_imag = [
        jnp.concatenate([value[0:wide, 0:tile], value[0:wide, fields : fields + tile]], axis=1)
        for value in (full_real, full_imag)
    ]

    def times(left, right):
        return lax.dot_general(
            left,
            right,
            (((1,), (1,)), ((), ())),
            precision=lax.Precision.HIGHEST,
            preferred_element_type=jnp.float32,
        )

    hessenberg_ref[0] = (
        times(lower_real, factor_real)
        + times(lower_imag, factor_imag)
        + shift_ref[0]
    )
    hessenberg_ref[1] = (
        times(lower_real, factor_imag)
        - times(lower_imag, factor_real)
        + shift_ref[1]
    )


def shards(initial_guess, velocity_class, layer_code, wavenumber, damping, shot_cells, wavelet):
    layers, parts, shots, width, lanes = initial_guess.shape
    devices = lax.axis_size("gz")
    assert layers == REACH + 1 and devices % 2 == 0
    fields = parts * shots
    rows = BLOCKS * fields
    span = width * lanes
    depth_total = devices * layers
    shot_cells = shot_cells.T

    smem = pl.BlockSpec(memory_space=pltpu.SMEM)
    vmem = pl.BlockSpec(memory_space=pltpu.VMEM)
    hbm = pl.BlockSpec(memory_space=pl.ANY)
    params = pltpu.CompilerParams(vmem_limit_bytes=VMEM_BYTES)


    def float_shape(*dims):
        return jax.ShapeDtypeStruct(dims, jnp.float32)

    odd_to_even = [(i, i + 1) for i in range(1, devices - 1, 2)]
    even_to_odd = [(i, i + 1) for i in range(0, devices, 2)]
    far_pairs = odd_to_even + [(b, a) for a, b in odd_to_even]
    near_pairs = even_to_odd + [(b, a) for a, b in even_to_odd]

    edge, following, near, codes = pl.pallas_call(
        pack_kernel,
        out_shape=(
            float_shape(fields + 2, width, lanes),
            float_shape(fields, width, lanes),
            float_shape(REACH * fields + 4, width, lanes),
            float_shape(2, layers, width, lanes),
        ),
        in_specs=[hbm, hbm, hbm],
        out_specs=(vmem, vmem, vmem, vmem),
        scratch_shapes=[
            pltpu.VMEM((2, layers, width, lanes), jnp.int32),
            pltpu.SemaphoreType.DMA((3 + REACH,)),
        ],
        compiler_params=params,
        name="pack",
    )(
        *(
            pltpu.with_memory_space_constraint(array, pltpu.HBM)
            for array in (initial_guess, velocity_class, layer_code)
        )
    )
    nearest = lax.ppermute(edge, "gz", far_pairs)
    second_far = lax.ppermute(following, "gz", far_pairs)
    own = near
    near = lax.ppermute(own, "gz", near_pairs)

    def planes(count):
        return float_shape(count, width, parts, shots, lanes)

    def tables(count):
        return float_shape(count, 4, width, lanes)

    def split(count):
        return jax.ShapeDtypeStruct((BLOCKS * rows, count * span), jnp.bfloat16)

    def scratch(shape):
        return pltpu.VMEM(shape.shape, shape.dtype)

    products = float_shape(BLOCKS * rows, BLOCKS * rows)
    cost = pl.CostEstimate(flops=10_000_000, bytes_accessed=16_000_000, transcendentals=0)
    common = (wavenumber, damping, shot_cells, wavelet)
    turned_shape = float_shape(2, 2 * shots, BLOCKS * shots)
    field, start, own_tables, shift = pl.pallas_call(
        functools.partial(early_kernel, depth_total),
        out_shape=(planes(layers + REACH), planes(layers + 1), tables(layers + 2), turned_shape),
        in_specs=[smem] * 4 + [vmem] * 4,
        out_specs=(vmem,) * 4,
        compiler_params=params,
        cost_estimate=cost,
        name="early",
    )(*common, edge, own, near, codes)
    first, early_split, early_products, send = pl.pallas_call(
        functools.partial(image_kernel, depth_total),
        out_shape=(planes(layers - 1), split(layers - 3), products, planes(1)),
        in_specs=[vmem] * 2,
        out_specs=(vmem,) * 4,
        scratch_shapes=[scratch(planes(layers - 3)), scratch(planes(1))],
        compiler_params=params,
        cost_estimate=cost,
        name="images",
    )(start, own_tables)
    third_far = lax.ppermute(send, "gz", far_pairs)
    shapes = {
        "field": planes(1),
        "start": planes(1),
        "first": planes(1),
        "second": planes(1),
        "tables": tables(1),
        "split": split(1),
        "next_split": split(1),
        "outer": planes(1),
        "base": planes(1),
        "products": products,
    }

    def run_stage(stage, far, old, extra, outs, temporaries):
        inputs = dict(zip(("wave", "damp", "cells", "wavelet"), common))
        scalars = len(inputs)
        inputs["far"] = far
        inputs.update({name: array for name, (array, _) in old.items()})
        inputs.update(extra)
        results = pl.pallas_call(
            functools.partial(
                stage_kernel,
                stage,
                depth_total,
                layers,
                list(inputs) + outs + temporaries,
                {name: place for name, (_, place) in old.items()},
            ),
            out_shape=tuple(shapes[name] for name in outs),
            in_specs=[smem] * scalars + [vmem] * (len(inputs) - scalars),
            out_specs=(vmem,) * len(outs),
            scratch_shapes=[scratch(shapes[name]) for name in temporaries],
            compiler_params=params,
            cost_estimate=cost,
            name="stage_%d" % stage,
        )(*inputs.values())
        return dict(zip(outs, results))

    zero = run_stage(
        0,
        nearest,
        {
            "field_a": (field, layers + 1),
            "field_b": (field, layers + 2),
            "start_a": (start, layers - 1),
            "start_b": (start, layers),
            "first_a": (first, layers - 3),
            "first_b": (first, layers - 2),
        },
        {"own_tables": own_tables, "products_in": early_products},
        ["field", "start", "first", "split", "products"],
        ["second"],
    )
    one = run_stage(
        1,
        second_far,
        {
            "field_a": (field, layers + 2),
            "field_b": (zero["field"], 0),
            "start_a": (start, layers),
            "start_b": (zero["start"], 0),
            "first_a": (first, layers - 2),
            "first_b": (zero["first"], 0),
        },
        {"own_tables": own_tables, "products_in": zero["products"], "nearest": nearest},
        ["base", "split", "products", "next_split"],
        ["field", "start", "first", "second", "tables", "outer"],
    )
    last_split, grams = pl.pallas_call(
        functools.partial(last_kernel, float(depth_total * span)),
        out_shape=(split(1), float_shape(devices, shots, 128)),
        in_specs=[vmem] * 4,
        out_specs=(vmem, vmem),
        input_output_aliases={3: 0},
        compiler_params=params,
        name="last",
    )(third_far, one["base"], one["products"], one["next_split"])
    grams = lax.all_to_all(grams, "gz", 0, 0)
    basis_two, turned = pl.pallas_call(
        back_kernel,
        out_shape=(
            jax.ShapeDtypeStruct(initial_guess.shape, jnp.float32),
            turned_shape,
        ),
        in_specs=[vmem] * 6,
        out_specs=(vmem, vmem),
        compiler_params=params,
        name="back",
    )(shift, grams, early_split, zero["split"], one["split"], last_split)
    return basis_two, jnp.swapaxes(turned, 1, 2)


def solution(mesh):
    return jax.shard_map(
        shards,
        mesh=mesh,
        in_specs=(
            P(("freq", "gz"), None, None, None, None),
            P("gz", None, None),
            P("gz", None, None),
            P("freq"),
            P(),
            P(),
            P("freq", None),
        ),
        out_specs=(P(("freq", "gz"), None, None, None, None), P("freq", None, None)),
        check_vma=False,
    )
```

```python
import functools

import jax
import jax.numpy as jnp
from jax import lax
from jax.experimental import pallas as pl
from jax.experimental.pallas import tpu as pltpu
from jax.sharding import PartitionSpec as P

SHIFT_BASE = 1.5
BLOCKS = 3
REACH = 3
VMEM_BYTES = 24 * 1024 * 1024
PAIRS = ((0, 0), (0, 1), (0, 2), (1, 1), (1, 2), (2, 2))


def shift_of(wave_ref, damp_ref):
    classes, levels = wave_ref.shape[0], damp_ref.shape[0]
    wave_mean = sum(wave_ref[i] for i in range(classes)) * (1.0 / classes)
    damp_mean = sum(damp_ref[i] for i in range(levels)) * (1.0 / levels)
    return SHIFT_BASE - wave_mean, -wave_mean * damp_mean


def edge_masks(shots, lanes):
    lane = lax.broadcasted_iota(jnp.int32, (shots, lanes), 1)
    return (
        jnp.where(lane == 0, 0.0, 1.0).astype(jnp.float32),
        jnp.where(lane == lanes - 1, 0.0, 1.0).astype(jnp.float32),
    )


def stencil_plane(sources, target, table, scale, keep):
    (low, low_plane), (mid, mid_plane), high = sources
    out, out_plane = target
    table_ref, table_plane, kind = table
    width = table_ref.shape[2]
    left, right = keep

    def load(column):
        center, away = [], []
        for part in range(2):
            v = mid[mid_plane, column, part]
            d = low[low_plane, column, part]
            if high is not None:
                d = d + high[0][high[1], column, part]
            center.append(v)
            away.append(d + 3.0 * v)
        return center, away

    here_v, here_u = load(0)
    before_v = [jnp.zeros_like(v) for v in here_v]
    before_u = before_v
    for column in range(width):
        if column + 1 < width:
            after_v, after_u = load(column + 1)
        else:
            after_v = [jnp.zeros_like(v) for v in here_v]
            after_u = after_v
        real_row, imag_row = [
            jnp.broadcast_to(table_ref[table_plane, 2 * kind + part, column : column + 1, :], here_v[0].shape)
            for part in range(2)
        ]
        for part in range(2):
            near = here_u[part] + (before_v[part] + after_v[part])
            wide = (before_u[part] + after_u[part]) + (3.0 * here_u[part] + 5.0 * here_v[part])
            sides = pltpu.roll(wide, 1, 1) * left + pltpu.roll(wide, 127, 1) * right
            total = 3.0 * wide + 5.0 * near + sides
            if part == 0:
                own = real_row * here_v[0] + imag_row * here_v[1]
            else:
                own = real_row * here_v[1] - imag_row * here_v[0]
            out[out_plane, column, part] = own - scale * total
        before_v, before_u, here_v, here_u = here_v, here_u, after_v, after_u


def couple_plane(source, target, scale, keep):
    ref, plane = source
    out, out_plane = target
    width = ref.shape[1]
    left, right = keep
    blank = jnp.zeros(ref.shape[3:], jnp.float32)
    for part in range(2):
        before, here = blank, ref[plane, 0, part]
        for column in range(width):
            after = ref[plane, column + 1, part] if column + 1 < width else blank
            wide = (before + after) + 3.0 * here
            sides = pltpu.roll(wide, 1, 1) * left + pltpu.roll(wide, 127, 1) * right
            out[out_plane, column, part] = scale * (3.0 * wide + 5.0 * here + sides)
            before, here = here, after


def bring(rows, first_row, field, plane):
    width, parts, shots = field.shape[1:4]
    for column in range(width):
        for part in range(parts):
            field[plane, column, part] = rows[
                pl.ds(first_row + part * shots * width + column, shots, stride=width), :
            ]


def fill_tables(tables, plane, labels, codes, inside_flag, wave_ref, damp_ref):
    shift_real, shift_imag = shift_of(wave_ref, damp_ref)
    wave = jnp.zeros(labels.shape, jnp.float32)
    for i in range(wave_ref.shape[0]):
        wave = jnp.where(labels == float(i), wave_ref[i], wave)
    loss = jnp.zeros(labels.shape, jnp.float32)
    for i in range(damp_ref.shape[0]):
        loss = jnp.where(codes == float(i), damp_ref[i], loss)
    real = 185.0 / 30.0 - wave
    imag = wave * loss
    tables[plane, 0] = -inside_flag * real
    tables[plane, 1] = -inside_flag * imag
    tables[plane, 2] = inside_flag * (real - shift_real)
    tables[plane, 3] = inside_flag * (imag + shift_imag)


def add_sources(start, first_start, place_of, cells_ref, wavelet_ref):
    count, _, _, shots, lanes = start.shape
    lane_row = lax.broadcasted_iota(jnp.int32, (1, lanes), 1)
    for s in range(shots):
        place = place_of(cells_ref[0, s]) - first_start

        @pl.when((place >= 0) & (place < count))
        def _():
            column = cells_ref[1, s]
            hit = lane_row == cells_ref[2, s]
            for part in range(2):
                start[place, column, part, s : s + 1, :] += jnp.where(hit, wavelet_ref[part, s], 0.0)


def split_level(source, level, split_ref, more=None):
    ref, plane = source
    width, parts, shots, lanes = ref.shape[1:]
    fields = parts * shots
    for column in range(width):
        value = ref[plane, column]
        if more is not None:
            value = value + more[0][more[1], column]
        value = value.reshape(fields, lanes)
        for part in range(3):
            short = value.astype(jnp.bfloat16)
            row = (part * BLOCKS + level) * fields
            split_ref[row : row + fields, column * lanes : (column + 1) * lanes] = short
            if part < 2:
                value = value - short.astype(jnp.float32)


def products_of(split_ref):
    chunk = split_ref[...]
    return lax.dot_general(
        chunk, chunk, (((1,), (1,)), ((), ())), preferred_element_type=jnp.float32
    )


def pack_kernel(guess_ref, class_ref, layer_ref, edge_ref, next_ref, near_ref, codes_ref, held, sems):
    layers, parts, shots, width, lanes = guess_ref.shape
    fields = parts * shots
    odd = lax.rem(lax.axis_index("gz"), 2) == 1
    planes = guess_ref.reshape(layers * fields, width, lanes)
    edge = jnp.where(odd, layers - 1, 0) * fields
    begin = jnp.where(odd, 0, layers - REACH) * fields
    code = jnp.where(odd, 0, layers - 2)
    edge_code = jnp.where(odd, layers - 1, 0)
    moves = [(class_ref, held.at[0]), (layer_ref, held.at[1])]
    moves.append((planes.at[pl.ds(edge, fields)], edge_ref.at[pl.ds(0, fields)]))
    for k in range(REACH):
        moves.append(
            (planes.at[pl.ds(begin + k * fields, fields)], near_ref.at[pl.ds(k * fields, fields)])
        )
    copies = []
    for number, (source, target) in enumerate(moves):
        copies.append(pltpu.make_async_copy(source, target, sems.at[number]))
        copies[-1].start()
    copies[0].wait()
    copies[1].wait()
    for kind in range(2):
        for q in range(layers):
            codes_ref[kind, q] = held[kind, q].astype(jnp.float32)
        for k in range(2):
            near_ref[REACH * fields + 2 * kind + k] = held[kind, code + k].astype(jnp.float32)
        edge_ref[fields + kind] = held[kind, edge_code].astype(jnp.float32)
    for copy in copies[2:]:
        copy.wait()
    following = jnp.where(odd, REACH - 1, 0) * fields
    next_ref[...] = near_ref[pl.ds(following, fields)]


def orientation(layers, depth_total):
    index = lax.axis_index("gz")
    odd = lax.rem(index, 2) == 1
    first_plane = index * layers

    def place_of(plane):
        local = plane - first_plane
        return jnp.where(odd, local, layers - 1 - local)

    def inside(place):
        plane = first_plane + jnp.where(odd, place, layers - 1 - place)
        return jnp.where((plane >= 0) & (plane < depth_total), 1.0, 0.0).astype(jnp.float32)

    return odd, place_of, inside


def early_kernel(
    depth_total,
    wave_ref,
    damp_ref,
    cells_ref,
    wavelet_ref,
    edge_ref,
    own_ref,
    near_ref,
    codes_ref,
    field,
    start,
    tables,
    shift_ref,
):
    _, layers, width, lanes = codes_ref.shape
    parts, shots = start.shape[2:4]
    fields = parts * shots
    odd, place_of, inside = orientation(layers, depth_total)
    own_rows = own_ref.reshape(own_ref.shape[0] * width, lanes)
    edge_rows = edge_ref.reshape(edge_ref.shape[0] * width, lanes)
    near_rows = near_ref.reshape(near_ref.shape[0] * width, lanes)
    span = fields * width
    keep = edge_masks(shots, lanes)
    diagonal = lax.broadcasted_iota(jnp.int32, shift_ref.shape[1:], 0) == lax.broadcasted_iota(
        jnp.int32, shift_ref.shape[1:], 1
    )
    for part, value in enumerate(shift_of(wave_ref, damp_ref)):
        shift_ref[part] = jnp.where(diagonal, value, 0.0)

    extra = REACH * fields
    for k in range(2):
        pick = jnp.where(odd, k, 1 - k)
        fill_tables(
            tables, k, near_ref[extra + pick], near_ref[extra + 2 + pick], inside(k - 2), wave_ref, damp_ref
        )
    for q in range(layers):
        pick = jnp.where(odd, q, layers - 1 - q)
        fill_tables(
            tables, q + 2, codes_ref[0, pick], codes_ref[1, pick], jnp.float32(1.0), wave_ref, damp_ref
        )

    def bring_near(k, carry):
        bring(near_rows, jnp.where(odd, k, REACH - 1 - k) * span, field, k)
        return carry

    def bring_own(q, carry):
        bring(own_rows, jnp.where(odd, q, REACH - 1 - q) * span, field, q + REACH)
        return carry

    lax.fori_loop(0, REACH, bring_near, 0)
    lax.fori_loop(0, REACH, bring_own, 0)
    bring(edge_rows, 0, field, REACH + layers - 1)

    def start_plane(i, carry):
        stencil_plane(
            ((field, i), (field, i + 1), (field, i + 2)),
            (start, i),
            (tables, i, 0),
            inside(i - 2) * (-1.0 / 30.0),
            keep,
        )
        return carry

    lax.fori_loop(0, layers + 1, start_plane, 0)
    add_sources(start, -2, place_of, cells_ref, wavelet_ref)


def image_kernel(
    depth_total,
    start,
    tables,
    first,
    split_ref,
    products_ref,
    send_ref,
    second,
    coupled,
):
    _, width, _, shots, lanes = start.shape
    layers = start.shape[0] - 1
    _, _, inside = orientation(layers, depth_total)
    keep = edge_masks(shots, lanes)
    couple_plane((start, layers), (coupled, 0), -1.0 / 30.0, keep)
    couple_plane((coupled, 0), (send_ref, 0), -1.0 / 30.0, keep)

    def first_plane(j, carry):
        stencil_plane(
            ((start, j), (start, j + 1), (start, j + 2)),
            (first, j),
            (tables, j + 1, 1),
            inside(j - 1) * (1.0 / 30.0),
            keep,
        )
        return carry

    lax.fori_loop(0, layers - 1, first_plane, 0)
    products = jnp.zeros(products_ref.shape, jnp.float32)
    for k in range(layers - 3):
        stencil_plane(
            ((first, k), (first, k + 1), (first, k + 2)),
            (second, k),
            (tables, k + 2, 1),
            1.0 / 30.0,
            keep,
        )
        for level, source in enumerate(((start, k + 2), (first, k + 1), (second, k))):
            split_level(source, level, split_ref)
        products += products_of(split_ref)
    products_ref[...] = products


def pack_gram(products, shots, cells):
    fields = 2 * shots
    rows = BLOCKS * fields
    summed = products[0:rows] + products[rows : 2 * rows] + products[2 * rows : 3 * rows]
    summed = summed[:, 0:rows] + summed[:, rows : 2 * rows] + summed[:, 2 * rows : 3 * rows]
    summed = summed * (1.0 / cells)
    summed = jnp.concatenate([summed, jnp.zeros((rows, 128 - rows), jnp.float32)], axis=1)
    lane = lax.broadcasted_iota(jnp.int32, (shots, 128), 1)
    blocks = []
    for level in range(BLOCKS):
        real_rows = summed[level * fields : level * fields + shots]
        imag_rows = summed[level * fields + shots : (level + 1) * fields]
        both = jnp.where(
            lax.rem(lane, fields) < shots,
            real_rows + pltpu.roll(imag_rows, 128 - shots, 1),
            real_rows - pltpu.roll(imag_rows, shots, 1),
        )
        blocks.append(both[:, level * fields : rows])
    blocks.append(jnp.zeros((shots, 128 - len(PAIRS) * fields), jnp.float32))
    return jnp.concatenate(blocks, axis=1)


def stage_kernel(stage, depth_total, layers, names, places, *refs):
    refs = dict(zip(names, refs))
    first, second, far_ref = refs["first"], refs["second"], refs["far"]
    field, start = refs["field"], refs["start"]
    own_tables = refs["own_tables"]
    _, width, parts, shots, lanes = first.shape
    odd, place_of, inside = orientation(layers, depth_total)
    keep = edge_masks(shots, lanes)
    top = layers - 1 + stage

    def old(name):
        return (refs[name], places[name])

    if stage == 0:
        start_table = (own_tables, top + 2, 0)
    else:
        fill_tables(
            refs["tables"],
            0,
            refs["nearest"][parts * shots],
            refs["nearest"][parts * shots + 1],
            inside(jnp.int32(top)),
            refs["wave"],
            refs["damp"],
        )
        start_table = (refs["tables"], 0, 0)
    bring(far_ref.reshape(far_ref.shape[0] * width, lanes), 0, field, 0)
    stencil_plane(
        (old("field_a"), old("field_b"), (field, 0)),
        (start, 0),
        start_table,
        inside(jnp.int32(top)) * (-1.0 / 30.0),
        keep,
    )
    add_sources(start, top, place_of, refs["cells"], refs["wavelet"])
    stencil_plane(
        (old("start_a"), old("start_b"), (start, 0)),
        (first, 0),
        (own_tables, top + 1, 1),
        1.0 / 30.0,
        keep,
    )
    stencil_plane(
        (old("first_a"), old("first_b"), (first, 0)),
        (second, 0),
        (own_tables, top, 1),
        1.0 / 30.0,
        keep,
    )
    if stage == 1:
        outer, base = refs["outer"], refs["base"]
        stencil_plane(
            (old("start_b"), (start, 0), None),
            (outer, 0),
            (refs["tables"], 0, 1),
            inside(jnp.int32(top)) * (1.0 / 30.0),
            keep,
        )
        stencil_plane(
            (old("first_b"), (first, 0), (outer, 0)),
            (base, 0),
            (own_tables, top + 1, 1),
            1.0 / 30.0,
            keep,
        )
    split_ref = refs["split"]
    for level, source in enumerate((old("start_a"), old("first_b"), (second, 0))):
        split_level(source, level, split_ref)
    if stage == 1:
        for level, source in enumerate((old("start_b"), (first, 0))):
            split_level(source, level, refs["next_split"])
    refs["products"][...] = refs["products_in"][...] + products_of(split_ref)


def last_kernel(cells, far_ref, base_ref, products_ref, begun_ref, split_ref, grams_ref):
    split_level((base_ref, 0), 2, split_ref, (far_ref, 0))
    packed = pack_gram(products_ref[...] + products_of(split_ref), far_ref.shape[3], cells)
    for copy in range(grams_ref.shape[0]):
        grams_ref[copy] = packed


def back_kernel(
    shift_ref, grams_ref, *rest
):
    basis_ref, hessenberg_ref = rest[-2:]
    layers, parts, shots, width, y = basis_ref.shape
    fields = parts * shots
    rows = BLOCKS * fields
    half = rows // 2
    tile = shots
    tiles = BLOCKS
    spread = BLOCKS * rows
    lanes = 128
    lead = spread - lanes

    grams = [grams_ref[i] for i in range(grams_ref.shape[0])]
    while len(grams) > 1:
        grams = [sum(grams[i : i + 2]) for i in range(0, len(grams), 2)]
    packed = grams[0]
    turned = packed.T
    lane = lax.broadcasted_iota(jnp.int32, (tile, lanes), 1)
    sub = lax.broadcasted_iota(jnp.int32, (tile, lanes), 0)
    wide_lane = lax.broadcasted_iota(jnp.int32, (tile, 2 * lanes), 1)
    wide_sub = lax.broadcasted_iota(jnp.int32, (tile, 2 * lanes), 0)
    column = lax.rem(wide_lane, rows) // fields * tile + lax.rem(wide_lane, tile)
    real, imag = [], []
    for t in range(tiles):
        match = (wide_lane < spread) & (column == wide_sub + t * tile)
        unit = jnp.where(match, 1.0, 0.0).astype(jnp.float32)
        blank = jnp.zeros((tile, lanes), jnp.float32)
        parts_of = []
        for part in range(2):
            blocks = [jnp.zeros((tile, lead), jnp.float32)]
            for j in range(tiles):
                if j >= t:
                    begin = (2 * PAIRS.index((t, j)) + part) * tile
                    blocks.append(packed[:, begin : begin + tile])
                else:
                    begin = (2 * PAIRS.index((j, t)) + part) * tile
                    block = turned[begin : begin + tile, 0:tile]
                    blocks.append(block if part == 0 else -block)
            blocks.append(jnp.zeros((tile, lanes - lead - half), jnp.float32))
            parts_of.append(jnp.concatenate(blocks, axis=1))
        real.append(unit + jnp.concatenate([blank, parts_of[0]], axis=1))
        imag.append(jnp.concatenate([blank, parts_of[1]], axis=1))
    pivots = []
    for owner in range(tiles):
        spots = [spread + owner * tile + r for r in range(tile)]
        shape = (tile, lanes)
        ahead = {
            (t, r): [
                jnp.broadcast_to(values[t][:, spots[r] : spots[r] + 1], shape) for values in (real, imag)
            ]
            for t in range(owner, tiles)
            for r in range(tile)
        }
        for r in range(tile):
            own_real, own_imag = ahead[owner, r]
            pivot = jnp.broadcast_to(own_real[r : r + 1], shape)
            pivots.append(pivot)
            inverse = pl.reciprocal(pivot, approx=True)
            inverse = inverse * (2.0 - pivot * inverse)
            scaled = {}
            for t in range(owner, tiles):
                column_real, column_imag = [value * inverse for value in ahead[t, r]]
                if t == owner:
                    column_real = jnp.where(sub > r, column_real, 0.0)
                    column_imag = jnp.where(sub > r, column_imag, 0.0)
                scaled[t] = column_real, column_imag
            for later in range(r + 1, tile):
                entry_real = jnp.broadcast_to(own_real[later : later + 1], shape)
                entry_imag = jnp.broadcast_to(own_imag[later : later + 1], shape)
                for t in range(owner, tiles):
                    column_real, column_imag = scaled[t]
                    old_real, old_imag = ahead[t, later]
                    ahead[t, later] = [
                        old_real - (column_real * entry_real + column_imag * entry_imag),
                        old_imag - (column_imag * entry_real - column_real * entry_imag),
                    ]
            row_real = real[owner][r : r + 1]
            row_imag = imag[owner][r : r + 1]
            for t in range(owner, tiles):
                column_real, column_imag = [
                    jnp.concatenate([value, value], axis=1) for value in scaled[t]
                ]
                new_real = real[t] - (column_real * row_real - column_imag * row_imag)
                new_imag = imag[t] - (column_real * row_imag + column_imag * row_real)
                real[t], imag[t] = new_real, new_imag
    for t in range(tiles):
        scales = pivots[t * tile]
        for r in range(1, tile):
            scales = jnp.where(sub == r, pivots[t * tile + r], scales)
        scales = lax.rsqrt(scales)
        scales = jnp.concatenate([scales, scales], axis=1)
        real[t] = real[t] * scales
        imag[t] = imag[t] * scales

    last_real, last_imag = real[tiles - 1], imag[tiles - 1]
    first_half = lax.rem(wide_lane, fields) < tile
    mix = jnp.concatenate(
        [
            jnp.where(first_half, last_real, last_imag),
            jnp.where(first_half, -last_imag, last_real),
        ],
        axis=0,
    )
    pieces = []
    for part in range(3):
        short = mix.astype(jnp.bfloat16)
        pieces.append(short)
        mix = mix - short.astype(jnp.float32)
    left = jnp.concatenate(pieces, axis=0)[:, 0:spread]

    odd = lax.rem(lax.axis_index("gz"), 2) == 1
    spots = [
        (ref, spot)
        for ref in rest[:-2]
        for spot in range(ref.shape[1] // (width * y))
    ]
    group = 16
    for q in range(layers):
        source, spot = spots[q]
        plane = jnp.where(odd, q, layers - 1 - q)
        for begin in range(0, width, group):
            offset = (spot * width + begin) * y
            mixed = jnp.dot(
                left, source[:, offset : offset + group * y], preferred_element_type=jnp.float32
            )
            mixed = mixed[0:fields] + mixed[fields : 2 * fields] + mixed[2 * fields : 3 * fields]
            turned = mixed.reshape(fields, group, y)
            for part in range(parts):
                basis_ref[plane, part, :, begin : begin + group] = turned[part * shots : (part + 1) * shots]

    wide = 2 * tile
    full_real = jnp.concatenate(real, axis=0)
    full_imag = jnp.concatenate(imag, axis=0)
    row_index = lax.broadcasted_iota(jnp.int32, (half, wide), 0)
    column_index = lax.broadcasted_iota(jnp.int32, (half, wide), 1)
    upper = row_index <= column_index + tile
    factor_real = jnp.where(upper, full_real[:, spread + tile : spread + half], 0.0)
    factor_imag = jnp.where(upper, full_imag[:, spread + tile : spread + half], 0.0)
    lower_real, lower_imag = [
        jnp.concatenate([value[0:wide, 0:tile], value[0:wide, fields : fields + tile]], axis=1)
        for value in (full_real, full_imag)
    ]

    def times(left, right):
        return lax.dot_general(
            left,
            right,
            (((1,), (1,)), ((), ())),
            precision=lax.Precision.HIGHEST,
            preferred_element_type=jnp.float32,
        )

    hessenberg_ref[0] = (
        times(lower_real, factor_real)
        + times(lower_imag, factor_imag)
        + shift_ref[0]
    )
    hessenberg_ref[1] = (
        times(lower_real, factor_imag)
        - times(lower_imag, factor_real)
        + shift_ref[1]
    )


def shards(initial_guess, velocity_class, layer_code, wavenumber, damping, shot_cells, wavelet):
    layers, parts, shots, width, lanes = initial_guess.shape
    devices = lax.axis_size("gz")
    assert layers == REACH + 1 and devices % 2 == 0
    fields = parts * shots
    rows = BLOCKS * fields
    span = width * lanes
    depth_total = devices * layers
    shot_cells = shot_cells.T

    smem = pl.BlockSpec(memory_space=pltpu.SMEM)
    vmem = pl.BlockSpec(memory_space=pltpu.VMEM)
    hbm = pl.BlockSpec(memory_space=pl.ANY)
    params = pltpu.CompilerParams(vmem_limit_bytes=VMEM_BYTES)


    def float_shape(*dims):
        return jax.ShapeDtypeStruct(dims, jnp.float32)

    odd_to_even = [(i, i + 1) for i in range(1, devices - 1, 2)]
    even_to_odd = [(i, i + 1) for i in range(0, devices, 2)]
    far_pairs = odd_to_even + [(b, a) for a, b in odd_to_even]
    near_pairs = even_to_odd + [(b, a) for a, b in even_to_odd]

    edge, following, near, codes = pl.pallas_call(
        pack_kernel,
        out_shape=(
            float_shape(fields + 2, width, lanes),
            float_shape(fields, width, lanes),
            float_shape(REACH * fields + 4, width, lanes),
            float_shape(2, layers, width, lanes),
        ),
        in_specs=[hbm, hbm, hbm],
        out_specs=(vmem, vmem, vmem, vmem),
        scratch_shapes=[
            pltpu.VMEM((2, layers, width, lanes), jnp.int32),
            pltpu.SemaphoreType.DMA((3 + REACH,)),
        ],
        compiler_params=params,
        name="pack",
    )(
        *(
            pltpu.with_memory_space_constraint(array, pltpu.HBM)
            for array in (initial_guess, velocity_class, layer_code)
        )
    )
    nearest = lax.ppermute(edge, "gz", far_pairs)
    second_far = lax.ppermute(following, "gz", far_pairs)
    own = near
    near = lax.ppermute(own, "gz", near_pairs)

    def planes(count):
        return float_shape(count, width, parts, shots, lanes)

    def tables(count):
        return float_shape(count, 4, width, lanes)

    def split(count):
        return jax.ShapeDtypeStruct((BLOCKS * rows, count * span), jnp.bfloat16)

    def scratch(shape):
        return pltpu.VMEM(shape.shape, shape.dtype)

    products = float_shape(BLOCKS * rows, BLOCKS * rows)
    cost = pl.CostEstimate(flops=10_000_000, bytes_accessed=16_000_000, transcendentals=0)
    common = (wavenumber, damping, shot_cells, wavelet)
    turned_shape = float_shape(2, 2 * shots, BLOCKS * shots)
    field, start, own_tables, shift = pl.pallas_call(
        functools.partial(early_kernel, depth_total),
        out_shape=(planes(layers + REACH), planes(layers + 1), tables(layers + 2), turned_shape),
        in_specs=[smem] * 4 + [vmem] * 4,
        out_specs=(vmem,) * 4,
        compiler_params=params,
        cost_estimate=cost,
        name="early",
    )(*common, edge, own, near, codes)
    first, early_split, early_products, send = pl.pallas_call(
        functools.partial(image_kernel, depth_total),
        out_shape=(planes(layers - 1), split(layers - 3), products, planes(1)),
        in_specs=[vmem] * 2,
        out_specs=(vmem,) * 4,
        scratch_shapes=[scratch(planes(layers - 3)), scratch(planes(1))],
        compiler_params=params,
        cost_estimate=cost,
        name="images",
    )(start, own_tables)
    third_far = lax.ppermute(send, "gz", far_pairs)
    shapes = {
        "field": planes(1),
        "start": planes(1),
        "first": planes(1),
        "second": planes(1),
        "tables": tables(1),
        "split": split(1),
        "next_split": split(1),
        "outer": planes(1),
        "base": planes(1),
        "products": products,
    }

    def run_stage(stage, far, old, extra, outs, temporaries):
        inputs = dict(zip(("wave", "damp", "cells", "wavelet"), common))
        scalars = len(inputs)
        inputs["far"] = far
        inputs.update({name: array for name, (array, _) in old.items()})
        inputs.update(extra)
        results = pl.pallas_call(
            functools.partial(
                stage_kernel,
                stage,
                depth_total,
                layers,
                list(inputs) + outs + temporaries,
                {name: place for name, (_, place) in old.items()},
            ),
            out_shape=tuple(shapes[name] for name in outs),
            in_specs=[smem] * scalars + [vmem] * (len(inputs) - scalars),
            out_specs=(vmem,) * len(outs),
            scratch_shapes=[scratch(shapes[name]) for name in temporaries],
            compiler_params=params,
            cost_estimate=cost,
            name="stage_%d" % stage,
        )(*inputs.values())
        return dict(zip(outs, results))

    zero = run_stage(
        0,
        nearest,
        {
            "field_a": (field, layers + 1),
            "field_b": (field, layers + 2),
            "start_a": (start, layers - 1),
            "start_b": (start, layers),
            "first_a": (first, layers - 3),
            "first_b": (first, layers - 2),
        },
        {"own_tables": own_tables, "products_in": early_products},
        ["field", "start", "first", "split", "products"],
        ["second"],
    )
    one = run_stage(
        1,
        second_far,
        {
            "field_a": (field, layers + 2),
            "field_b": (zero["field"], 0),
            "start_a": (start, layers),
            "start_b": (zero["start"], 0),
            "first_a": (first, layers - 2),
            "first_b": (zero["first"], 0),
        },
        {"own_tables": own_tables, "products_in": zero["products"], "nearest": nearest},
        ["base", "split", "products", "next_split"],
        ["field", "start", "first", "second", "tables", "outer"],
    )
    last_split, grams = pl.pallas_call(
        functools.partial(last_kernel, float(depth_total * span)),
        out_shape=(split(1), float_shape(devices, shots, 128)),
        in_specs=[vmem] * 4,
        out_specs=(vmem, vmem),
        input_output_aliases={3: 0},
        compiler_params=params,
        name="last",
    )(third_far, one["base"], one["products"], one["next_split"])
    grams = lax.all_to_all(grams, "gz", 0, 0)
    basis_two, turned = pl.pallas_call(
        back_kernel,
        out_shape=(
            jax.ShapeDtypeStruct(initial_guess.shape, jnp.float32),
            turned_shape,
        ),
        in_specs=[vmem] * 6,
        out_specs=(vmem, vmem),
        compiler_params=params,
        name="back",
    )(shift, grams, early_split, zero["split"], one["split"], last_split)
    return basis_two, jnp.swapaxes(turned, 1, 2)


def solution(mesh):
    return jax.shard_map(
        shards,
        mesh=mesh,
        in_specs=(
            P(("freq", "gz"), None, None, None, None),
            P("gz", None, None),
            P("gz", None, None),
            P("freq"),
            P(),
            P(),
            P("freq", None),
        ),
        out_specs=(P(("freq", "gz"), None, None, None, None), P("freq", None, None)),
        check_vma=False,
    )
```
